512 devices in a mesh: gx: 16 (over z_hi, x, core), gy: 32 (over z_lo, y).
Axes of the slice: x: 4, y: 4, z: 16 (z_hi: 2, z_lo: 8; z = z_hi * 8 + z_lo), core: 2. Of those that a mesh axis runs over, the one named last changes fastest.
Arguments:
- p_now: float32 [18, 2048, 2048], P(None, 'gy', 'gx'), may hold values from -2 to 2
- p_prev: float32 [18, 2048, 2048], P(None, 'gy', 'gx'), may hold values from -2 to 2
- phase: int32 [18, 2048, 2048], P(None, 'gy', 'gx'), may hold values 0 or 1
- div_star: float32 [16, 2048, 2048], P(None, 'gy', 'gx'), may hold values from -6 to 6
Outputs:
- spectrum: float32 [2, 16, 32, 64, 16, 128], P(None, None, 'gy', None, 'gx')
The draws below stay inside these ranges and needn't reach their ends.
Inputs may be any that keep to these rules, and one draw needn't show every extreme that they name: `phase`: 0 marks gas, 1 liquid.
All inputs are finite; a program needn't handle non-finite values. No bound on the sum of `phase` on one device may be relied on, other than what follows from the above.
Results may differ from the reference program's by a relative error of at most 0.000098.
Values sent between devices are 32-bit elements; how exact they have to be, the bound alone decides.
No kernel may reach another device: no remote copies, remote signals or barrier semaphores. Data moves between devices by JAX's collectives and lax.ppermute only.
A program may use at most 64 MiB of HBM per device.

```python
import jax
import jax.numpy as jnp
import numpy as np

NX = 2048
NY = 2048
PLANES = 16
LX = 128
LY = 64
N_GX = 16
N_GY = 32


def plant(values, stream_key, smallest, largest):
    longest = values.shape.index(max(values.shape))
    spots = []
    for shift in (0, 1):
        where = [jax.random.randint(jax.random.fold_in(stream_key, axis), (), 0, length) for axis, length in enumerate(values.shape)]
        where[longest] = (where[longest] + shift) % values.shape[longest]
        spots.append(tuple(where))
    return values.at[spots[0]].set(smallest).at[spots[1]].set(largest)


def shard_levels(own_key, dims, pieces, smallest, top_value):
    loudness, own = 1.0, jax.random.fold_in(own_key, 6)
    for position, shards_of in pieces:
        steps = jnp.exp(jax.random.uniform(jax.random.fold_in(own, position), (shards_of,), jnp.float32, smallest / len(pieces), top_value / len(pieces)))
        loudness = loudness * jnp.repeat(steps, dims[position] // shards_of).reshape([-1 if axis == position else 1 for axis in range(len(dims))])
    return loudness


def gaussian(key, extent, spread, bound, split=(), held_as=jnp.bfloat16):
    entries = jax.random.normal(key, extent, jnp.float32) * spread
    if len(split) > 0:
        entries = shard_levels(key, extent, split, -0.22, 0.18) * entries
    return jnp.clip(entries, min=-bound, max=bound).astype(held_as)


def setup_inputs(seed: int = 0) -> dict:
    keys = jax.random.split(jax.random.key(seed), 5)
    return {
        "p_now": gaussian(keys[0], (PLANES + 2, NY, NX), 0.25, 2.0, ((1, 32), (2, 16)), jnp.float32),
        "p_prev": gaussian(keys[1], (PLANES + 2, NY, NX), 0.25, 2.0, ((1, 32), (2, 16)), jnp.float32),
        "phase": plant((jax.random.randint(keys[2], (PLANES + 2, NY, NX), 0, 2) < 1).astype(jnp.int32), jax.random.fold_in(keys[2], 1), 0, 1),
        "div_star": gaussian(keys[3], (PLANES, NY, NX), 1.0, 6.0, ((1, 32), (2, 16)), jnp.float32),
    }


RHO_GAS = 1.0
RHO_LIQUID = 8.0
SOURCE = 1.0


def static_reversal(count):
    digits = count.bit_length() - 1
    table = []
    for counter in range(count):
        total = 0
        for place in range(digits):
            total = total * 2 + (counter >> place) % 2
        table.append(total)
    return np.array(table, dtype=np.int32)


def coefficient(first, second):
    return 1.0 - RHO_GAS / (0.5 * (first + second))


def periodic_term(field, weight, axis):
    ahead_field = jnp.roll(field, -1, axis)
    ahead_weight = jnp.roll(weight, -1, axis)
    flux = coefficient(weight, ahead_weight) * (ahead_field - field)
    return flux - jnp.roll(flux, 1, axis)


def reference(p_now, p_prev, phase, div_star):
    extrapolated = 2.0 * p_now - p_prev
    density = jnp.where(phase == 1, RHO_LIQUID, RHO_GAS).astype(p_now.dtype)
    inner_field = extrapolated[1:-1]
    inner_weight = density[1:-1]
    term_x = periodic_term(inner_field, inner_weight, 2)
    term_y = periodic_term(inner_field, inner_weight, 1)
    flux_z = coefficient(density[:-1], density[1:]) * (extrapolated[1:] - extrapolated[:-1])
    term_z = flux_z[1:] - flux_z[:-1]
    rhs = term_x + term_y + term_z + SOURCE * div_star
    spectral = jnp.fft.fft2(rhs, norm="ortho")
    stacked = jnp.stack([jnp.real(spectral), jnp.imag(spectral)]).astype(p_now.dtype)
    shaped = stacked.reshape(2, PLANES, LY, N_GY, LX, N_GX)
    shaped = jnp.take(shaped, static_reversal(N_GY), axis=3)
    shaped = jnp.take(shaped, static_reversal(N_GX), axis=5)
    return jnp.transpose(shaped, (0, 1, 3, 2, 5, 4))
```

```python
import math

import jax
import jax.numpy as jnp
import ml_dtypes
import numpy as np
from jax import lax
from jax.experimental import pallas as pl
from jax.experimental.pallas import tpu as pltpu
from jax.sharding import PartitionSpec as P

NX = 2048
NY = 2048
PLANES = 16
LY = 64
LX = 128
N_GX = 16
N_GY = 32
N_ALL = N_GX * N_GY
F32 = jnp.float32
BF16 = jnp.bfloat16

QUAD = 7.0 / 16.0 - 7.0 / 9.0
LIN = 7.0 / 9.0 - QUAD


def reversal(index, digits):
    total = 0
    for place in range(digits):
        total = total * 2 + ((index >> place) & 1)
    return total


def split(value):
    high = value.astype(BF16)
    return high, (value - high.astype(F32)).astype(BF16)


def dot3(left, right):
    left_high, left_low = left
    right_high, right_low = right
    return (
        jnp.dot(left_high, right_high, preferred_element_type=F32)
        + jnp.dot(left_high, right_low, preferred_element_type=F32)
        + jnp.dot(left_low, right_high, preferred_element_type=F32)
    )


def flux(liquid_a, liquid_b, field_a, field_b):
    count = liquid_a + liquid_b
    return count * (LIN + QUAD * count) * (field_b - field_a)


def edges_kernel(now_ref, prev_ref, phase_ref, x_low, x_high, y_low, y_high):
    lane = lax.broadcasted_iota(jnp.int32, (LY, LX), 1)
    low = jnp.zeros((LY, LX), F32)
    high = jnp.zeros((LY, LX), F32)
    for k in range(PLANES):
        field = 2.0 * now_ref[k + 1] - prev_ref[k + 1]
        liquid = phase_ref[k + 1].astype(F32)
        y_low[k : k + 1, :] = field[0:1]
        y_low[PLANES + k : PLANES + k + 1, :] = liquid[0:1]
        y_high[k : k + 1, :] = field[LY - 1 : LY]
        y_high[PLANES + k : PLANES + k + 1, :] = liquid[LY - 1 : LY]
        low = jnp.where(lane == k, jnp.broadcast_to(field[:, 0:1], (LY, LX)), low)
        low = jnp.where(lane == PLANES + k, jnp.broadcast_to(liquid[:, 0:1], (LY, LX)), low)
        high = jnp.where(lane == k, jnp.broadcast_to(field[:, LX - 1 : LX], (LY, LX)), high)
        high = jnp.where(
            lane == PLANES + k, jnp.broadcast_to(liquid[:, LX - 1 : LX], (LY, LX)), high
        )
    x_low[...] = low
    x_high[...] = high


def stencil_kernel(now_ref, prev_ref, phase_ref, div_ref, x_below, x_above, y_below, y_above, out):
    lane = lax.broadcasted_iota(jnp.int32, (LY, LX), 1)
    row = lax.broadcasted_iota(jnp.int32, (LY, LX), 0)

    def plane(k):
        return 2.0 * now_ref[k] - prev_ref[k], phase_ref[k].astype(F32)

    def wide(ref, k):
        return jnp.broadcast_to(ref[:, k : k + 1], (LY, LX))

    def tall(ref, k):
        return jnp.broadcast_to(ref[k : k + 1, :], (LY, LX))

    field_before, liquid_before = plane(0)
    field, liquid = plane(1)
    flux_z = flux(liquid_before, liquid, field_before, field)
    for k in range(PLANES):
        field_after, liquid_after = plane(k + 2)
        flux_z_upper = flux(liquid, liquid_after, field, field_after)
        total = div_ref[k] + (flux_z_upper - flux_z)
        right = jnp.where(lane == LX - 1, wide(x_above, k), pltpu.roll(field, LX - 1, 1))
        right_liquid = jnp.where(
            lane == LX - 1, wide(x_above, PLANES + k), pltpu.roll(liquid, LX - 1, 1)
        )
        upper = flux(liquid, right_liquid, field, right)
        entering = flux(wide(x_below, PLANES + k), liquid, wide(x_below, k), field)
        total = total + (upper - jnp.where(lane == 0, entering, pltpu.roll(upper, 1, 1)))
        above = jnp.where(row == LY - 1, tall(y_above, k), pltpu.roll(field, LY - 1, 0))
        above_liquid = jnp.where(
            row == LY - 1, tall(y_above, PLANES + k), pltpu.roll(liquid, LY - 1, 0)
        )
        upper = flux(liquid, above_liquid, field, above)
        entering = flux(tall(y_below, PLANES + k), liquid, tall(y_below, k), field)
        total = total + (upper - jnp.where(row == 0, entering, pltpu.roll(upper, 1, 0)))
        out[k] = total
        field, liquid, flux_z = field_after, liquid_after, flux_z_upper


def device_kernel(x_ref, high_ref, low_ref, out):
    both = jnp.concatenate(
        [x_ref[pl.ds(0, N_ALL, stride=2), :], x_ref[pl.ds(1, N_ALL, stride=2), :]], axis=1
    )
    right = split(both)
    for part in range(2):
        rows = pl.ds(part * N_ALL, N_ALL)
        result = dot3((high_ref[rows, :], low_ref[rows, :]), right)
        out[pl.ds(2 * part, N_ALL, stride=4), :] = result[:, :LX]
        out[pl.ds(2 * part + 1, N_ALL, stride=4), :] = result[:, LX:]


def local_kernel(x_ref, y_matrix_ref, x_matrix_ref, out):
    y_matrix = split(y_matrix_ref[...])
    x_matrix = split(x_matrix_ref[...])
    for k in range(PLANES):
        lines = dot3(y_matrix, split(x_ref[pl.ds(k * 2 * LY, 2 * LY), :]))
        lines = jnp.concatenate([lines[:LY], lines[LY:]], axis=1)
        modes = dot3(split(lines), x_matrix)
        out[0, k] = modes[:, :LX]
        out[1, k] = modes[:, LX:]


def device_tables():
    source = np.arange(N_ALL)
    rev_p = np.array([reversal(i, 4) for i in range(N_GX)])
    rev_q = np.array([reversal(i, 5) for i in range(N_GY)])
    kx = rev_p[source // N_GY][:, None]
    ky = rev_q[source % N_GY][:, None]
    turns = (2 * kx * (source // N_GY)[None] + ky * (source % N_GY)[None]) % N_GY
    angle = turns * (2.0 * math.pi / N_GY)
    table = np.concatenate([np.cos(angle), -np.sin(angle)])
    high = table.astype(ml_dtypes.bfloat16)
    return high, (table - high.astype(np.float64)).astype(ml_dtypes.bfloat16)


def cos_sin(place, mode, length):
    angle = ((place * mode) % length).astype(F32) * (2.0 * math.pi / length)
    return jnp.cos(angle), jnp.sin(angle)


def local_tables():
    rp = reversal(lax.axis_index("gx"), 4)
    rq = reversal(lax.axis_index("gy"), 5)
    line = lax.broadcasted_iota(jnp.int32, (2 * LY, 2 * LY), 0)
    col = lax.broadcasted_iota(jnp.int32, (2 * LY, 2 * LY), 1)
    cosine, sine = cos_sin((col >> 2) * 2 + (col & 1), 32 * (line % LY) + rq, NY)
    part_out, part_in = line // LY, (col >> 1) & 1
    sign = jnp.where(part_out < part_in, 1.0, -1.0)
    y_matrix = jnp.where(part_out == part_in, cosine, sign * sine) * (1.0 / math.sqrt(NX * NY))
    line = lax.broadcasted_iota(jnp.int32, (2 * LX, 2 * LX), 0)
    col = lax.broadcasted_iota(jnp.int32, (2 * LX, 2 * LX), 1)
    cosine, sine = cos_sin(line % LX, 16 * (col % LX) + rp, NX)
    part_in, part_out = line // LX, col // LX
    sign = jnp.where(part_out < part_in, 1.0, -1.0)
    x_matrix = jnp.where(part_out == part_in, cosine, sign * sine)
    return y_matrix, x_matrix


def call(kernel, outs, *args):
    return pl.pallas_call(
        kernel,
        out_shape=outs,
        compiler_params=pltpu.CompilerParams(vmem_limit_bytes=40 * 1024 * 1024),
    )(*args)


def shape(*dims):
    return jax.ShapeDtypeStruct(dims, F32)


def body(p_now, p_prev, phase, div_star):
    x_low, x_high, y_low, y_high = call(
        edges_kernel,
        (shape(LY, LX), shape(LY, LX), shape(2 * PLANES, LX), shape(2 * PLANES, LX)),
        p_now,
        p_prev,
        phase,
    )
    up_x = [(i, (i + 1) % N_GX) for i in range(N_GX)]
    up_y = [(i, (i + 1) % N_GY) for i in range(N_GY)]
    down_x = [(b, a) for a, b in up_x]
    down_y = [(b, a) for a, b in up_y]
    x_below = lax.ppermute(x_high, "gx", up_x)
    x_above = lax.ppermute(x_low, "gx", down_x)
    y_below = lax.ppermute(y_high, "gy", up_y)
    y_above = lax.ppermute(y_low, "gy", down_y)
    rhs = call(
        stencil_kernel,
        shape(PLANES, LY, LX),
        p_now,
        p_prev,
        phase,
        div_star,
        x_below,
        x_above,
        y_below,
        y_above,
    )
    everywhere = ("gx", "gy")
    chunks = lax.all_to_all(rhs.reshape(N_ALL, 2, LX), everywhere, 0, 0, tiled=True)
    high, low = device_tables()
    modes = call(
        device_kernel,
        shape(4 * N_ALL, LX),
        chunks.reshape(2 * N_ALL, LX),
        jnp.asarray(high),
        jnp.asarray(low),
    )
    back = lax.all_to_all(modes.reshape(N_ALL, 4, LX), everywhere, 0, 0, tiled=True)
    y_matrix, x_matrix = local_tables()
    result = call(
        local_kernel,
        shape(2, PLANES, LY, LX),
        back.reshape(4 * N_ALL, LX),
        y_matrix,
        x_matrix,
    )
    return result.reshape(2, PLANES, 1, LY, 1, LX)


def solution(mesh):
    spec = P(None, "gy", "gx")
    return jax.shard_map(
        body,
        mesh=mesh,
        in_specs=(spec, spec, spec, spec),
        out_specs=P(None, None, "gy", None, "gx", None),
        check_vma=False,
    )
```

```python
import math

import jax
import jax.numpy as jnp
import ml_dtypes
import numpy as np
from jax import lax
from jax.experimental import pallas as pl
from jax.experimental.pallas import tpu as pltpu
from jax.sharding import PartitionSpec as P

NX = 2048
NY = 2048
PLANES = 16
LY = 64
LX = 128
N_GX = 16
N_GY = 32
N_ALL = N_GX * N_GY
F32 = jnp.float32
BF16 = jnp.bfloat16

QUAD = 7.0 / 16.0 - 7.0 / 9.0
LIN = 7.0 / 9.0 - QUAD

PIECES = 8
PIECE = LX // PIECES
SHIFT = 8
PER_PLANE = N_ALL // PLANES
WIDE = PER_PLANE - PIECES


def reversal(index, digits):
    total = 0
    for place in range(digits):
        total = total * 2 + ((index >> place) & 1)
    return total


def split(value):
    high = value.astype(BF16)
    return high, (value - high.astype(F32)).astype(BF16)


def dot3(left, right):
    left_high, left_low = left
    right_high, right_low = right
    return (
        jnp.dot(left_high, right_high, preferred_element_type=F32)
        + jnp.dot(left_high, right_low, preferred_element_type=F32)
        + jnp.dot(left_low, right_high, preferred_element_type=F32)
    )


def flux(liquid_a, liquid_b, field_a, field_b):
    count = liquid_a + liquid_b
    return count * (LIN + QUAD * count) * (field_b - field_a)


def roll(value, by, axis):
    by = by % value.shape[axis]
    return pltpu.roll(value, by, axis) if by else value


def lanes_of(rows):
    return lax.broadcasted_iota(jnp.int32, (rows, LX), 1)


def rows_of(rows):
    return lax.broadcasted_iota(jnp.int32, (rows, LX), 0)


def exchange_pieces(value):
    offset = (lanes_of(PIECES) // PIECE - rows_of(PIECES)) & (PIECES - 1)
    total = value
    for d in range(1, PIECES):
        total = jnp.where(offset == d, roll(roll(value, -d, 0), PIECE * d, 1), total)
    return total


def stencil_kernel(now_ref, prev_ref, phase_ref, div_ref, out):
    lane = lanes_of(LY)
    row = rows_of(LY)
    edge_lane = (lane == 0) | (lane == LX - 1)
    sub = rows_of(PIECES)
    first_half = lanes_of(PIECES) % PIECE < PIECE // 2

    def plane(k):
        return 2.0 * now_ref[k] - prev_ref[k], phase_ref[k].astype(F32)

    field_before, liquid_before = plane(0)
    field, liquid = plane(1)
    flux_z = flux(liquid_before, liquid, field_before, field)
    for k in range(PLANES):
        field_after, liquid_after = plane(k + 2)
        flux_z_upper = flux(liquid, liquid_after, field, field_after)
        total = div_ref[k] + (flux_z_upper - flux_z)
        upper = flux(liquid, roll(liquid, -1, 1), field, roll(field, -1, 1))
        upper = jnp.where(lane == LX - 1, 0.0, upper)
        total = total + (upper - roll(upper, 1, 1))
        upper = flux(liquid, roll(liquid, -1, 0), field, roll(field, -1, 0))
        upper = jnp.where(row == LY - 1, 0.0, upper)
        total = total + (upper - roll(upper, 1, 0))
        total = roll(total, SHIFT, 1)
        faces = jnp.where(edge_lane, field, 0.0) + roll(jnp.where(edge_lane, liquid, 0.0), 2, 1)
        faces = roll(faces, SHIFT, 1)
        lines = [field[0:1], liquid[0:1], field[LY - 1 : LY], liquid[LY - 1 : LY]]
        pairs = jnp.zeros((PIECES, LX), F32)
        for f, line in enumerate(lines):
            pairs = jnp.where(sub // 2 == f, jnp.broadcast_to(line, (PIECES, LX)), pairs)
        pairs = jnp.where(sub % 2 == 0, roll(pairs, SHIFT, 1), pairs)
        pairs = roll(exchange_pieces(jnp.where(first_half, pairs, 0.0)), -1, 1)

        start = k * PER_PLANE * 3
        low, high = slice(0, PIECES), slice(LY - PIECES, LY)
        out[pl.ds(start, PIECES, stride=3), :] = exchange_pieces(total[low])
        out[pl.ds(start + 1, PIECES, stride=3), :] = exchange_pieces(total[high])
        out[pl.ds(start + 2, PIECES, stride=3), :] = (
            exchange_pieces(faces[low] + roll(faces[high], 4, 1)) + pairs
        )
        start += PIECES * 3
        low, high = slice(PIECES, PIECES + WIDE), slice(PIECES + WIDE, PIECES + 2 * WIDE)
        out[pl.ds(start, WIDE, stride=3), :] = total[low]
        out[pl.ds(start + 1, WIDE, stride=3), :] = total[high]
        out[pl.ds(start + 2, WIDE, stride=3), :] = faces[low] + roll(faces[high], 4, 1)
        field, liquid, flux_z = field_after, liquid_after, flux_z_upper


def device_kernel(x_ref, high_ref, low_ref, out, cells):
    lane = lanes_of(N_GY)
    place = lane % PIECE
    row = rows_of(N_GY)
    x_face = place == 7
    y_first = (lane == LX - 1) | (lane < 7)
    y_second = (lane >= 15) & (lane < 23)

    def group(g, r):
        return x_ref[pl.ds((g % N_GX) * N_GY * 3 + r, N_GY, stride=3), :]

    def x_flux(here, there, t):
        through = flux(
            roll(here, -2 - 4 * t, 1),
            roll(there, -3 - 4 * t, 1),
            roll(here, -4 * t, 1),
            roll(there, -1 - 4 * t, 1),
        )
        return jnp.where(x_face, through, 0.0)

    last = group(N_GX - 1, 2)
    here = group(0, 2)
    entering = [x_flux(last, here, t) for t in range(2)]
    for g in range(N_GX):
        there = group(g + 1, 2)
        first, second = group(g, 0), group(g, 1)
        leaving = [x_flux(here, there, t) for t in range(2)]
        first = first + (leaving[0] - roll(entering[0], 1, 1))
        second = second + (leaving[1] - roll(entering[1], 1, 1))
        after = roll(here, -1, 0)
        through = flux(roll(here, -96, 1), roll(after, -32, 1), roll(here, -64, 1), after)
        through_first = jnp.where(y_first, through, 0.0)
        through_second = jnp.where(y_second, through, 0.0)
        before = roll(through_first, 1, 1) + roll(through_second, -7, 1)
        first = first - roll(before, 1, 0)
        second = second + roll(before, LX - PIECE, 1)
        cells[pl.ds(g * N_GY, N_GY), :LX] = first
        cells[pl.ds(g * N_GY, N_GY), LX:] = second
        here, entering = there, leaving

    right = split(cells[...])
    for part in range(2):
        rows = pl.ds(part * N_ALL, N_ALL)
        result = dot3((high_ref[rows, :], low_ref[rows, :]), right)
        out[pl.ds(2 * part, N_ALL, stride=4), :] = result[:, :LX]
        out[pl.ds(2 * part + 1, N_ALL, stride=4), :] = result[:, LX:]


def local_kernel(x_ref, y_matrix_ref, x_matrix_ref, out):
    y_matrix = split(y_matrix_ref[...])
    x_matrix = split(x_matrix_ref[...])
    for k in range(PLANES):
        start = k * 2 * LY
        lines = [
            exchange_pieces(x_ref[pl.ds(start + kind, PIECES, stride=4), :]) for kind in range(4)
        ]
        lines.append(x_ref[pl.ds(start + 4 * PIECES, 4 * WIDE), :])
        lines = dot3(y_matrix, split(jnp.concatenate(lines, axis=0)))
        lines = jnp.concatenate([lines[:LY], lines[LY:]], axis=1)
        modes = dot3(split(lines), x_matrix)
        out[0, k] = modes[:, :LX]
        out[1, k] = modes[:, LX:]


def device_tables():
    source = np.arange(N_ALL)
    rev_p = np.array([reversal(i, 4) for i in range(N_GX)])
    rev_q = np.array([reversal(i, 5) for i in range(N_GY)])
    kx = rev_p[source // N_GY][:, None]
    ky = rev_q[source % N_GY][:, None]
    turns = (2 * kx * (source // N_GY)[None] + ky * (source % N_GY)[None]) % N_GY
    angle = turns * (2.0 * math.pi / N_GY)
    table = np.concatenate([np.cos(angle), -np.sin(angle)])
    high = table.astype(ml_dtypes.bfloat16)
    return high, (table - high.astype(np.float64)).astype(ml_dtypes.bfloat16)


def cos_sin(place, mode, length):
    angle = ((place * mode) % length).astype(F32) * (2.0 * math.pi / length)
    return jnp.cos(angle), jnp.sin(angle)


def local_tables():
    rp = reversal(lax.axis_index("gx"), 4)
    rq = reversal(lax.axis_index("gy"), 5)
    line = lax.broadcasted_iota(jnp.int32, (2 * LY, 2 * LY), 0)
    col = lax.broadcasted_iota(jnp.int32, (2 * LY, 2 * LY), 1)
    rest = col - 4 * PIECES
    in_piece = rest < 0
    part_in = jnp.where(in_piece, col >> 4, rest >> 1) & 1
    place = jnp.where(
        in_piece,
        (col & 7) + (LY - PIECES) * ((col >> 3) & 1),
        PIECES + (rest >> 2) + WIDE * (rest & 1),
    )
    cosine, sine = cos_sin(place, 32 * (line % LY) + rq, NY)
    part_out = line // LY
    sign = jnp.where(part_out < part_in, 1.0, -1.0)
    y_matrix = jnp.where(part_out == part_in, cosine, sign * sine) * (1.0 / math.sqrt(NX * NY))
    line = lax.broadcasted_iota(jnp.int32, (2 * LX, 2 * LX), 0)
    col = lax.broadcasted_iota(jnp.int32, (2 * LX, 2 * LX), 1)
    cosine, sine = cos_sin((line + LX - SHIFT) % LX, 16 * (col % LX) + rp, NX)
    part_in, part_out = line // LX, col // LX
    sign = jnp.where(part_out < part_in, 1.0, -1.0)
    x_matrix = jnp.where(part_out == part_in, cosine, sign * sine)
    return y_matrix, x_matrix


def call(kernel, outs, *args, scratch=()):
    return pl.pallas_call(
        kernel,
        out_shape=outs,
        scratch_shapes=scratch,
        compiler_params=pltpu.CompilerParams(vmem_limit_bytes=40 * 1024 * 1024),
    )(*args)


def shape(*dims):
    return jax.ShapeDtypeStruct(dims, F32)


def body(p_now, p_prev, phase, div_star):
    chunks = call(stencil_kernel, shape(3 * N_ALL, LX), p_now, p_prev, phase, div_star)
    everywhere = ("gx", "gy")
    chunks = lax.all_to_all(chunks.reshape(N_ALL, 1, 3 * LX), everywhere, 0, 0, tiled=True)
    high, low = device_tables()
    modes = call(
        device_kernel,
        shape(4 * N_ALL, LX),
        chunks.reshape(3 * N_ALL, LX),
        jnp.asarray(high),
        jnp.asarray(low),
        scratch=[pltpu.VMEM((N_ALL, 2 * LX), F32)],
    )
    back = lax.all_to_all(modes.reshape(N_ALL, 4, LX), everywhere, 0, 0, tiled=True)
    y_matrix, x_matrix = local_tables()
    result = call(
        local_kernel,
        shape(2, PLANES, LY, LX),
        back.reshape(4 * N_ALL, LX),
        y_matrix,
        x_matrix,
    )
    return result.reshape(2, PLANES, 1, LY, 1, LX)


def solution(mesh):
    spec = P(None, "gy", "gx")
    return jax.shard_map(
        body,
        mesh=mesh,
        in_specs=(spec, spec, spec, spec),
        out_specs=P(None, None, "gy", None, "gx", None),
        check_vma=False,
    )
```

```python
import math

import jax
import jax.numpy as jnp
import ml_dtypes
import numpy as np
from jax import lax
from jax.experimental import pallas as pl
from jax.experimental.pallas import tpu as pltpu
from jax.sharding import PartitionSpec as P

NX = 2048
NY = 2048
PLANES = 16
LY = 64
LX = 128
N_GX = 16
N_GY = 32
N_ALL = N_GX * N_GY
F32 = jnp.float32
BF16 = jnp.bfloat16

QUAD = 7.0 / 16.0 - 7.0 / 9.0
LIN = 7.0 / 9.0 - QUAD

BLOCKS = 8
BLOCK = LX // BLOCKS
PER_PLANE = N_ALL // PLANES
WIDE = PER_PLANE - BLOCKS
HALF = LY // 2
GROUP = 4


def reversal(index, digits):
    total = 0
    for place in range(digits):
        total = total * 2 + ((index >> place) & 1)
    return total


def split(value):
    high = value.astype(BF16)
    return high, (value - high.astype(F32)).astype(BF16)


def dot3(left, right):
    left_high, left_low = left
    right_high, right_low = right
    return (
        jnp.dot(left_high, right_high, preferred_element_type=F32)
        + jnp.dot(left_high, right_low, preferred_element_type=F32)
        + jnp.dot(left_low, right_high, preferred_element_type=F32)
    )


def flux(liquid_a, liquid_b, field_a, field_b):
    count = liquid_a + liquid_b
    return count * (LIN + QUAD * count) * (field_b - field_a)


def roll(value, by, axis):
    by = by % value.shape[axis]
    return pltpu.roll(value, by, axis) if by else value


def lanes_of(rows):
    return lax.broadcasted_iota(jnp.int32, (rows, LX), 1)


def rows_of(rows):
    return lax.broadcasted_iota(jnp.int32, (rows, LX), 0)


def turn(value, block, sign, offset):
    value = roll(value, -offset, 0)
    for bit in (1, 2, 4):
        value = jnp.where((block & bit) != 0, roll(value, -sign * bit, 0), value)
    return value


def cell_block():
    return ((lanes_of(BLOCKS) + BLOCK // 2) // BLOCK) & (BLOCKS - 1)


def face_block(rows):
    lane = (lanes_of(rows) + LX - 1) & (LX - 1)
    return lane // BLOCK, lane % BLOCK < BLOCK // 2


def stencil_kernel(
    now_hbm,
    prev_hbm,
    phase_hbm,
    div_hbm,
    out_hbm,
    now_ref,
    prev_ref,
    phase_ref,
    div_ref,
    out,
    sems,
    out_sems,
):
    copies, sent = [], []
    for g in range(PLANES // GROUP):
        first = GROUP * g + 2 if g else 0
        planes = pl.ds(first, GROUP * (g + 1) + 2 - first)
        inner = pl.ds(GROUP * g, GROUP)
        copies.append(
            [
                pltpu.make_async_copy(source.at[part], target.at[part], sems.at[g, a])
                for a, (source, target, part) in enumerate(
                    (
                        (now_hbm, now_ref, planes),
                        (prev_hbm, prev_ref, planes),
                        (phase_hbm, phase_ref, planes),
                        (div_hbm, div_ref, inner),
                    )
                )
            ]
        )
        for copy in copies[-1]:
            copy.start()

    lane = lanes_of(LY)
    row = rows_of(LY)
    edge_lane = (lane == 0) | (lane == LX - 1)
    sub = rows_of(BLOCKS)
    block = cell_block()
    line_block, in_half = face_block(BLOCKS)

    def plane(k):
        return 2.0 * now_ref[k] - prev_ref[k], phase_ref[k].astype(F32)

    for k in range(PLANES):
        if k % GROUP == 0:
            for copy in copies[k // GROUP]:
                copy.wait()
        if k == 0:
            field_before, liquid_before = plane(0)
            field, liquid = plane(1)
            flux_z = flux(liquid_before, liquid, field_before, field)
        field_after, liquid_after = plane(k + 2)
        flux_z_upper = flux(liquid, liquid_after, field, field_after)
        total = div_ref[k] + (flux_z_upper - flux_z)
        upper = flux(liquid, roll(liquid, -1, 1), field, roll(field, -1, 1))
        upper = jnp.where(lane == LX - 1, 0.0, upper)
        total = total + (upper - roll(upper, 1, 1))
        upper = flux(liquid, roll(liquid, -1, 0), field, roll(field, -1, 0))
        upper = jnp.where(row == LY - 1, 0.0, upper)
        total = total + (upper - roll(upper, 1, 0))
        ends = jnp.where(edge_lane, field, 0.0)
        wet_ends = jnp.where(edge_lane, liquid, 0.0)
        first = ends[:HALF] + roll(wet_ends[:HALF], -2, 1)
        second = roll(ends[HALF:], -4, 1) + roll(wet_ends[HALF:], -6, 1)
        lines = jnp.broadcast_to(liquid[LY - 1 : LY], (BLOCKS, LX))
        for f, line in ((2, field[LY - 1 : LY]), (1, liquid[0:1]), (0, field[0:1])):
            lines = jnp.where(sub < 2 * f + 2, jnp.broadcast_to(line, (BLOCKS, LX)), lines)
        lines = roll(lines, 9, 1)
        for bit, by in ((1, 8), (2, 32), (4, 64)):
            lines = jnp.where((sub & bit) != 0, roll(lines, by, 1), lines)
        lines = turn(jnp.where(in_half, lines, 0.0), line_block, 1, 0)

        start = k * PER_PLANE * 3
        out[pl.ds(start, BLOCKS, stride=3), :] = turn(total[:BLOCKS], block, 1, 0)
        out[pl.ds(start + 1, BLOCKS, stride=3), :] = turn(total[LY - BLOCKS :], block, 1, 7)
        out[pl.ds(start + 2, BLOCKS, stride=3), :] = (
            first[:BLOCKS] + roll(second[WIDE:], 1, 0) + lines
        )
        start += BLOCKS * 3
        out[pl.ds(start, WIDE, stride=3), :] = total[BLOCKS:HALF]
        out[pl.ds(start + 1, WIDE, stride=3), :] = total[HALF : HALF + WIDE]
        out[pl.ds(start + 2, WIDE, stride=3), :] = first[BLOCKS:] + second[:WIDE]
        field, liquid, flux_z = field_after, liquid_after, flux_z_upper
        if k % GROUP == GROUP - 1:
            g = k // GROUP
            rows = pl.ds(g * GROUP * PER_PLANE * 3, GROUP * PER_PLANE * 3)
            sent.append(pltpu.make_async_copy(out.at[rows], out_hbm.at[rows], out_sems.at[g]))
            sent[-1].start()
    for copy in sent:
        copy.wait()


def device_kernel(x_ref, high_ref, low_ref, out, cells):
    last_lane = lanes_of(N_GY) == LX - 1
    own = (BLOCKS - lax.axis_index("gy") % BLOCKS) % BLOCKS
    line_block, in_half = face_block(N_GY)
    first_half = in_half & (line_block == own)
    second_half = in_half & (line_block == (own + 1) % BLOCKS)

    def group(g, r):
        return x_ref[pl.ds((g % N_GX) * N_GY * 3 + r, N_GY, stride=3), :]

    def x_flux(here, there, t):
        through = flux(
            roll(here, 2 + 4 * t, 1),
            roll(there, 1 + 4 * t, 1),
            roll(here, 4 * t, 1),
            roll(there, 4 * t - 1, 1),
        )
        return jnp.where(last_lane, through, 0.0)

    last = group(N_GX - 1, 2)
    here = group(0, 2)
    entering = [x_flux(last, here, t) for t in range(2)]
    for g in range(N_GX):
        there = group(g + 1, 2)
        first, second = group(g, 0), group(g, 1)
        leaving = [x_flux(here, there, t) for t in range(2)]
        first = first + (leaving[0] - roll(entering[0], 1, 1))
        second = second + (leaving[1] - roll(entering[1], 1, 1))
        after = roll(here, -1, 0)
        through = flux(roll(here, -96, 1), roll(after, -32, 1), roll(here, -64, 1), after)
        through = roll(jnp.where(first_half, through, 0.0), -9, 1) + roll(
            jnp.where(second_half, through, 0.0), -17, 1
        )
        cells[pl.ds(g * N_GY, N_GY), :LX] = first - roll(through, 1, 0)
        cells[pl.ds(g * N_GY, N_GY), LX:] = second + through
        here, entering = there, leaving

    right = split(cells[...])
    for part in range(2):
        rows = pl.ds(part * N_ALL, N_ALL)
        result = dot3((high_ref[rows, :], low_ref[rows, :]), right)
        out[pl.ds(2 * part, N_ALL, stride=4), :] = result[:, :LX]
        out[pl.ds(2 * part + 1, N_ALL, stride=4), :] = result[:, LX:]


def local_kernel(x_ref, y_matrix_ref, x_matrix_ref, out_hbm, out, sems):
    y_matrix = split(y_matrix_ref[...])
    x_matrix = split(x_matrix_ref[...])
    block = cell_block()
    copies = []
    for k in range(PLANES):
        start = k * 2 * LY
        lines = [
            turn(x_ref[pl.ds(start + kind, BLOCKS, stride=4), :], block, -1, kind & 1)
            for kind in range(4)
        ]
        lines.append(x_ref[pl.ds(start + 4 * BLOCKS, 4 * WIDE), :])
        lines = dot3(y_matrix, split(jnp.concatenate(lines, axis=0)))
        lines = jnp.concatenate([lines[:LY], lines[LY:]], axis=1)
        modes = dot3(split(lines), x_matrix)
        out[0, k] = modes[:, :LX]
        out[1, k] = modes[:, LX:]
        if k % GROUP == GROUP - 1:
            g = k // GROUP
            for part in range(2):
                planes = (part, pl.ds(g * GROUP, GROUP))
                copies.append(
                    pltpu.make_async_copy(
                        out.at[planes], out_hbm.at[planes], sems.at[g, part]
                    )
                )
                copies[-1].start()
    for copy in copies:
        copy.wait()


def device_tables():
    source = np.arange(N_ALL)
    rev_p = np.array([reversal(i, 4) for i in range(N_GX)])
    rev_q = np.array([reversal(i, 5) for i in range(N_GY)])
    kx = rev_p[source // N_GY][:, None]
    ky = rev_q[source % N_GY][:, None]
    turns = (2 * kx * (source // N_GY)[None] + ky * (source % N_GY)[None]) % N_GY
    angle = turns * (2.0 * math.pi / N_GY)
    table = np.concatenate([np.cos(angle), -np.sin(angle)])
    high = table.astype(ml_dtypes.bfloat16)
    return high, (table - high.astype(np.float64)).astype(ml_dtypes.bfloat16)


def cos_sin(place, mode, length):
    angle = ((place * mode) % length).astype(F32) * (2.0 * math.pi / length)
    return jnp.cos(angle), jnp.sin(angle)


def local_tables():
    rp = reversal(lax.axis_index("gx"), 4)
    rq = reversal(lax.axis_index("gy"), 5)
    line = lax.broadcasted_iota(jnp.int32, (2 * LY, 2 * LY), 0)
    col = lax.broadcasted_iota(jnp.int32, (2 * LY, 2 * LY), 1)
    rest = col - 4 * BLOCKS
    in_block = rest < 0
    part_in = jnp.where(in_block, col >> 4, rest >> 1) & 1
    place = jnp.where(
        in_block,
        (col & 7) + (LY - BLOCKS) * ((col >> 3) & 1),
        BLOCKS + (rest >> 2) + WIDE * (rest & 1),
    )
    cosine, sine = cos_sin(place, 32 * (line % LY) + rq, NY)
    part_out = line // LY
    sign = jnp.where(part_out < part_in, 1.0, -1.0)
    y_matrix = jnp.where(part_out == part_in, cosine, sign * sine) * (1.0 / math.sqrt(NX * NY))
    line = lax.broadcasted_iota(jnp.int32, (2 * LX, 2 * LX), 0)
    col = lax.broadcasted_iota(jnp.int32, (2 * LX, 2 * LX), 1)
    cosine, sine = cos_sin(line % LX, 16 * (col % LX) + rp, NX)
    part_in, part_out = line // LX, col // LX
    sign = jnp.where(part_out < part_in, 1.0, -1.0)
    x_matrix = jnp.where(part_out == part_in, cosine, sign * sine)
    return y_matrix, x_matrix


def call(kernel, outs, *args, scratch=(), in_hbm=False, out_hbm=False, mib=40):
    def spec(hbm):
        return pl.BlockSpec(memory_space=pltpu.HBM if hbm else pltpu.VMEM)

    return pl.pallas_call(
        kernel,
        out_shape=outs,
        in_specs=[spec(in_hbm)] * len(args),
        out_specs=spec(out_hbm),
        scratch_shapes=scratch,
        compiler_params=pltpu.CompilerParams(vmem_limit_bytes=mib * 1024 * 1024),
    )(*args)


def shape(*dims):
    return jax.ShapeDtypeStruct(dims, F32)


def body(p_now, p_prev, phase, div_star):
    padded = (PLANES + 2, LY, LX)
    chunks = call(
        stencil_kernel,
        shape(3 * N_ALL, LX),
        p_now,
        p_prev,
        phase,
        div_star,
        scratch=[
            pltpu.VMEM(padded, F32),
            pltpu.VMEM(padded, F32),
            pltpu.VMEM(padded, jnp.int32),
            pltpu.VMEM((PLANES, LY, LX), F32),
            pltpu.VMEM((3 * N_ALL, LX), F32),
            pltpu.SemaphoreType.DMA((PLANES // GROUP, 4)),
            pltpu.SemaphoreType.DMA((PLANES // GROUP,)),
        ],
        in_hbm=True,
        out_hbm=True,
        mib=60,
    )
    everywhere = ("gx", "gy")
    chunks = lax.all_to_all(chunks.reshape(N_ALL, 1, 3 * LX), everywhere, 0, 0, tiled=True)
    high, low = device_tables()
    modes = call(
        device_kernel,
        shape(4 * N_ALL, LX),
        chunks.reshape(3 * N_ALL, LX),
        jnp.asarray(high),
        jnp.asarray(low),
        scratch=[pltpu.VMEM((N_ALL, 2 * LX), F32)],
    )
    back = lax.all_to_all(modes.reshape(N_ALL, 4, LX), everywhere, 0, 0, tiled=True)
    y_matrix, x_matrix = local_tables()
    result = call(
        local_kernel,
        shape(2, PLANES, LY, LX),
        back.reshape(4 * N_ALL, LX),
        y_matrix,
        x_matrix,
        scratch=[
            pltpu.VMEM((2, PLANES, LY, LX), F32),
            pltpu.SemaphoreType.DMA((PLANES // GROUP, 2)),
        ],
        out_hbm=True,
    )
    return result.reshape(2, PLANES, 1, LY, 1, LX)


def solution(mesh):
    spec = P(None, "gy", "gx")
    return jax.shard_map(
        body,
        mesh=mesh,
        in_specs=(spec, spec, spec, spec),
        out_specs=P(None, None, "gy", None, "gx", None),
        check_vma=False,
    )
```

```python
import functools
import math

import jax
import jax.numpy as jnp
import ml_dtypes
import numpy as np
from jax import lax
from jax.experimental import pallas as pl
from jax.experimental.pallas import tpu as pltpu
from jax.sharding import Mesh
from jax.sharding import PartitionSpec as P

NX = 2048
NY = 2048
PLANES = 16
LY = 64
LX = 128
N_GX = 16
N_GY = 32
N_ALL = N_GX * N_GY
N_CHIP = N_ALL // 2
F32 = jnp.float32
BF16 = jnp.bfloat16

CHIPS = ("zh", "x", "zl", "y")
EVERYWHERE = ("zh", "x", "c", "zl", "y")

QUAD = 7.0 / 16.0 - 7.0 / 9.0
LIN = 7.0 / 9.0 - QUAD

BLOCKS = 16
BLOCK = LX // BLOCKS
PER_PLANE = N_ALL // PLANES
WIDE = PER_PLANE - BLOCKS
HALF = LY // 2
SHARE = PLANES // 2
GROUP = 4
QUARTER = LX // 4


def reversal(index, digits):
    total = 0
    for place in range(digits):
        total = total * 2 + ((index >> place) & 1)
    return total


def split(value):
    high = value.astype(BF16)
    return high, (value - high.astype(F32)).astype(BF16)


def dot3(left, right):
    left_high, left_low = left
    right_high, right_low = right
    return (
        jnp.dot(left_high, right_high, preferred_element_type=F32)
        + jnp.dot(left_high, right_low, preferred_element_type=F32)
        + jnp.dot(left_low, right_high, preferred_element_type=F32)
    )


def weighted(count, difference):
    return count * (LIN + QUAD * count) * difference


def flux(liquid_a, liquid_b, field_a, field_b):
    return weighted(liquid_a + liquid_b, field_b - field_a)


def roll(value, by, axis):
    if isinstance(by, int):
        by = by % value.shape[axis]
        return pltpu.roll(value, by, axis) if by else value
    return pltpu.roll(value, by & (value.shape[axis] - 1), axis)


def lanes_of(rows):
    return lax.broadcasted_iota(jnp.int32, (rows, LX), 1)


def rows_of(rows):
    return lax.broadcasted_iota(jnp.int32, (rows, LX), 0)


def within(lane, start, count):
    return ((lane - start) & (LX - 1)) < count


def turn(value, block, sign, offset):
    value = roll(value, -offset, 0)
    for bit in (1, 2, 4, 8):
        value = jnp.where((block & bit) != 0, roll(value, -sign * bit, 0), value)
    return value


def cell_block():
    return ((lanes_of(BLOCKS) + BLOCK // 2) // BLOCK) & (BLOCKS - 1)


def stencil_kernel(
    give,
    now_hbm,
    prev_hbm,
    phase_hbm,
    div_hbm,
    *refs,
):
    if give:
        out_hbm, now_ref, prev_ref, phase_ref, div_ref, out, sems, out_sems = refs
    else:
        (
            other_hbm, out_hbm, now_ref, prev_ref, phase_ref, div_ref, out, sems, out_sems,
            other, other_sem,
        ) = refs
    core = lax.axis_index("c")
    base = SHARE * (1 - core if give else core)
    copies, sent = [], []
    for g in range(SHARE // GROUP):
        first = GROUP * g + 2 if g else 0
        count = GROUP * (g + 1) + 2 - first
        copies.append(
            [
                pltpu.make_async_copy(
                    source.at[pl.ds(base + start, size)],
                    target.at[pl.ds(start, size)],
                    sems.at[g, a],
                )
                for a, (source, target, start, size) in enumerate(
                    (
                        (now_hbm, now_ref, first, count),
                        (prev_hbm, prev_ref, first, count),
                        (phase_hbm, phase_ref, first, count),
                        (div_hbm, div_ref, GROUP * g, GROUP),
                    )
                )
            ]
        )
        for copy in copies[-1]:
            copy.start()
    if not give:
        other_copy = pltpu.make_async_copy(other_hbm, other, other_sem.at[0])
        other_copy.start()

    lane = lanes_of(LY)
    row = rows_of(LY)
    sub = rows_of(8)
    block = cell_block()
    lane_in = lanes_of(PER_PLANE)
    slots = [(1 - core) * 16, (1 - core) * 16, core * 16, core * 16]
    x_lanes = [
        [within(lane_in, QUARTER * q + slots[q] + 8 + 2 * t, 2) for t in range(2)] for q in range(4)
    ]
    owner = rows_of(BLOCKS) * BLOCK
    y_lanes = [within(lanes_of(BLOCKS), QUARTER * f + 16 * core + owner, BLOCK) for f in range(4)]

    def plane(k):
        return 2.0 * now_ref[k] - prev_ref[k], phase_ref[k].astype(F32)

    for k in range(SHARE):
        if k % GROUP == 0:
            for copy in copies[k // GROUP]:
                copy.wait()
        if k == 0:
            field_before, liquid_before = plane(0)
            field, liquid = plane(1)
            flux_z = flux(liquid_before, liquid, field_before, field)
        field_after, liquid_after = plane(k + 2)
        flux_z_upper = flux(liquid, liquid_after, field, field_after)
        total = div_ref[k] + (flux_z_upper - flux_z)
        upper = flux(liquid, roll(liquid, -1, 1), field, roll(field, -1, 1))
        upper = jnp.where(lane == LX - 1, 0.0, upper)
        total = total + (upper - roll(upper, 1, 1))
        upper = flux(liquid, roll(liquid, -1, 0), field, roll(field, -1, 0))
        upper = jnp.where(row == LY - 1, 0.0, upper)
        total = total + (upper - roll(upper, 1, 0))
        faces = jnp.zeros((PER_PLANE, LX), F32)
        for q, column in enumerate(
            (field[:, 0:1], liquid[:, 0:1], field[:, LX - 1 : LX], liquid[:, LX - 1 : LX])
        ):
            column = jnp.broadcast_to(column, (LY, LX))
            faces = jnp.where(x_lanes[q][0], column[:HALF], faces)
            second = jnp.concatenate(
                [roll(column[HALF + WIDE :], 1, 0), column[HALF : HALF + WIDE]], axis=0
            )
            faces = jnp.where(x_lanes[q][1], second, faces)
        faces = pltpu.roll(faces, 0, 1, stride=BLOCK, stride_axis=0)
        lines = jnp.broadcast_to(liquid[LY - 1 : LY], (8, LX))
        for f, line in ((2, field[LY - 1 : LY]), (1, liquid[0:1]), (0, field[0:1])):
            lines = jnp.where(sub <= f, jnp.broadcast_to(line, (8, LX)), lines)
        lines = roll(lines, BLOCK // 2 + 16 * core, 1)
        for bit in (1, 2):
            lines = jnp.where((sub & bit) != 0, roll(lines, QUARTER * bit, 1), lines)
        y_faces = faces[:BLOCKS]
        for f in range(4):
            y_faces = jnp.where(
                y_lanes[f], jnp.broadcast_to(lines[f : f + 1], (BLOCKS, LX)), y_faces
            )

        rows = (
            jnp.concatenate([turn(total[:BLOCKS], block, -1, 0), total[BLOCKS:HALF]], axis=0),
            jnp.concatenate(
                [turn(total[HALF + WIDE :], block, -1, 15), total[HALF : HALF + WIDE]], axis=0
            ),
            jnp.concatenate([y_faces, faces[BLOCKS:]], axis=0),
        )
        if give:
            for r in range(3):
                out[pl.ds(k * PER_PLANE * 3 + r, PER_PLANE, stride=3), :] = rows[r]
        else:
            if k == 0:
                other_copy.wait()
            start = k * PER_PLANE * 3
            theirs = [other[pl.ds(start + r, PER_PLANE, stride=3), :] for r in range(3)]
            start = k * PER_PLANE * 5
            for r in range(2):
                lower = jnp.where(core == 0, rows[r], theirs[r])
                upper = jnp.where(core == 0, theirs[r], rows[r])
                out[pl.ds(start + r, PER_PLANE, stride=5), :] = lower
                out[pl.ds(start + 2 + r, PER_PLANE, stride=5), :] = upper
            out[pl.ds(start + 4, PER_PLANE, stride=5), :] = rows[2] + theirs[2]
        field, liquid, flux_z = field_after, liquid_after, flux_z_upper
        if k % GROUP == GROUP - 1:
            g = k // GROUP
            size = GROUP * PER_PLANE * (3 if give else 5)
            part = pl.ds(g * size, size)
            sent.append(pltpu.make_async_copy(out.at[part], out_hbm.at[part], out_sems.at[g]))
            sent[-1].start()
    for copy in sent:
        copy.wait()


def device_kernel(x_ref, high_ref, low_ref, out, cells):
    lane = lanes_of(N_GY)
    in_y = (lane & 15) < BLOCK
    next_chip = (lane & 16) != 0
    at_last, at_first = lane == LX - 1, lane == 0
    own = (lax.axis_index("zl") * 4 + lax.axis_index("y")) % BLOCKS * BLOCK
    groups = N_GX // 2

    def rows(g, r):
        return x_ref[pl.ds((g % groups) * N_GY * 5 + r, N_GY, stride=5), :]

    def aligned(g):
        return roll(rows(g, 4), LX - own, 1)

    def face_flux(here, there):
        lower = jnp.where(in_y, roll(here, -1, 0), jnp.where(next_chip, there, here))
        upper = roll(here, -2 * QUARTER, 1)
        return weighted(roll(upper + lower, -QUARTER, 1), lower - upper)

    def x_parts(through, c):
        return [roll(through, LX - 1 - (16 * c + 8 + 2 * t), 1) for t in range(2)]

    last, here = aligned(groups - 1), aligned(0)
    entering = x_parts(face_flux(last, here), 1)
    for g in range(groups):
        there = aligned(g + 1)
        through = face_flux(here, there)
        leaving = [x_parts(through, c) for c in range(2)]
        for c in range(2):
            along_y = jnp.where(within(lane, 16 * c, BLOCK), through, 0.0)
            along_y = roll(along_y, own + (LX - BLOCK // 2 - 16 * c), 1)
            before = leaving[0] if c else entering
            part = [
                rows(g, 2 * c + t)
                + jnp.where(at_last, leaving[c][t], 0.0)
                - jnp.where(at_first, before[t], 0.0)
                for t in range(2)
            ]
            place = pl.ds(c * N_CHIP + g * N_GY, N_GY)
            cells[place, :LX] = part[0] - roll(along_y, 1, 0)
            cells[place, LX:] = part[1] + along_y
        here, entering = there, leaving[1]

    right = split(cells[...])
    for part in range(2):
        table = pl.ds(part * N_ALL, N_ALL)
        result = dot3((high_ref[table, :], low_ref[table, :]), right)
        out[pl.ds(2 * part, N_ALL, stride=4), :] = result[:, :LX]
        out[pl.ds(2 * part + 1, N_ALL, stride=4), :] = result[:, LX:]


def local_kernel(x_ref, y_matrix_ref, x_matrix_ref, out_hbm, out, sems):
    y_matrix = split(y_matrix_ref[...])
    x_matrix = split(x_matrix_ref[...])
    block = cell_block()
    copies = []
    for k in range(PLANES):
        start = (2 * (k % SHARE) + k // SHARE) * 2 * LY
        lines = [
            turn(x_ref[pl.ds(start + kind, BLOCKS, stride=4), :], block, 1, kind & 1)
            for kind in range(4)
        ]
        lines.append(x_ref[pl.ds(start + 4 * BLOCKS, 4 * WIDE), :])
        lines = dot3(y_matrix, split(jnp.concatenate(lines, axis=0)))
        lines = jnp.concatenate([lines[:LY], lines[LY:]], axis=1)
        modes = dot3(split(lines), x_matrix)
        out[0, k] = modes[:, :LX]
        out[1, k] = modes[:, LX:]
        if k % GROUP == GROUP - 1:
            g = k // GROUP
            for part in range(2):
                planes = (part, pl.ds(g * GROUP, GROUP))
                copies.append(
                    pltpu.make_async_copy(out.at[planes], out_hbm.at[planes], sems.at[g, part])
                )
                copies[-1].start()
    for copy in copies:
        copy.wait()


def device_tables():
    dest = np.arange(N_ALL)
    rev_p = np.array([reversal(i, 4) for i in range(N_GX)])
    rev_q = np.array([reversal(i, 5) for i in range(N_GY)])
    kx = rev_p[dest // N_GY][:, None]
    ky = rev_q[dest % N_GY][:, None]
    source = np.arange(N_ALL)
    gx = (2 * (source % N_CHIP // N_GY) + source // N_CHIP)[None]
    gy = (source % N_GY)[None]
    angle = (2 * kx * gx + ky * gy) % N_GY * (2.0 * math.pi / N_GY)
    table = np.concatenate([np.cos(angle), -np.sin(angle)])
    high = table.astype(ml_dtypes.bfloat16)
    return high, (table - high.astype(np.float64)).astype(ml_dtypes.bfloat16)


def cos_sin(place, mode, length):
    angle = ((place * mode) % length).astype(F32) * (2.0 * math.pi / length)
    return jnp.cos(angle), jnp.sin(angle)


def local_tables():
    rp = reversal(lax.axis_index(("zh", "x", "c")), 4)
    rq = reversal(lax.axis_index(("zl", "y")), 5)
    line = lax.broadcasted_iota(jnp.int32, (2 * LY, 2 * LY), 0)
    col = lax.broadcasted_iota(jnp.int32, (2 * LY, 2 * LY), 1)
    rest = col - 4 * BLOCKS
    in_block = rest < 0
    part_in = jnp.where(in_block, col // (2 * BLOCKS), rest >> 1) & 1
    place = jnp.where(
        in_block,
        col % BLOCKS + (LY - BLOCKS) * (col // BLOCKS & 1),
        BLOCKS + (rest >> 2) + WIDE * (rest & 1),
    )
    cosine, sine = cos_sin(place, 32 * (line % LY) + rq, NY)
    part_out = line // LY
    sign = jnp.where(part_out < part_in, 1.0, -1.0)
    y_matrix = jnp.where(part_out == part_in, cosine, sign * sine) * (1.0 / math.sqrt(NX * NY))
    line = lax.broadcasted_iota(jnp.int32, (2 * LX, 2 * LX), 0)
    col = lax.broadcasted_iota(jnp.int32, (2 * LX, 2 * LX), 1)
    cosine, sine = cos_sin(line % LX, 16 * (col % LX) + rp, NX)
    part_in, part_out = line // LX, col // LX
    sign = jnp.where(part_out < part_in, 1.0, -1.0)
    x_matrix = jnp.where(part_out == part_in, cosine, sign * sine)
    return y_matrix, x_matrix


def call(kernel, outs, *args, scratch=(), in_hbm=False, out_hbm=False, mib=40):
    def spec(hbm):
        return pl.BlockSpec(memory_space=pltpu.HBM if hbm else pltpu.VMEM)

    in_specs = [spec(in_hbm)] * len(args)
    if in_hbm:
        in_specs[4:] = [pl.BlockSpec(memory_space=pl.ANY)] * len(in_specs[4:])

    return pl.pallas_call(
        kernel,
        out_shape=outs,
        in_specs=in_specs,
        out_specs=spec(out_hbm),
        scratch_shapes=scratch,
        compiler_params=pltpu.CompilerParams(vmem_limit_bytes=mib * 1024 * 1024),
    )(*args)


def shape(*dims):
    return jax.ShapeDtypeStruct(dims, F32)


def stencil(give, rows, *args):
    padded = (SHARE + 2, LY, LX)
    scratch = [
        pltpu.VMEM(padded, F32),
        pltpu.VMEM(padded, F32),
        pltpu.VMEM(padded, jnp.int32),
        pltpu.VMEM((SHARE, LY, LX), F32),
        pltpu.VMEM((rows * N_CHIP, LX), F32),
        pltpu.SemaphoreType.DMA((SHARE // GROUP, 4)),
        pltpu.SemaphoreType.DMA((SHARE // GROUP,)),
    ]
    if not give:
        scratch += [pltpu.VMEM((3 * N_CHIP, LX), F32), pltpu.SemaphoreType.DMA((1,))]
    return call(
        functools.partial(stencil_kernel, give),
        shape(rows * N_CHIP, LX),
        *args,
        scratch=scratch,
        in_hbm=True,
        out_hbm=True,
        mib=60,
    )


def body(*args):
    given = stencil(True, 3, *args)
    given = lax.ppermute(given, "c", [(0, 1), (1, 0)])
    chunks = stencil(False, 5, *args, given)
    chunks = lax.all_to_all(chunks.reshape(N_CHIP, 1, 5 * LX), CHIPS, 0, 0, tiled=True)
    high, low = device_tables()
    modes = call(
        device_kernel,
        shape(4 * N_ALL, LX),
        chunks.reshape(5 * N_CHIP, LX),
        jnp.asarray(high),
        jnp.asarray(low),
        scratch=[pltpu.VMEM((N_ALL, 2 * LX), F32)],
    )
    back = lax.all_to_all(modes.reshape(N_ALL, 4, LX), EVERYWHERE, 0, 0, tiled=True)
    y_matrix, x_matrix = local_tables()
    result = call(
        local_kernel,
        shape(2, PLANES, LY, LX),
        back.reshape(4 * N_ALL, LX),
        y_matrix,
        x_matrix,
        scratch=[
            pltpu.VMEM((2, PLANES, LY, LX), F32),
            pltpu.SemaphoreType.DMA((PLANES // GROUP, 2)),
        ],
        out_hbm=True,
    )
    return result.reshape(2, PLANES, 1, LY, 1, LX)


def solution(mesh):
    fine = Mesh(mesh.devices.reshape(2, 4, 2, 8, 4), EVERYWHERE)
    spec = P(None, ("zl", "y"), ("zh", "x", "c"))
    return jax.shard_map(
        body,
        mesh=fine,
        in_specs=(spec, spec, spec, spec),
        out_specs=P(None, None, ("zl", "y"), None, ("zh", "x", "c"), None),
        check_vma=False,
    )
```

```python
import math

import jax
import jax.numpy as jnp
import ml_dtypes
import numpy as np
from jax import lax
from jax.experimental import pallas as pl
from jax.experimental.pallas import tpu as pltpu
from jax.sharding import PartitionSpec as P

NX = 2048
NY = 2048
PLANES = 16
LY = 64
LX = 128
N_GX = 16
N_GY = 32
N_ALL = N_GX * N_GY
F32 = jnp.float32
BF16 = jnp.bfloat16

QUAD = 7.0 / 16.0 - 7.0 / 9.0
LIN = 7.0 / 9.0 - QUAD

BLOCKS = 8
BLOCK = LX // BLOCKS
PER_PLANE = N_ALL // PLANES
WIDE = PER_PLANE - BLOCKS
HALF = LY // 2
GROUP = 4


def reversal(index, digits):
    total = 0
    for place in range(digits):
        total = total * 2 + ((index >> place) & 1)
    return total


def split(value):
    high = value.astype(BF16)
    return high, (value - high.astype(F32)).astype(BF16)


def dot3(left, right):
    left_high, left_low = left
    right_high, right_low = right
    return (
        jnp.dot(left_high, right_high, preferred_element_type=F32)
        + jnp.dot(left_high, right_low, preferred_element_type=F32)
        + jnp.dot(left_low, right_high, preferred_element_type=F32)
    )


def flux(liquid_a, liquid_b, field_a, field_b):
    count = liquid_a + liquid_b
    return count * (LIN + QUAD * count) * (field_b - field_a)


def roll(value, by, axis):
    by = by % value.shape[axis]
    return pltpu.roll(value, by, axis) if by else value


def lanes_of(rows):
    return lax.broadcasted_iota(jnp.int32, (rows, LX), 1)


def rows_of(rows):
    return lax.broadcasted_iota(jnp.int32, (rows, LX), 0)


def turn(value, block, sign, offset):
    value = roll(value, -offset, 0)
    for bit in (1, 2, 4):
        value = jnp.where((block & bit) != 0, roll(value, -sign * bit, 0), value)
    return value


def cell_block():
    return ((lanes_of(BLOCKS) + BLOCK // 2) // BLOCK) & (BLOCKS - 1)


def face_block(rows):
    lane = (lanes_of(rows) + LX - 1) & (LX - 1)
    return lane // BLOCK, lane % BLOCK < BLOCK // 2


def stencil_kernel(
    now_hbm,
    prev_hbm,
    phase_hbm,
    div_hbm,
    out_hbm,
    now_ref,
    prev_ref,
    phase_ref,
    div_ref,
    out,
    sems,
    out_sems,
):
    copies, sent = [], []
    for g in range(PLANES // GROUP):
        first = GROUP * g + 2 if g else 0
        planes = pl.ds(first, GROUP * (g + 1) + 2 - first)
        inner = pl.ds(GROUP * g, GROUP)
        copies.append(
            [
                pltpu.make_async_copy(source.at[part], target.at[part], sems.at[g, a])
                for a, (source, target, part) in enumerate(
                    (
                        (now_hbm, now_ref, planes),
                        (prev_hbm, prev_ref, planes),
                        (phase_hbm, phase_ref, planes),
                        (div_hbm, div_ref, inner),
                    )
                )
            ]
        )
        for copy in copies[-1]:
            copy.start()

    lane = lanes_of(LY)
    row = rows_of(LY)
    edge_lane = (lane == 0) | (lane == LX - 1)
    sub = rows_of(BLOCKS)
    block = cell_block()
    line_block, in_half = face_block(BLOCKS)

    def plane(k):
        return 2.0 * now_ref[k] - prev_ref[k], phase_ref[k].astype(F32)

    for k in range(PLANES):
        if k % GROUP == 0:
            for copy in copies[k // GROUP]:
                copy.wait()
        if k == 0:
            field_before, liquid_before = plane(0)
            field, liquid = plane(1)
            flux_z = flux(liquid_before, liquid, field_before, field)
        field_after, liquid_after = plane(k + 2)
        flux_z_upper = flux(liquid, liquid_after, field, field_after)
        total = div_ref[k] + (flux_z_upper - flux_z)
        upper = flux(liquid, roll(liquid, -1, 1), field, roll(field, -1, 1))
        upper = jnp.where(lane == LX - 1, 0.0, upper)
        total = total + (upper - roll(upper, 1, 1))
        upper = flux(liquid, roll(liquid, -1, 0), field, roll(field, -1, 0))
        upper = jnp.where(row == LY - 1, 0.0, upper)
        total = total + (upper - roll(upper, 1, 0))
        ends = jnp.where(edge_lane, field, 0.0)
        wet_ends = jnp.where(edge_lane, liquid, 0.0)
        first = ends[:HALF] + roll(wet_ends[:HALF], -2, 1)
        second = roll(ends[HALF:], -4, 1) + roll(wet_ends[HALF:], -6, 1)
        lines = jnp.broadcast_to(liquid[LY - 1 : LY], (BLOCKS, LX))
        for f, line in ((2, field[LY - 1 : LY]), (1, liquid[0:1]), (0, field[0:1])):
            lines = jnp.where(sub < 2 * f + 2, jnp.broadcast_to(line, (BLOCKS, LX)), lines)
        lines = roll(lines, 9, 1)
        for bit, by in ((1, 8), (2, 32), (4, 64)):
            lines = jnp.where((sub & bit) != 0, roll(lines, by, 1), lines)
        lines = turn(jnp.where(in_half, lines, 0.0), line_block, 1, 0)

        start = k * PER_PLANE * 3
        out[pl.ds(start, BLOCKS, stride=3), :] = turn(total[:BLOCKS], block, 1, 0)
        out[pl.ds(start + 1, BLOCKS, stride=3), :] = turn(total[LY - BLOCKS :], block, 1, 7)
        out[pl.ds(start + 2, BLOCKS, stride=3), :] = (
            first[:BLOCKS] + roll(second[WIDE:], 1, 0) + lines
        )
        start += BLOCKS * 3
        out[pl.ds(start, WIDE, stride=3), :] = total[BLOCKS:HALF]
        out[pl.ds(start + 1, WIDE, stride=3), :] = total[HALF : HALF + WIDE]
        out[pl.ds(start + 2, WIDE, stride=3), :] = first[BLOCKS:] + second[:WIDE]
        field, liquid, flux_z = field_after, liquid_after, flux_z_upper
        if k % GROUP == GROUP - 1:
            g = k // GROUP
            rows = pl.ds(g * GROUP * PER_PLANE * 3, GROUP * PER_PLANE * 3)
            sent.append(pltpu.make_async_copy(out.at[rows], out_hbm.at[rows], out_sems.at[g]))
            sent[-1].start()
    for copy in sent:
        copy.wait()


def device_kernel(x_ref, high_ref, low_ref, out, cells):
    last_lane = lanes_of(N_GY) == LX - 1
    own = (BLOCKS - lax.axis_index("gy") % BLOCKS) % BLOCKS
    line_block, in_half = face_block(N_GY)
    first_half = in_half & (line_block == own)
    second_half = in_half & (line_block == (own + 1) % BLOCKS)

    def group(g, r):
        return x_ref[pl.ds((g % N_GX) * N_GY * 3 + r, N_GY, stride=3), :]

    def x_flux(here, there, t):
        through = flux(
            roll(here, 2 + 4 * t, 1),
            roll(there, 1 + 4 * t, 1),
            roll(here, 4 * t, 1),
            roll(there, 4 * t - 1, 1),
        )
        return jnp.where(last_lane, through, 0.0)

    last = group(N_GX - 1, 2)
    here = group(0, 2)
    entering = [x_flux(last, here, t) for t in range(2)]
    for g in range(N_GX):
        there = group(g + 1, 2)
        first, second = group(g, 0), group(g, 1)
        leaving = [x_flux(here, there, t) for t in range(2)]
        first = first + (leaving[0] - roll(entering[0], 1, 1))
        second = second + (leaving[1] - roll(entering[1], 1, 1))
        after = roll(here, -1, 0)
        through = flux(roll(here, -96, 1), roll(after, -32, 1), roll(here, -64, 1), after)
        through = roll(jnp.where(first_half, through, 0.0), -9, 1) + roll(
            jnp.where(second_half, through, 0.0), -17, 1
        )
        cells[pl.ds(g * N_GY, N_GY), :LX] = first - roll(through, 1, 0)
        cells[pl.ds(g * N_GY, N_GY), LX:] = second + through
        here, entering = there, leaving

    right_high, right_low = split(cells[...])
    result = dot3((high_ref[...], low_ref[...]), (right_high, right_low))
    for part in range(2):
        rows = slice(part * N_ALL, (part + 1) * N_ALL)
        out[pl.ds(2 * part, N_ALL, stride=4), :] = result[rows, :LX]
        out[pl.ds(2 * part + 1, N_ALL, stride=4), :] = result[rows, LX:]


def local_kernel(x_ref, y_matrix_ref, cos_ref, sin_ref, out_hbm, out, sems):
    y_matrix = split(y_matrix_ref[...])
    x_matrix = split(
        jnp.concatenate(
            [
                jnp.concatenate([cos_ref[...], -sin_ref[...]], axis=1),
                jnp.concatenate([sin_ref[...], cos_ref[...]], axis=1),
            ],
            axis=0,
        )
    )
    block = cell_block()
    copies = []
    for g in range(PLANES // GROUP):
        group = []
        for k in range(GROUP * g, GROUP * (g + 1)):
            start = k * 2 * LY
            lines = [
                turn(x_ref[pl.ds(start + kind, BLOCKS, stride=4), :], block, -1, kind & 1)
                for kind in range(4)
            ]
            lines.append(x_ref[pl.ds(start + 4 * BLOCKS, 4 * WIDE), :])
            group.append(jnp.concatenate(lines, axis=0))
        lines = dot3(y_matrix, split(jnp.concatenate(group, axis=1)))
        lines = jnp.concatenate(
            [
                jnp.concatenate(
                    [lines[:LY, k * LX : (k + 1) * LX], lines[LY:, k * LX : (k + 1) * LX]], axis=1
                )
                for k in range(GROUP)
            ],
            axis=0,
        )
        modes = dot3(split(lines), x_matrix)
        for part in range(2):
            for k in range(GROUP):
                out[part, GROUP * g + k] = modes[k * LY : (k + 1) * LY, part * LX : (part + 1) * LX]
            planes = (part, pl.ds(g * GROUP, GROUP))
            copies.append(
                pltpu.make_async_copy(out.at[planes], out_hbm.at[planes], sems.at[g, part])
            )
            copies[-1].start()
    for copy in copies:
        copy.wait()


def device_tables():
    source = np.arange(N_ALL)
    rev_p = np.array([reversal(i, 4) for i in range(N_GX)])
    rev_q = np.array([reversal(i, 5) for i in range(N_GY)])
    kx = rev_p[source // N_GY][:, None]
    ky = rev_q[source % N_GY][:, None]
    turns = (2 * kx * (source // N_GY)[None] + ky * (source % N_GY)[None]) % N_GY
    angle = turns * (2.0 * math.pi / N_GY)
    table = np.concatenate([np.cos(angle), -np.sin(angle)])
    high = table.astype(ml_dtypes.bfloat16)
    return high, (table - high.astype(np.float64)).astype(ml_dtypes.bfloat16)


def cos_sin(place, mode, length):
    angle = ((place * mode) % length).astype(F32) * (2.0 * math.pi / length)
    return jnp.cos(angle), jnp.sin(angle)


def local_tables(rp, rq):
    line = lax.broadcasted_iota(jnp.int32, (2 * LY, 2 * LY), 0)
    col = lax.broadcasted_iota(jnp.int32, (2 * LY, 2 * LY), 1)
    rest = col - 4 * BLOCKS
    in_block = rest < 0
    part_in = jnp.where(in_block, col >> 4, rest >> 1) & 1
    place = jnp.where(
        in_block,
        (col & 7) + (LY - BLOCKS) * ((col >> 3) & 1),
        BLOCKS + (rest >> 2) + WIDE * (rest & 1),
    )
    cosine, sine = cos_sin(place, 32 * (line % LY) + rq, NY)
    part_out = line // LY
    sign = jnp.where(part_out < part_in, 1.0, -1.0)
    y_matrix = jnp.where(part_out == part_in, cosine, sign * sine) * (1.0 / math.sqrt(NX * NY))
    line = lax.broadcasted_iota(jnp.int32, (LX, LX), 0)
    col = lax.broadcasted_iota(jnp.int32, (LX, LX), 1)
    return (y_matrix, *cos_sin(line, 16 * col + rp, NX))


def call(kernel, outs, *args, scratch=(), in_hbm=False, out_hbm=False, mib=40):
    def spec(hbm):
        return pl.BlockSpec(memory_space=pltpu.HBM if hbm else pltpu.VMEM)

    return pl.pallas_call(
        kernel,
        out_shape=outs,
        in_specs=[spec(in_hbm)] * len(args),
        out_specs=spec(out_hbm),
        scratch_shapes=scratch,
        compiler_params=pltpu.CompilerParams(vmem_limit_bytes=mib * 1024 * 1024),
    )(*args)


def shape(*dims):
    return jax.ShapeDtypeStruct(dims, F32)


def body(p_now, p_prev, phase, div_star):
    padded = (PLANES + 2, LY, LX)
    chunks = call(
        stencil_kernel,
        shape(3 * N_ALL, LX),
        p_now,
        p_prev,
        phase,
        div_star,
        scratch=[
            pltpu.VMEM(padded, F32),
            pltpu.VMEM(padded, F32),
            pltpu.VMEM(padded, jnp.int32),
            pltpu.VMEM((PLANES, LY, LX), F32),
            pltpu.VMEM((3 * N_ALL, LX), F32),
            pltpu.SemaphoreType.DMA((PLANES // GROUP, 4)),
            pltpu.SemaphoreType.DMA((PLANES // GROUP,)),
        ],
        in_hbm=True,
        out_hbm=True,
        mib=60,
    )
    everywhere = ("gx", "gy")
    chunks, rp, rq = lax.optimization_barrier(
        (chunks, reversal(lax.axis_index("gx"), 4), reversal(lax.axis_index("gy"), 5))
    )
    tables = local_tables(rp, rq)
    chunks = lax.all_to_all(chunks.reshape(N_ALL, 1, 3 * LX), everywhere, 0, 0, tiled=True)
    chunks, tables = lax.optimization_barrier((chunks, tables))
    high, low = device_tables()
    modes = call(
        device_kernel,
        shape(4 * N_ALL, LX),
        chunks.reshape(3 * N_ALL, LX),
        jnp.asarray(high),
        jnp.asarray(low),
        scratch=[pltpu.VMEM((N_ALL, 2 * LX), F32)],
    )
    back = lax.all_to_all(modes.reshape(N_ALL, 4, LX), everywhere, 0, 0, tiled=True)
    result = call(
        local_kernel,
        shape(2, PLANES, LY, LX),
        back.reshape(4 * N_ALL, LX),
        *tables,
        scratch=[
            pltpu.VMEM((2, PLANES, LY, LX), F32),
            pltpu.SemaphoreType.DMA((PLANES // GROUP, 2)),
        ],
        out_hbm=True,
    )
    return result.reshape(2, PLANES, 1, LY, 1, LX)


def solution(mesh):
    spec = P(None, "gy", "gx")
    return jax.shard_map(
        body,
        mesh=mesh,
        in_specs=(spec, spec, spec, spec),
        out_specs=P(None, None, "gy", None, "gx", None),
        check_vma=False,
    )
```

```python
import math

import jax
import jax.numpy as jnp
import ml_dtypes
import numpy as np
from jax import lax
from jax.experimental import pallas as pl
from jax.experimental.pallas import tpu as pltpu
from jax.sharding import Mesh
from jax.sharding import PartitionSpec as P

NX = 2048
NY = 2048
PLANES = 16
LY = 64
LX = 128
N_GX = 16
N_GY = 32
N_ALL = N_GX * N_GY
N_CHIP = N_ALL // 2
F32 = jnp.float32
BF16 = jnp.bfloat16

CHIPS = ("zh", "x", "zl", "y")
EVERYWHERE = ("zh", "x", "c", "zl", "y")

QUAD = 7.0 / 16.0 - 7.0 / 9.0
LIN = 7.0 / 9.0 - QUAD

BLOCKS = 16
BLOCK = LX // BLOCKS
WIDE = 16
HALF = LY // 2
TEAMS = PLANES
ROWS = 5
GROUP = 4
QUARTER = LX // 4


def reversal(index, digits):
    total = 0
    for place in range(digits):
        total = total * 2 + ((index >> place) & 1)
    return total


def split(value):
    high = value.astype(BF16)
    return high, (value - high.astype(F32)).astype(BF16)


def dot3(left, right):
    left_high, left_low = left
    right_high, right_low = right
    return (
        jnp.dot(left_high, right_high, preferred_element_type=F32)
        + jnp.dot(left_high, right_low, preferred_element_type=F32)
        + jnp.dot(left_low, right_high, preferred_element_type=F32)
    )


def weighted(count, difference):
    return count * (LIN + QUAD * count) * difference


def flux(liquid_a, liquid_b, field_a, field_b):
    return weighted(liquid_a + liquid_b, field_b - field_a)


def roll(value, by, axis):
    if isinstance(by, int):
        by = by % value.shape[axis]
        return pltpu.roll(value, by, axis) if by else value
    return pltpu.roll(value, by & (value.shape[axis] - 1), axis)


def lanes_of(rows):
    return lax.broadcasted_iota(jnp.int32, (rows, LX), 1)


def rows_of(rows):
    return lax.broadcasted_iota(jnp.int32, (rows, LX), 0)


def within(lane, start, count):
    return ((lane - start) & (LX - 1)) < count


def turn(value, block, sign, offset):
    value = roll(value, -offset, 0)
    for bit in (1, 2, 4, 8):
        value = jnp.where((block & bit) != 0, roll(value, -sign * bit, 0), value)
    return value


def cell_block():
    return ((lanes_of(BLOCKS) + BLOCK // 2) // BLOCK) & (BLOCKS - 1)


def stencil_kernel(
    now_hbm,
    prev_hbm,
    phase_hbm,
    div_hbm,
    out_hbm,
    now_ref,
    prev_ref,
    phase_ref,
    div_ref,
    out,
    sems,
    out_sems,
):
    copies, sent = [], []
    for g in range(PLANES // GROUP):
        first = GROUP * g + 2 if g else 0
        planes = pl.ds(first, GROUP * (g + 1) + 2 - first)
        inner = pl.ds(GROUP * g, GROUP)
        copies.append(
            [
                pltpu.make_async_copy(source.at[part], target.at[part], sems.at[g, a])
                for a, (source, target, part) in enumerate(
                    (
                        (now_hbm, now_ref, planes),
                        (prev_hbm, prev_ref, planes),
                        (phase_hbm, phase_ref, planes),
                        (div_hbm, div_ref, inner),
                    )
                )
            ]
        )
        for copy in copies[-1]:
            copy.start()

    lane = lanes_of(LY)
    row = rows_of(LY)
    sub = rows_of(8)
    block = cell_block()
    lane_in = lanes_of(TEAMS)
    owner = rows_of(TEAMS) * BLOCK
    x_lanes = [
        [within(lane_in, QUARTER * q + 8 + 2 * t, 2) for t in range(4)] for q in range(4)
    ]
    y_lanes = [within(lane_in, QUARTER * f + owner, BLOCK) for f in range(4)]

    def plane(k):
        return 2.0 * now_ref[k] - prev_ref[k], phase_ref[k].astype(F32)

    for k in range(PLANES):
        if k % GROUP == 0:
            for copy in copies[k // GROUP]:
                copy.wait()
        if k == 0:
            field_before, liquid_before = plane(0)
            field, liquid = plane(1)
            flux_z = flux(liquid_before, liquid, field_before, field)
        field_after, liquid_after = plane(k + 2)
        flux_z_upper = flux(liquid, liquid_after, field, field_after)
        total = div_ref[k] + (flux_z_upper - flux_z)
        upper = flux(liquid, roll(liquid, -1, 1), field, roll(field, -1, 1))
        upper = jnp.where(lane == LX - 1, 0.0, upper)
        total = total + (upper - roll(upper, 1, 1))
        upper = flux(liquid, roll(liquid, -1, 0), field, roll(field, -1, 0))
        upper = jnp.where(row == LY - 1, 0.0, upper)
        total = total + (upper - roll(upper, 1, 0))
        faces = jnp.zeros((TEAMS, LX), F32)
        for q, column in enumerate(
            (field[:, 0:1], liquid[:, 0:1], field[:, LX - 1 : LX], liquid[:, LX - 1 : LX])
        ):
            column = jnp.broadcast_to(column, (LY, LX))
            edge = roll(column[LY - BLOCKS :], 1, 0)
            for t, part in enumerate(
                (column[:BLOCKS], edge, column[BLOCKS:HALF], column[HALF : HALF + WIDE])
            ):
                faces = jnp.where(x_lanes[q][t], part, faces)
        faces = pltpu.roll(faces, 0, 1, stride=BLOCK, stride_axis=0)
        lines = jnp.broadcast_to(liquid[LY - 1 : LY], (8, LX))
        for f, line in ((2, field[LY - 1 : LY]), (1, liquid[0:1]), (0, field[0:1])):
            lines = jnp.where(sub <= f, jnp.broadcast_to(line, (8, LX)), lines)
        lines = roll(lines, BLOCK // 2, 1)
        for bit in (1, 2):
            lines = jnp.where((sub & bit) != 0, roll(lines, QUARTER * bit, 1), lines)
        for f in range(4):
            faces = jnp.where(y_lanes[f], jnp.broadcast_to(lines[f : f + 1], (TEAMS, LX)), faces)

        start = k * TEAMS * ROWS
        for r, value in enumerate(
            (
                turn(total[:BLOCKS], block, -1, 0),
                turn(total[LY - BLOCKS :], block, -1, 15),
                total[BLOCKS:HALF],
                total[HALF : HALF + WIDE],
                faces,
            )
        ):
            out[pl.ds(start + r, TEAMS, stride=ROWS), :] = value
        field, liquid, flux_z = field_after, liquid_after, flux_z_upper
        if k % GROUP == GROUP - 1:
            g = k // GROUP
            rows = pl.ds(g * GROUP * TEAMS * ROWS, GROUP * TEAMS * ROWS)
            sent.append(pltpu.make_async_copy(out.at[rows], out_hbm.at[rows], out_sems.at[g]))
            sent[-1].start()
    for copy in sent:
        copy.wait()


def device_kernel(own_ref, other_ref, high_ref, low_ref, out, cells):
    lane = lanes_of(N_GY)
    core = lax.axis_index("c")
    team = (lax.axis_index("zl") * 4 + lax.axis_index("y")) % TEAMS * BLOCK
    in_y = (lane & 15) < BLOCK
    own_y = (lane < BLOCK) & (core == 0)
    at_last, at_first = lane == LX - 1, lane == 0
    groups = N_GX // 2

    def rows(c, g, r):
        place = pl.ds((g % groups) * N_GY * ROWS + r, N_GY, stride=ROWS)
        return jnp.where(core == c, own_ref[place, :], other_ref[place, :])

    def aligned(c, g):
        return roll(rows(c, g, 4), 2 * LX - team - 4 * core, 1)

    def through(here, there):
        lower = jnp.where(in_y, roll(here, -1, 0), there)
        upper = roll(here, -2 * QUARTER, 1)
        return weighted(roll(upper + lower, -QUARTER, 1), lower - upper)

    def x_parts(value):
        return [roll(value, LX - 1 - (8 + 2 * t), 1) for t in range(2)]

    faces = [aligned(c, 0) for c in range(2)]
    entering = x_parts(through(aligned(1, groups - 1), faces[0]))
    for g in range(groups):
        after = [aligned(c, g + 1) for c in range(2)]
        for c in range(2):
            value = through(faces[c], after[0] if c else faces[1])
            leaving = x_parts(value)
            along_y = roll(jnp.where(own_y, value, 0.0), team + (LX - BLOCK // 2), 1)
            part = [
                rows(c, g, 2 * core + t)
                + jnp.where(at_last, leaving[t], 0.0)
                - jnp.where(at_first, entering[t], 0.0)
                for t in range(2)
            ]
            place = pl.ds(c * N_CHIP + g * N_GY, N_GY)
            cells[place, :LX] = part[0] - roll(along_y, 1, 0)
            cells[place, LX:] = part[1] + along_y
            entering = leaving
        faces = after

    right_high, right_low = split(cells[...])
    result = dot3((high_ref[...], low_ref[...]), (right_high, right_low))
    for part in range(2):
        rows = slice(part * N_ALL, (part + 1) * N_ALL)
        out[pl.ds(2 * part, N_ALL, stride=4), :] = result[rows, :LX]
        out[pl.ds(2 * part + 1, N_ALL, stride=4), :] = result[rows, LX:]


def local_kernel(x_ref, y_matrix_ref, cos_ref, sin_ref, out_hbm, out, sems):
    y_matrix = split(y_matrix_ref[...])
    x_matrix = split(
        jnp.concatenate(
            [
                jnp.concatenate([cos_ref[...], -sin_ref[...]], axis=1),
                jnp.concatenate([sin_ref[...], cos_ref[...]], axis=1),
            ],
            axis=0,
        )
    )
    block = cell_block()
    copies = []
    for g in range(PLANES // GROUP):
        group = []
        for k in range(GROUP * g, GROUP * (g + 1)):
            start = (k // 2) * 4 * LY + (k % 2) * LY
            lines = [
                turn(x_ref[pl.ds(start + kind, BLOCKS, stride=4), :], block, 1, kind & 1)
                for kind in range(4)
            ]
            lines.append(x_ref[pl.ds(start + 2 * LY, LY), :])
            group.append(jnp.concatenate(lines, axis=0))
        lines = dot3(y_matrix, split(jnp.concatenate(group, axis=1)))
        lines = jnp.concatenate(
            [
                jnp.concatenate(
                    [lines[:LY, k * LX : (k + 1) * LX], lines[LY:, k * LX : (k + 1) * LX]], axis=1
                )
                for k in range(GROUP)
            ],
            axis=0,
        )
        modes = dot3(split(lines), x_matrix)
        for part in range(2):
            for k in range(GROUP):
                out[part, GROUP * g + k] = modes[k * LY : (k + 1) * LY, part * LX : (part + 1) * LX]
            planes = (part, pl.ds(g * GROUP, GROUP))
            copies.append(
                pltpu.make_async_copy(out.at[planes], out_hbm.at[planes], sems.at[g, part])
            )
            copies[-1].start()
    for copy in copies:
        copy.wait()


def device_tables():
    dest = np.arange(N_ALL)
    rev_p = np.array([reversal(i, 4) for i in range(N_GX)])
    rev_q = np.array([reversal(i, 5) for i in range(N_GY)])
    kx = rev_p[dest // N_GY][:, None]
    ky = rev_q[dest % N_GY][:, None]
    source = np.arange(N_ALL)
    gx = (2 * (source % N_CHIP // N_GY) + source // N_CHIP)[None]
    gy = (source % N_GY)[None]
    angle = (2 * kx * gx + ky * gy) % N_GY * (2.0 * math.pi / N_GY)
    table = np.concatenate([np.cos(angle), -np.sin(angle)])
    high = table.astype(ml_dtypes.bfloat16)
    return high, (table - high.astype(np.float64)).astype(ml_dtypes.bfloat16)


def cos_sin(place, mode, length):
    angle = ((place * mode) % length).astype(F32) * (2.0 * math.pi / length)
    return jnp.cos(angle), jnp.sin(angle)


def local_tables(rp, rq):
    line = lax.broadcasted_iota(jnp.int32, (2 * LY, 2 * LY), 0)
    col = lax.broadcasted_iota(jnp.int32, (2 * LY, 2 * LY), 1)
    rest = col - 4 * BLOCKS
    in_block = rest < 0
    part_in = jnp.where(in_block, col // (2 * BLOCKS), rest >> 1) & 1
    place = jnp.where(
        in_block,
        col % BLOCKS + (LY - BLOCKS) * (col // BLOCKS & 1),
        BLOCKS + (rest >> 2) + WIDE * (rest & 1),
    )
    cosine, sine = cos_sin(place, 32 * (line % LY) + rq, NY)
    part_out = line // LY
    sign = jnp.where(part_out < part_in, 1.0, -1.0)
    y_matrix = jnp.where(part_out == part_in, cosine, sign * sine) * (1.0 / math.sqrt(NX * NY))
    line = lax.broadcasted_iota(jnp.int32, (LX, LX), 0)
    col = lax.broadcasted_iota(jnp.int32, (LX, LX), 1)
    return (y_matrix, *cos_sin(line, 16 * col + rp, NX))


def call(kernel, outs, *args, scratch=(), in_hbm=False, out_hbm=False, mib=40):
    def spec(hbm):
        return pl.BlockSpec(memory_space=pltpu.HBM if hbm else pltpu.VMEM)

    return pl.pallas_call(
        kernel,
        out_shape=outs,
        in_specs=[spec(in_hbm)] * len(args),
        out_specs=spec(out_hbm),
        scratch_shapes=scratch,
        compiler_params=pltpu.CompilerParams(vmem_limit_bytes=mib * 1024 * 1024),
    )(*args)


def shape(*dims):
    return jax.ShapeDtypeStruct(dims, F32)


def body(p_now, p_prev, phase, div_star):
    padded = (PLANES + 2, LY, LX)
    chunks = call(
        stencil_kernel,
        shape(ROWS * N_CHIP, LX),
        p_now,
        p_prev,
        phase,
        div_star,
        scratch=[
            pltpu.VMEM(padded, F32),
            pltpu.VMEM(padded, F32),
            pltpu.VMEM(padded, jnp.int32),
            pltpu.VMEM((PLANES, LY, LX), F32),
            pltpu.VMEM((ROWS * N_CHIP, LX), F32),
            pltpu.SemaphoreType.DMA((PLANES // GROUP, 4)),
            pltpu.SemaphoreType.DMA((PLANES // GROUP,)),
        ],
        in_hbm=True,
        out_hbm=True,
        mib=60,
    )
    chunks, rp, rq = lax.optimization_barrier(
        (
            chunks,
            reversal(lax.axis_index(("zh", "x", "c")), 4),
            reversal(lax.axis_index(("zl", "y")), 5),
        )
    )
    tables = local_tables(rp, rq)
    chunks = lax.all_to_all(chunks.reshape(N_CHIP, 1, ROWS * LX), CHIPS, 0, 0, tiled=True)
    chunks, tables = lax.optimization_barrier((chunks, tables))
    chunks = chunks.reshape(ROWS * N_CHIP, LX)
    other = lax.ppermute(chunks, "c", [(0, 1), (1, 0)])
    high, low = device_tables()
    modes = call(
        device_kernel,
        shape(4 * N_ALL, LX),
        chunks,
        other,
        jnp.asarray(high),
        jnp.asarray(low),
        scratch=[pltpu.VMEM((N_ALL, 2 * LX), F32)],
    )
    back = lax.all_to_all(modes.reshape(N_ALL, 4, LX), EVERYWHERE, 0, 0, tiled=True)
    result = call(
        local_kernel,
        shape(2, PLANES, LY, LX),
        back.reshape(4 * N_ALL, LX),
        *tables,
        scratch=[
            pltpu.VMEM((2, PLANES, LY, LX), F32),
            pltpu.SemaphoreType.DMA((PLANES // GROUP, 2)),
        ],
        out_hbm=True,
    )
    return result.reshape(2, PLANES, 1, LY, 1, LX)


def solution(mesh):
    fine = Mesh(mesh.devices.reshape(2, 4, 2, 8, 4), EVERYWHERE)
    spec = P(None, ("zl", "y"), ("zh", "x", "c"))
    return jax.shard_map(
        body,
        mesh=fine,
        in_specs=(spec, spec, spec, spec),
        out_specs=P(None, None, ("zl", "y"), None, ("zh", "x", "c"), None),
        check_vma=False,
    )
```

```python
import math

import jax
import jax.numpy as jnp
import ml_dtypes
import numpy as np
from jax import lax
from jax.experimental import pallas as pl
from jax.experimental.pallas import tpu as pltpu
from jax.sharding import Mesh
from jax.sharding import PartitionSpec as P

NX = 2048
NY = 2048
PLANES = 16
LY = 64
LX = 128
N_GX = 16
N_GY = 32
N_ALL = N_GX * N_GY
N_CHIP = N_ALL // 2
F32 = jnp.float32
BF16 = jnp.bfloat16

CHIPS = ("zh", "x", "zl", "y")
EVERYWHERE = ("zh", "x", "c", "zl", "y")

QUAD = 7.0 / 16.0 - 7.0 / 9.0
LIN = 7.0 / 9.0 - QUAD

BLOCKS = 16
BLOCK = LX // BLOCKS
WIDE = 16
HALF = LY // 2
TEAMS = PLANES
ROWS = 5
GROUP = 4
QUARTER = LX // 4


def reversal(index, digits):
    total = 0
    for place in range(digits):
        total = total * 2 + ((index >> place) & 1)
    return total


def split(value):
    high = value.astype(BF16)
    return high, (value - high.astype(F32)).astype(BF16)


def dot3(left, right):
    left_high, left_low = left
    right_high, right_low = right
    return (
        jnp.dot(left_high, right_high, preferred_element_type=F32)
        + jnp.dot(left_high, right_low, preferred_element_type=F32)
        + jnp.dot(left_low, right_high, preferred_element_type=F32)
    )


def weighted(count, difference):
    return count * (LIN + QUAD * count) * difference


def flux(liquid_a, liquid_b, field_a, field_b):
    return weighted(liquid_a + liquid_b, field_b - field_a)


def roll(value, by, axis):
    if isinstance(by, int):
        by = by % value.shape[axis]
        return pltpu.roll(value, by, axis) if by else value
    return pltpu.roll(value, by & (value.shape[axis] - 1), axis)


def lanes_of(rows):
    return lax.broadcasted_iota(jnp.int32, (rows, LX), 1)


def rows_of(rows):
    return lax.broadcasted_iota(jnp.int32, (rows, LX), 0)


def within(lane, start, count):
    return ((lane - start) & (LX - 1)) < count


def turn(value, block, sign, offset):
    value = roll(value, -offset, 0)
    for bit in (1, 2, 4, 8):
        value = jnp.where((block & bit) != 0, roll(value, -sign * bit, 0), value)
    return value


def cell_block():
    return ((lanes_of(BLOCKS) + BLOCK // 2) // BLOCK) & (BLOCKS - 1)


def stencil_kernel(
    now_hbm,
    prev_hbm,
    phase_hbm,
    div_hbm,
    out_hbm,
    now_ref,
    prev_ref,
    phase_ref,
    div_ref,
    out,
    sems,
    out_sems,
):
    copies, sent = [], []
    for g in range(PLANES // GROUP):
        first = GROUP * g + 2 if g else 0
        planes = pl.ds(first, GROUP * (g + 1) + 2 - first)
        inner = pl.ds(GROUP * g, GROUP)
        copies.append(
            [
                pltpu.make_async_copy(source.at[part], target.at[part], sems.at[g, a])
                for a, (source, target, part) in enumerate(
                    (
                        (now_hbm, now_ref, planes),
                        (prev_hbm, prev_ref, planes),
                        (phase_hbm, phase_ref, planes),
                        (div_hbm, div_ref, inner),
                    )
                )
            ]
        )
        for copy in copies[-1]:
            copy.start()

    lane = lanes_of(LY)
    row = rows_of(LY)
    sub = rows_of(8)
    block = cell_block()
    lane_in = lanes_of(TEAMS)
    owner = rows_of(TEAMS) * BLOCK
    moved = rows_of(TEAMS) % 4 == 0
    edge_lane = (lane == 0) | (lane == LX - 1)
    y_lanes = [within(lane_in, QUARTER * f + owner, BLOCK) for f in range(4)]

    def plane(k):
        return 2.0 * now_ref[k] - prev_ref[k], phase_ref[k].astype(F32)

    for k in range(PLANES):
        if k % GROUP == 0:
            for copy in copies[k // GROUP]:
                copy.wait()
        if k == 0:
            field_before, liquid_before = plane(0)
            field, liquid = plane(1)
            flux_z = flux(liquid_before, liquid, field_before, field)
        field_after, liquid_after = plane(k + 2)
        flux_z_upper = flux(liquid, liquid_after, field, field_after)
        total = div_ref[k] + (flux_z_upper - flux_z)
        upper = flux(liquid, roll(liquid, -1, 1), field, roll(field, -1, 1))
        upper = jnp.where(lane == LX - 1, 0.0, upper)
        total = total + (upper - roll(upper, 1, 1))
        upper = flux(liquid, roll(liquid, -1, 0), field, roll(field, -1, 0))
        upper = jnp.where(row == LY - 1, 0.0, upper)
        total = total + (upper - roll(upper, 1, 0))
        ends = jnp.where(edge_lane, field, 0.0) + roll(
            jnp.where(edge_lane, liquid, 0.0), QUARTER, 1
        )
        faces = roll(ends[:BLOCKS], 1, 1)
        faces = faces + roll(roll(ends[LY - BLOCKS :], 1, 0), 3, 1)
        faces = faces + roll(ends[BLOCKS:HALF], 5, 1)
        faces = faces + roll(ends[HALF : HALF + WIDE], 7, 1)
        faces = jnp.where(moved, roll(faces, BLOCK, 1), faces)
        lines = jnp.broadcast_to(liquid[LY - 1 : LY], (8, LX))
        for f, line in ((2, field[LY - 1 : LY]), (1, liquid[0:1]), (0, field[0:1])):
            lines = jnp.where(sub <= f, jnp.broadcast_to(line, (8, LX)), lines)
        lines = roll(lines, BLOCK // 2, 1)
        for bit in (1, 2):
            lines = jnp.where((sub & bit) != 0, roll(lines, QUARTER * bit, 1), lines)
        for f in range(4):
            faces = jnp.where(y_lanes[f], jnp.broadcast_to(lines[f : f + 1], (TEAMS, LX)), faces)

        start = k * TEAMS * ROWS
        for r, value in enumerate(
            (
                turn(total[:BLOCKS], block, -1, 0),
                turn(total[LY - BLOCKS :], block, -1, 15),
                total[BLOCKS:HALF],
                total[HALF : HALF + WIDE],
                faces,
            )
        ):
            out[pl.ds(start + r, TEAMS, stride=ROWS), :] = value
        field, liquid, flux_z = field_after, liquid_after, flux_z_upper
        if k % GROUP == GROUP - 1:
            g = k // GROUP
            rows = pl.ds(g * GROUP * TEAMS * ROWS, GROUP * TEAMS * ROWS)
            sent.append(pltpu.make_async_copy(out.at[rows], out_hbm.at[rows], out_sems.at[g]))
            sent[-1].start()
    for copy in sent:
        copy.wait()


def device_kernel(own_ref, other_ref, high_ref, low_ref, out, cells):
    lane = lanes_of(N_GY)
    core = lax.axis_index("c")
    team = (lax.axis_index("zl") * 4 + lax.axis_index("y")) % TEAMS * BLOCK
    own_y = (lane < BLOCK) & (core == 0)
    at_last, at_first = lane == LX - 1, lane == 0
    groups = N_GX // 2

    def rows(c, g, r):
        place = pl.ds((g % groups) * N_GY * ROWS + r, N_GY, stride=ROWS)
        return jnp.where(core == c, own_ref[place, :], other_ref[place, :])

    def x_aligned(value):
        return roll(value, 2 * LX - 1 - 4 * core - BLOCK * (team % (4 * BLOCK) == 0), 1)

    def x_parts(here, there):
        lower = roll(there, -1, 1)
        value = weighted(roll(here + lower, -QUARTER, 1), lower - here)
        return [(value, roll(value, 1, 1)), (roll(value, -2, 1), roll(value, -1, 1))]

    def y_part(here):
        here = roll(here, LX - team, 1)
        lower = roll(here, -1, 0)
        upper = roll(here, -2 * QUARTER, 1)
        value = weighted(roll(upper + lower, -QUARTER, 1), lower - upper)
        return roll(jnp.where(own_y, value, 0.0), team + (LX - BLOCK // 2), 1)

    raw = [rows(c, 0, 4) for c in range(2)]
    faces = [x_aligned(value) for value in raw]
    entering = x_parts(x_aligned(rows(1, groups - 1, 4)), faces[0])
    for g in range(groups):
        next_raw = [rows(c, g + 1, 4) for c in range(2)]
        after = [x_aligned(value) for value in next_raw]
        for c in range(2):
            leaving = x_parts(faces[c], after[0] if c else faces[1])
            along_y = y_part(raw[c])
            part = [
                rows(c, g, 2 * core + t)
                + jnp.where(at_last, leaving[t][0], 0.0)
                - jnp.where(at_first, entering[t][1], 0.0)
                for t in range(2)
            ]
            place = pl.ds(c * N_CHIP + g * N_GY, N_GY)
            cells[place, :LX] = part[0] - roll(along_y, 1, 0)
            cells[place, LX:] = part[1] + along_y
            entering = leaving
        raw, faces = next_raw, after

    right_high, right_low = split(cells[...])
    result = dot3((high_ref[...], low_ref[...]), (right_high, right_low))
    for part in range(2):
        rows = slice(part * N_ALL, (part + 1) * N_ALL)
        out[pl.ds(2 * part, N_ALL, stride=4), :] = result[rows, :LX]
        out[pl.ds(2 * part + 1, N_ALL, stride=4), :] = result[rows, LX:]


def local_kernel(x_ref, y_matrix_ref, cos_ref, sin_ref, out_hbm, out, sems):
    y_matrix = split(y_matrix_ref[...])
    x_matrix = split(
        jnp.concatenate(
            [
                jnp.concatenate([cos_ref[...], -sin_ref[...]], axis=1),
                jnp.concatenate([sin_ref[...], cos_ref[...]], axis=1),
            ],
            axis=0,
        )
    )
    block = cell_block()
    copies = []
    for g in range(PLANES // GROUP):
        group = []
        for k in range(GROUP * g, GROUP * (g + 1)):
            start = (k // 2) * 4 * LY + (k % 2) * LY
            lines = [
                turn(x_ref[pl.ds(start + kind, BLOCKS, stride=4), :], block, 1, kind & 1)
                for kind in range(4)
            ]
            lines.append(x_ref[pl.ds(start + 2 * LY, LY), :])
            group.append(jnp.concatenate(lines, axis=0))
        lines = dot3(y_matrix, split(jnp.concatenate(group, axis=1)))
        lines = jnp.concatenate(
            [
                jnp.concatenate(
                    [lines[:LY, k * LX : (k + 1) * LX], lines[LY:, k * LX : (k + 1) * LX]], axis=1
                )
                for k in range(GROUP)
            ],
            axis=0,
        )
        modes = dot3(split(lines), x_matrix)
        for part in range(2):
            for k in range(GROUP):
                out[part, GROUP * g + k] = modes[k * LY : (k + 1) * LY, part * LX : (part + 1) * LX]
            planes = (part, pl.ds(g * GROUP, GROUP))
            copies.append(
                pltpu.make_async_copy(out.at[planes], out_hbm.at[planes], sems.at[g, part])
            )
            copies[-1].start()
    for copy in copies:
        copy.wait()


def device_tables():
    dest = np.arange(N_ALL)
    rev_p = np.array([reversal(i, 4) for i in range(N_GX)])
    rev_q = np.array([reversal(i, 5) for i in range(N_GY)])
    kx = rev_p[dest // N_GY][:, None]
    ky = rev_q[dest % N_GY][:, None]
    source = np.arange(N_ALL)
    gx = (2 * (source % N_CHIP // N_GY) + source // N_CHIP)[None]
    gy = (source % N_GY)[None]
    angle = (2 * kx * gx + ky * gy) % N_GY * (2.0 * math.pi / N_GY)
    table = np.concatenate([np.cos(angle), -np.sin(angle)])
    high = table.astype(ml_dtypes.bfloat16)
    return high, (table - high.astype(np.float64)).astype(ml_dtypes.bfloat16)


def cos_sin(place, mode, length):
    angle = ((place * mode) % length).astype(F32) * (2.0 * math.pi / length)
    return jnp.cos(angle), jnp.sin(angle)


def local_tables(rp, rq):
    line = lax.broadcasted_iota(jnp.int32, (2 * LY, 2 * LY), 0)
    col = lax.broadcasted_iota(jnp.int32, (2 * LY, 2 * LY), 1)
    rest = col - 4 * BLOCKS
    in_block = rest < 0
    part_in = jnp.where(in_block, col // (2 * BLOCKS), rest >> 1) & 1
    place = jnp.where(
        in_block,
        col % BLOCKS + (LY - BLOCKS) * (col // BLOCKS & 1),
        BLOCKS + (rest >> 2) + WIDE * (rest & 1),
    )
    cosine, sine = cos_sin(place, 32 * (line % LY) + rq, NY)
    part_out = line // LY
    sign = jnp.where(part_out < part_in, 1.0, -1.0)
    y_matrix = jnp.where(part_out == part_in, cosine, sign * sine) * (1.0 / math.sqrt(NX * NY))
    line = lax.broadcasted_iota(jnp.int32, (LX, LX), 0)
    col = lax.broadcasted_iota(jnp.int32, (LX, LX), 1)
    return (y_matrix, *cos_sin(line, 16 * col + rp, NX))


def call(kernel, outs, *args, scratch=(), in_hbm=False, out_hbm=False, mib=40):
    def spec(hbm):
        return pl.BlockSpec(memory_space=pltpu.HBM if hbm else pltpu.VMEM)

    return pl.pallas_call(
        kernel,
        out_shape=outs,
        in_specs=[spec(in_hbm)] * len(args),
        out_specs=spec(out_hbm),
        scratch_shapes=scratch,
        compiler_params=pltpu.CompilerParams(vmem_limit_bytes=mib * 1024 * 1024),
    )(*args)


def shape(*dims):
    return jax.ShapeDtypeStruct(dims, F32)


def body(p_now, p_prev, phase, div_star):
    padded = (PLANES + 2, LY, LX)
    chunks = call(
        stencil_kernel,
        shape(ROWS * N_CHIP, LX),
        p_now,
        p_prev,
        phase,
        div_star,
        scratch=[
            pltpu.VMEM(padded, F32),
            pltpu.VMEM(padded, F32),
            pltpu.VMEM(padded, jnp.int32),
            pltpu.VMEM((PLANES, LY, LX), F32),
            pltpu.VMEM((ROWS * N_CHIP, LX), F32),
            pltpu.SemaphoreType.DMA((PLANES // GROUP, 4)),
            pltpu.SemaphoreType.DMA((PLANES // GROUP,)),
        ],
        in_hbm=True,
        out_hbm=True,
        mib=60,
    )
    chunks, rp, rq = lax.optimization_barrier(
        (
            chunks,
            reversal(lax.axis_index(("zh", "x", "c")), 4),
            reversal(lax.axis_index(("zl", "y")), 5),
        )
    )
    tables = local_tables(rp, rq)
    chunks = lax.all_to_all(chunks.reshape(N_CHIP, 1, ROWS * LX), CHIPS, 0, 0, tiled=True)
    chunks, tables = lax.optimization_barrier((chunks, tables))
    chunks = chunks.reshape(ROWS * N_CHIP, LX)
    other = lax.ppermute(chunks, "c", [(0, 1), (1, 0)])
    high, low = device_tables()
    modes = call(
        device_kernel,
        shape(4 * N_ALL, LX),
        chunks,
        other,
        jnp.asarray(high),
        jnp.asarray(low),
        scratch=[pltpu.VMEM((N_ALL, 2 * LX), F32)],
    )
    back = lax.all_to_all(modes.reshape(N_ALL, 4, LX), EVERYWHERE, 0, 0, tiled=True)
    result = call(
        local_kernel,
        shape(2, PLANES, LY, LX),
        back.reshape(4 * N_ALL, LX),
        *tables,
        scratch=[
            pltpu.VMEM((2, PLANES, LY, LX), F32),
            pltpu.SemaphoreType.DMA((PLANES // GROUP, 2)),
        ],
        out_hbm=True,
    )
    return result.reshape(2, PLANES, 1, LY, 1, LX)


def solution(mesh):
    fine = Mesh(mesh.devices.reshape(2, 4, 2, 8, 4), EVERYWHERE)
    spec = P(None, ("zl", "y"), ("zh", "x", "c"))
    return jax.shard_map(
        body,
        mesh=fine,
        in_specs=(spec, spec, spec, spec),
        out_specs=P(None, None, ("zl", "y"), None, ("zh", "x", "c"), None),
        check_vma=False,
    )
```

```python
import math

import jax
import jax.numpy as jnp
import ml_dtypes
import numpy as np
from jax import lax
from jax.experimental import pallas as pl
from jax.experimental.pallas import tpu as pltpu
from jax.sharding import Mesh
from jax.sharding import PartitionSpec as P

NX = 2048
NY = 2048
PLANES = 16
LY = 64
LX = 128
N_GX = 16
N_GY = 32
N_ALL = N_GX * N_GY
N_CHIP = N_ALL // 2
F32 = jnp.float32
BF16 = jnp.bfloat16

CHIPS = ("zh", "x", "zl", "y")
EVERYWHERE = ("zh", "x", "c", "zl", "y")

LIQUID = 7.0 / 8.0
MIXED = 7.0 / 9.0
QUAD = -4.0 / 9.0
LIN = 11.5 / 9.0

BLOCKS = 16
BLOCK = LX // BLOCKS
WIDE = 16
HALF = LY // 2
TEAMS = PLANES
ROWS = 5
GROUP = 4
PAIR = 2
QUARTER = LX // 4


def reversal(index, digits):
    total = 0
    for place in range(digits):
        total = total * 2 + ((index >> place) & 1)
    return total


def split(value):
    high = value.astype(BF16)
    return high, (value - high.astype(F32)).astype(BF16)


def dot3(left, right):
    left_high, left_low = left
    right_high, right_low = right
    return (
        jnp.dot(left_high, right_high, preferred_element_type=F32)
        + jnp.dot(left_high, right_low, preferred_element_type=F32)
        + jnp.dot(left_low, right_high, preferred_element_type=F32)
    )


def weighted(count, difference):
    return count * (LIN + QUAD * count) * difference


def flux(liquid_a, liquid_b, field_a, field_b):
    return jnp.where(liquid_a == liquid_b, liquid_a, MIXED) * (field_b - field_a)


def roll(value, by, axis):
    if isinstance(by, int):
        by = by % value.shape[axis]
        return pltpu.roll(value, by, axis) if by else value
    return pltpu.roll(value, by & (value.shape[axis] - 1), axis)


def lanes_of(rows):
    return lax.broadcasted_iota(jnp.int32, (rows, LX), 1)


def rows_of(rows):
    return lax.broadcasted_iota(jnp.int32, (rows, LX), 0)


def within(lane, start, count):
    return ((lane - start) & (LX - 1)) < count


def turn(value, block, sign, offset):
    value = roll(value, -offset, 0)
    for bit in (1, 2, 4, 8):
        value = jnp.where((block & bit) != 0, roll(value, -sign * bit, 0), value)
    return value


def cell_block():
    return ((lanes_of(BLOCKS) + BLOCK // 2) // BLOCK) & (BLOCKS - 1)


def stencil_kernel(
    now_hbm,
    prev_hbm,
    phase_hbm,
    div_hbm,
    out_hbm,
    now_ref,
    prev_ref,
    phase_ref,
    div_ref,
    out,
    sems,
    out_sems,
):
    copies, sent = [], []
    for g in range(PLANES // GROUP):
        first = GROUP * g + 2 if g else 0
        planes = pl.ds(first, GROUP * (g + 1) + 2 - first)
        inner = pl.ds(GROUP * g, GROUP)
        copies.append(
            [
                pltpu.make_async_copy(source.at[part], target.at[part], sems.at[g, a])
                for a, (source, target, part) in enumerate(
                    (
                        (now_hbm, now_ref, planes),
                        (prev_hbm, prev_ref, planes),
                        (phase_hbm, phase_ref, planes),
                        (div_hbm, div_ref, inner),
                    )
                )
            ]
        )
        for copy in copies[-1]:
            copy.start()

    lane = lanes_of(LY)
    row = rows_of(LY)
    sub = rows_of(8)
    block = cell_block()
    lane_in = lanes_of(TEAMS)
    owner = rows_of(TEAMS) * BLOCK
    moved = rows_of(TEAMS) % 4 == 0
    edge_lane = (lane == 0) | (lane == LX - 1)
    y_lanes = [within(lane_in, QUARTER * f + owner, BLOCK) for f in range(4)]

    def plane(k):
        return 2.0 * now_ref[k] - prev_ref[k], jnp.where(phase_ref[k] == 1, LIQUID, 0.0)

    for k in range(PLANES):
        if k % GROUP == 0:
            for copy in copies[k // GROUP]:
                copy.wait()
        if k == 0:
            field_before, liquid_before = plane(0)
            field, liquid = plane(1)
            flux_z = flux(liquid_before, liquid, field_before, field)
        field_after, liquid_after = plane(k + 2)
        flux_z_upper = flux(liquid, liquid_after, field, field_after)
        total = div_ref[k] + (flux_z_upper - flux_z)
        upper = flux(liquid, roll(liquid, -1, 1), field, roll(field, -1, 1))
        upper = jnp.where(lane == LX - 1, 0.0, upper)
        total = total + (upper - roll(upper, 1, 1))
        upper = flux(liquid, roll(liquid, -1, 0), field, roll(field, -1, 0))
        upper = jnp.where(row == LY - 1, 0.0, upper)
        total = total + (upper - roll(upper, 1, 0))
        ends = jnp.where(edge_lane, field, 0.0) + roll(
            jnp.where(edge_lane, liquid, 0.0), QUARTER, 1
        )
        faces = roll(ends[:BLOCKS], 1, 1)
        faces = faces + roll(roll(ends[LY - BLOCKS :], 1, 0), 3, 1)
        faces = faces + roll(ends[BLOCKS:HALF], 5, 1)
        faces = faces + roll(ends[HALF : HALF + WIDE], 7, 1)
        faces = jnp.where(moved, roll(faces, BLOCK, 1), faces)
        lines = jnp.broadcast_to(liquid[LY - 1 : LY], (8, LX))
        for f, line in ((2, field[LY - 1 : LY]), (1, liquid[0:1]), (0, field[0:1])):
            lines = jnp.where(sub <= f, jnp.broadcast_to(line, (8, LX)), lines)
        lines = roll(lines, BLOCK // 2, 1)
        for bit in (1, 2):
            lines = jnp.where((sub & bit) != 0, roll(lines, QUARTER * bit, 1), lines)
        for f in range(4):
            faces = jnp.where(y_lanes[f], jnp.broadcast_to(lines[f : f + 1], (TEAMS, LX)), faces)

        start = k * TEAMS * ROWS
        for r, value in enumerate(
            (
                turn(total[:BLOCKS], block, -1, 0),
                turn(total[LY - BLOCKS :], block, -1, 15),
                total[BLOCKS:HALF],
                total[HALF : HALF + WIDE],
                faces,
            )
        ):
            out[pl.ds(start + r, TEAMS, stride=ROWS), :] = value
        field, liquid, flux_z = field_after, liquid_after, flux_z_upper
        if k % GROUP == GROUP - 1:
            g = k // GROUP
            rows = pl.ds(g * GROUP * TEAMS * ROWS, GROUP * TEAMS * ROWS)
            sent.append(pltpu.make_async_copy(out.at[rows], out_hbm.at[rows], out_sems.at[g]))
            sent[-1].start()
    for copy in sent:
        copy.wait()


def device_kernel(own_ref, other_ref, high_ref, low_ref, out, cells):
    lane = lanes_of(N_GY)
    core = lax.axis_index("c")
    team = (lax.axis_index("zl") * 4 + lax.axis_index("y")) % TEAMS * BLOCK
    own_y = (lane < BLOCK) & (core == 0)
    at_last, at_first = lane == LX - 1, lane == 0
    groups = N_GX // 2

    def row(ref, g, r):
        return ref[pl.ds((g % groups) * N_GY * ROWS + r, N_GY, stride=ROWS), :]

    def mine(c, g, t):
        refs = (own_ref, other_ref) if c == 0 else (other_ref, own_ref)
        return jnp.where(core == 0, row(refs[0], g, t), row(refs[1], g, 2 + t))

    def face_row(c, g):
        refs = (own_ref, other_ref) if c == 0 else (other_ref, own_ref)
        return jnp.where(core == 0, row(refs[0], g, 4), row(refs[1], g, 4))

    def x_aligned(value):
        return roll(value, 2 * LX - 1 - 4 * core - BLOCK * (team % (4 * BLOCK) == 0), 1)

    def x_parts(here, there):
        lower = roll(there, -1, 1)
        value = weighted(roll(here + lower, -QUARTER, 1), lower - here)
        return [(value, roll(value, 1, 1)), (roll(value, -2, 1), roll(value, -1, 1))]

    def y_part(here):
        here = roll(here, LX - team, 1)
        lower = roll(here, -1, 0)
        upper = roll(here, -2 * QUARTER, 1)
        value = weighted(roll(upper + lower, -QUARTER, 1), lower - upper)
        return roll(jnp.where(own_y, value, 0.0), team + (LX - BLOCK // 2), 1)

    raw = [face_row(c, 0) for c in range(2)]
    faces = [x_aligned(value) for value in raw]
    entering = x_parts(x_aligned(face_row(1, groups - 1)), faces[0])
    for g in range(groups):
        next_raw = [face_row(c, g + 1) for c in range(2)]
        after = [x_aligned(value) for value in next_raw]
        for c in range(2):
            leaving = x_parts(faces[c], after[0] if c else faces[1])
            along_y = y_part(raw[c])
            part = [
                mine(c, g, t)
                + jnp.where(at_last, leaving[t][0], 0.0)
                - jnp.where(at_first, entering[t][1], 0.0)
                for t in range(2)
            ]
            place = pl.ds(c * N_CHIP + g * N_GY, N_GY)
            cells[place, :LX] = part[0] - roll(along_y, 1, 0)
            cells[place, LX:] = part[1] + along_y
            entering = leaving
        raw, faces = next_raw, after

    right_high, right_low = split(cells[...])
    result = dot3((high_ref[...], low_ref[...]), (right_high, right_low))
    for part in range(2):
        rows = slice(part * N_ALL, (part + 1) * N_ALL)
        out[pl.ds(2 * part, N_ALL, stride=4), :] = result[rows, :LX]
        out[pl.ds(2 * part + 1, N_ALL, stride=4), :] = result[rows, LX:]


def local_kernel(x_ref, y_matrix_ref, cos_ref, sin_ref, out_hbm, out, sems):
    y_matrix = split(y_matrix_ref[...])
    x_matrix = split(
        jnp.concatenate(
            [
                jnp.concatenate([cos_ref[...], -sin_ref[...]], axis=1),
                jnp.concatenate([sin_ref[...], cos_ref[...]], axis=1),
            ],
            axis=0,
        )
    )
    block = cell_block()
    copies = []
    for g in range(PLANES // PAIR):
        group = []
        for k in range(PAIR * g, PAIR * (g + 1)):
            start = (k // 2) * 4 * LY + (k % 2) * LY
            lines = [
                turn(x_ref[pl.ds(start + kind, BLOCKS, stride=4), :], block, 1, kind & 1)
                for kind in range(4)
            ]
            lines.append(x_ref[pl.ds(start + 2 * LY, LY), :])
            group.append(jnp.concatenate(lines, axis=0))
        lines = dot3(y_matrix, split(jnp.concatenate(group, axis=1)))
        lines = jnp.concatenate(
            [
                jnp.concatenate(
                    [lines[:LY, k * LX : (k + 1) * LX], lines[LY:, k * LX : (k + 1) * LX]], axis=1
                )
                for k in range(PAIR)
            ],
            axis=0,
        )
        modes = dot3(split(lines), x_matrix)
        for part in range(2):
            for k in range(PAIR):
                out[part, PAIR * g + k] = modes[k * LY : (k + 1) * LY, part * LX : (part + 1) * LX]
            planes = (part, pl.ds(g * PAIR, PAIR))
            copies.append(
                pltpu.make_async_copy(out.at[planes], out_hbm.at[planes], sems.at[g, part])
            )
            copies[-1].start()
    for copy in copies:
        copy.wait()


def device_tables():
    dest = np.arange(N_ALL)
    rev_p = np.array([reversal(i, 4) for i in range(N_GX)])
    rev_q = np.array([reversal(i, 5) for i in range(N_GY)])
    kx = rev_p[dest // N_GY][:, None]
    ky = rev_q[dest % N_GY][:, None]
    source = np.arange(N_ALL)
    gx = (2 * (source % N_CHIP // N_GY) + source // N_CHIP)[None]
    gy = (source % N_GY)[None]
    angle = (2 * kx * gx + ky * gy) % N_GY * (2.0 * math.pi / N_GY)
    table = np.concatenate([np.cos(angle), -np.sin(angle)])
    high = table.astype(ml_dtypes.bfloat16)
    return high, (table - high.astype(np.float64)).astype(ml_dtypes.bfloat16)


def cos_sin(place, mode, length):
    angle = ((place * mode) % length).astype(F32) * (2.0 * math.pi / length)
    return jnp.cos(angle), jnp.sin(angle)


def local_tables(rp, rq):
    line = lax.broadcasted_iota(jnp.int32, (2 * LY, 2 * LY), 0)
    col = lax.broadcasted_iota(jnp.int32, (2 * LY, 2 * LY), 1)
    rest = col - 4 * BLOCKS
    in_block = rest < 0
    part_in = jnp.where(in_block, col // (2 * BLOCKS), rest >> 1) & 1
    place = jnp.where(
        in_block,
        col % BLOCKS + (LY - BLOCKS) * (col // BLOCKS & 1),
        BLOCKS + (rest >> 2) + WIDE * (rest & 1),
    )
    cosine, sine = cos_sin(place, 32 * (line % LY) + rq, NY)
    part_out = line // LY
    sign = jnp.where(part_out < part_in, 1.0, -1.0)
    y_matrix = jnp.where(part_out == part_in, cosine, sign * sine) * (1.0 / math.sqrt(NX * NY))
    line = lax.broadcasted_iota(jnp.int32, (LX, LX), 0)
    col = lax.broadcasted_iota(jnp.int32, (LX, LX), 1)
    return (y_matrix, *cos_sin(line, 16 * col + rp, NX))


def call(kernel, outs, *args, scratch=(), in_hbm=False, out_hbm=False, mib=40):
    def spec(hbm):
        return pl.BlockSpec(memory_space=pltpu.HBM if hbm else pltpu.VMEM)

    return pl.pallas_call(
        kernel,
        out_shape=outs,
        in_specs=[spec(in_hbm)] * len(args),
        out_specs=spec(out_hbm),
        scratch_shapes=scratch,
        compiler_params=pltpu.CompilerParams(vmem_limit_bytes=mib * 1024 * 1024),
    )(*args)


def shape(*dims):
    return jax.ShapeDtypeStruct(dims, F32)


def body(p_now, p_prev, phase, div_star):
    padded = (PLANES + 2, LY, LX)
    chunks = call(
        stencil_kernel,
        shape(ROWS * N_CHIP, LX),
        p_now,
        p_prev,
        phase,
        div_star,
        scratch=[
            pltpu.VMEM(padded, F32),
            pltpu.VMEM(padded, F32),
            pltpu.VMEM(padded, jnp.int32),
            pltpu.VMEM((PLANES, LY, LX), F32),
            pltpu.VMEM((ROWS * N_CHIP, LX), F32),
            pltpu.SemaphoreType.DMA((PLANES // GROUP, 4)),
            pltpu.SemaphoreType.DMA((PLANES // GROUP,)),
        ],
        in_hbm=True,
        out_hbm=True,
        mib=60,
    )
    chunks, rp, rq = lax.optimization_barrier(
        (
            chunks,
            reversal(lax.axis_index(("zh", "x", "c")), 4),
            reversal(lax.axis_index(("zl", "y")), 5),
        )
    )
    tables = local_tables(rp, rq)
    chunks = lax.all_to_all(chunks.reshape(N_CHIP, 1, ROWS * LX), CHIPS, 0, 0, tiled=True)
    chunks, tables = lax.optimization_barrier((chunks, tables))
    chunks = chunks.reshape(ROWS * N_CHIP, LX)
    other = lax.ppermute(chunks, "c", [(0, 1), (1, 0)])
    high, low = device_tables()
    modes = call(
        device_kernel,
        shape(4 * N_ALL, LX),
        chunks,
        other,
        jnp.asarray(high),
        jnp.asarray(low),
        scratch=[pltpu.VMEM((N_ALL, 2 * LX), F32)],
    )
    back = lax.all_to_all(modes.reshape(N_ALL, 4, LX), EVERYWHERE, 0, 0, tiled=True)
    result = call(
        local_kernel,
        shape(2, PLANES, LY, LX),
        back.reshape(4 * N_ALL, LX),
        *tables,
        scratch=[
            pltpu.VMEM((2, PLANES, LY, LX), F32),
            pltpu.SemaphoreType.DMA((PLANES // PAIR, 2)),
        ],
        out_hbm=True,
    )
    return result.reshape(2, PLANES, 1, LY, 1, LX)


def solution(mesh):
    fine = Mesh(mesh.devices.reshape(2, 4, 2, 8, 4), EVERYWHERE)
    spec = P(None, ("zl", "y"), ("zh", "x", "c"))
    return jax.shard_map(
        body,
        mesh=fine,
        in_specs=(spec, spec, spec, spec),
        out_specs=P(None, None, ("zl", "y"), None, ("zh", "x", "c"), None),
        check_vma=False,
    )
```

```python
import math

import jax
import jax.numpy as jnp
import ml_dtypes
import numpy as np
from jax import lax
from jax.experimental import pallas as pl
from jax.experimental.pallas import tpu as pltpu
from jax.sharding import Mesh
from jax.sharding import PartitionSpec as P

NX = 2048
NY = 2048
PLANES = 16
LY = 64
LX = 128
N_GX = 16
N_GY = 32
N_ALL = N_GX * N_GY
N_CHIP = N_ALL // 2
F32 = jnp.float32
BF16 = jnp.bfloat16

CHIPS = ("zh", "x", "zl", "y")
EVERYWHERE = ("zh", "x", "c", "zl", "y")

LIQUID = 7.0 / 8.0
MIXED = 7.0 / 9.0
QUAD = -4.0 / 9.0
LIN = 11.5 / 9.0

BLOCKS = 16
BLOCK = LX // BLOCKS
WIDE = 16
HALF = LY // 2
TEAMS = PLANES
ROWS = 5
GROUP = 4
PAIR = 2
QUARTER = LX // 4


def reversal(index, digits):
    total = 0
    for place in range(digits):
        total = total * 2 + ((index >> place) & 1)
    return total


def split(value):
    high = value.astype(BF16)
    return high, (value - high.astype(F32)).astype(BF16)


def dot3(left, right):
    left_high, left_low = left
    right_high, right_low = right
    return (
        jnp.dot(left_high, right_high, preferred_element_type=F32)
        + jnp.dot(left_high, right_low, preferred_element_type=F32)
        + jnp.dot(left_low, right_high, preferred_element_type=F32)
    )


def weighted(count, difference):
    return count * (LIN + QUAD * count) * difference


def flux(liquid_a, liquid_b, field_a, field_b):
    return jnp.where(liquid_a == liquid_b, liquid_a, MIXED) * (field_b - field_a)


def roll(value, by, axis):
    if isinstance(by, int):
        by = by % value.shape[axis]
        return pltpu.roll(value, by, axis) if by else value
    return pltpu.roll(value, by & (value.shape[axis] - 1), axis)


def lanes_of(rows):
    return lax.broadcasted_iota(jnp.int32, (rows, LX), 1)


def rows_of(rows):
    return lax.broadcasted_iota(jnp.int32, (rows, LX), 0)


def within(lane, start, count):
    return ((lane - start) & (LX - 1)) < count


def turn(value, block, sign, offset):
    value = roll(value, -offset, 0)
    for bit in (1, 2, 4, 8):
        value = jnp.where((block & bit) != 0, roll(value, -sign * bit, 0), value)
    return value


def cell_block():
    return ((lanes_of(BLOCKS) + BLOCK // 2) // BLOCK) & (BLOCKS - 1)


def stencil_kernel(
    now_hbm,
    prev_hbm,
    phase_hbm,
    div_hbm,
    out_hbm,
    now_ref,
    prev_ref,
    phase_ref,
    div_ref,
    out,
    sems,
    out_sems,
):
    copies, sent = [], []
    for g in range(PLANES // GROUP):
        first = GROUP * g + 2 if g else 0
        planes = pl.ds(first, GROUP * (g + 1) + 2 - first)
        inner = pl.ds(GROUP * g, GROUP)
        copies.append(
            [
                pltpu.make_async_copy(source.at[part], target.at[part], sems.at[g, a])
                for a, (source, target, part) in enumerate(
                    (
                        (now_hbm, now_ref, planes),
                        (prev_hbm, prev_ref, planes),
                        (phase_hbm, phase_ref, planes),
                        (div_hbm, div_ref, inner),
                    )
                )
            ]
        )
        for copy in copies[-1]:
            copy.start()

    lane = lanes_of(LY)
    row = rows_of(LY)
    sub = rows_of(8)
    block = cell_block()
    lane_in = lanes_of(TEAMS)
    owner = rows_of(TEAMS) * BLOCK
    moved = rows_of(TEAMS) % 4 == 0
    edge_lane = (lane == 0) | (lane == LX - 1)
    y_lanes = [within(lane_in, QUARTER * f + owner, BLOCK) for f in range(4)]

    def plane(k):
        return 2.0 * now_ref[k] - prev_ref[k], jnp.where(phase_ref[k] == 1, LIQUID, 0.0)

    for k in range(PLANES):
        if k % GROUP == 0:
            for copy in copies[k // GROUP]:
                copy.wait()
        if k == 0:
            field_before, liquid_before = plane(0)
            field, liquid = plane(1)
            flux_z = flux(liquid_before, liquid, field_before, field)
        field_after, liquid_after = plane(k + 2)
        flux_z_upper = flux(liquid, liquid_after, field, field_after)
        total = div_ref[k] + (flux_z_upper - flux_z)
        upper = flux(liquid, roll(liquid, -1, 1), field, roll(field, -1, 1))
        upper = jnp.where(lane == LX - 1, 0.0, upper)
        total = total + (upper - roll(upper, 1, 1))
        upper = flux(liquid, roll(liquid, -1, 0), field, roll(field, -1, 0))
        upper = jnp.where(row == LY - 1, 0.0, upper)
        total = total + (upper - roll(upper, 1, 0))
        ends = jnp.where(edge_lane, field, 0.0) + roll(
            jnp.where(edge_lane, liquid, 0.0), QUARTER, 1
        )
        faces = roll(ends[:BLOCKS], 1, 1)
        faces = faces + roll(roll(ends[LY - BLOCKS :], 1, 0), 3, 1)
        faces = faces + roll(ends[BLOCKS:HALF], 5, 1)
        faces = faces + roll(ends[HALF : HALF + WIDE], 7, 1)
        faces = jnp.where(moved, roll(faces, BLOCK, 1), faces)
        lines = jnp.broadcast_to(liquid[LY - 1 : LY], (8, LX))
        for f, line in ((2, field[LY - 1 : LY]), (1, liquid[0:1]), (0, field[0:1])):
            lines = jnp.where(sub <= f, jnp.broadcast_to(line, (8, LX)), lines)
        lines = roll(lines, BLOCK // 2, 1)
        for bit in (1, 2):
            lines = jnp.where((sub & bit) != 0, roll(lines, QUARTER * bit, 1), lines)
        for f in range(4):
            faces = jnp.where(y_lanes[f], jnp.broadcast_to(lines[f : f + 1], (TEAMS, LX)), faces)

        start = k * TEAMS * ROWS
        for r, value in enumerate(
            (
                turn(total[:BLOCKS], block, -1, 0),
                turn(total[LY - BLOCKS :], block, -1, 15),
                total[BLOCKS:HALF],
                total[HALF : HALF + WIDE],
                faces,
            )
        ):
            out[pl.ds(start + r, TEAMS, stride=ROWS), :] = value
        field, liquid, flux_z = field_after, liquid_after, flux_z_upper
        if k % GROUP == GROUP - 1:
            g = k // GROUP
            rows = pl.ds(g * GROUP * TEAMS * ROWS, GROUP * TEAMS * ROWS)
            sent.append(pltpu.make_async_copy(out.at[rows], out_hbm.at[rows], out_sems.at[g]))
            sent[-1].start()
    for copy in sent:
        copy.wait()


def device_kernel(own_ref, other_ref, high_ref, low_ref, out, cells):
    lane = lanes_of(N_GY)
    core = lax.axis_index("c")
    team = (lax.axis_index("zl") * 4 + lax.axis_index("y")) % TEAMS * BLOCK
    own_y = (lane < BLOCK) & (core == 0)
    at_last, at_first = lane == LX - 1, lane == 0
    groups = N_GX // 2

    def row(ref, g, r):
        return ref[pl.ds((g % groups) * N_GY * ROWS + r, N_GY, stride=ROWS), :]

    def mine(c, g, t):
        refs = (own_ref, other_ref) if c == 0 else (other_ref, own_ref)
        return jnp.where(core == 0, row(refs[0], g, t), row(refs[1], g, 2 + t))

    def face_row(c, g):
        refs = (own_ref, other_ref) if c == 0 else (other_ref, own_ref)
        return jnp.where(core == 0, row(refs[0], g, 4), row(refs[1], g, 4))

    def x_aligned(value):
        return roll(value, 2 * LX - 1 - 4 * core - BLOCK * (team % (4 * BLOCK) == 0), 1)

    def x_parts(here, there):
        lower = roll(there, -1, 1)
        value = weighted(roll(here + lower, -QUARTER, 1), lower - here)
        return [(value, roll(value, 1, 1)), (roll(value, -2, 1), roll(value, -1, 1))]

    def y_part(here):
        here = roll(here, LX - team, 1)
        lower = roll(here, -1, 0)
        upper = roll(here, -2 * QUARTER, 1)
        value = weighted(roll(upper + lower, -QUARTER, 1), lower - upper)
        return roll(jnp.where(own_y, value, 0.0), team + (LX - BLOCK // 2), 1)

    raw = [face_row(c, 0) for c in range(2)]
    faces = [x_aligned(value) for value in raw]
    entering = x_parts(x_aligned(face_row(1, groups - 1)), faces[0])
    for g in range(groups):
        next_raw = [face_row(c, g + 1) for c in range(2)]
        after = [x_aligned(value) for value in next_raw]
        for c in range(2):
            leaving = x_parts(faces[c], after[0] if c else faces[1])
            along_y = y_part(raw[c])
            part = [
                mine(c, g, t)
                + jnp.where(at_last, leaving[t][0], 0.0)
                - jnp.where(at_first, entering[t][1], 0.0)
                for t in range(2)
            ]
            place = pl.ds(c * N_CHIP + g * N_GY, N_GY)
            cells[place, :LX] = part[0] - roll(along_y, 1, 0)
            cells[place, LX:] = part[1] + along_y
            entering = leaving
        raw, faces = next_raw, after

    right_high, right_low = split(cells[...])
    result = dot3((high_ref[...], low_ref[...]), (right_high, right_low))
    for part in range(2):
        rows = slice(part * N_ALL, (part + 1) * N_ALL)
        out[pl.ds(2 * part, N_ALL, stride=4), :] = result[rows, :LX]
        out[pl.ds(2 * part + 1, N_ALL, stride=4), :] = result[rows, LX:]


def local_kernel(x_ref, y_matrix_ref, cos_ref, sin_ref, out_hbm, out, sems):
    y_matrix = split(y_matrix_ref[...])
    x_matrix = split(
        jnp.concatenate(
            [
                jnp.concatenate([cos_ref[...], -sin_ref[...]], axis=1),
                jnp.concatenate([sin_ref[...], cos_ref[...]], axis=1),
            ],
            axis=0,
        )
    )
    block = cell_block()
    copies = []
    for g in range(PLANES // PAIR):
        group = []
        for k in range(PAIR * g, PAIR * (g + 1)):
            start = (k // 2) * 4 * LY + (k % 2) * LY
            lines = [
                turn(x_ref[pl.ds(start + kind, BLOCKS, stride=4), :], block, 1, kind & 1)
                for kind in range(4)
            ]
            lines.append(x_ref[pl.ds(start + 2 * LY, LY), :])
            group.append(jnp.concatenate(lines, axis=0))
        lines = dot3(y_matrix, split(jnp.concatenate(group, axis=1)))
        lines = jnp.concatenate(
            [
                jnp.concatenate(
                    [lines[:LY, k * LX : (k + 1) * LX], lines[LY:, k * LX : (k + 1) * LX]], axis=1
                )
                for k in range(PAIR)
            ],
            axis=0,
        )
        modes = dot3(split(lines), x_matrix)
        for part in range(2):
            for k in range(PAIR):
                out[part, PAIR * g + k] = modes[k * LY : (k + 1) * LY, part * LX : (part + 1) * LX]
            planes = (part, pl.ds(g * PAIR, PAIR))
            copies.append(
                pltpu.make_async_copy(out.at[planes], out_hbm.at[planes], sems.at[g, part])
            )
            copies[-1].start()
    for copy in copies:
        copy.wait()


def device_tables():
    dest = np.arange(N_ALL)
    rev_p = np.array([reversal(i, 4) for i in range(N_GX)])
    rev_q = np.array([reversal(i, 5) for i in range(N_GY)])
    kx = rev_p[dest // N_GY][:, None]
    ky = rev_q[dest % N_GY][:, None]
    source = np.arange(N_ALL)
    gx = (2 * (source % N_CHIP // N_GY) + source // N_CHIP)[None]
    gy = (source % N_GY)[None]
    angle = (2 * kx * gx + ky * gy) % N_GY * (2.0 * math.pi / N_GY)
    table = np.concatenate([np.cos(angle), -np.sin(angle)])
    high = table.astype(ml_dtypes.bfloat16)
    return high, (table - high.astype(np.float64)).astype(ml_dtypes.bfloat16)


def cos_sin(place, mode, length):
    angle = ((place * mode) % length).astype(F32) * (2.0 * math.pi / length)
    return jnp.cos(angle), jnp.sin(angle)


def local_tables(rp, rq):
    line = lax.broadcasted_iota(jnp.int32, (2 * LY, 2 * LY), 0)
    col = lax.broadcasted_iota(jnp.int32, (2 * LY, 2 * LY), 1)
    rest = col - 4 * BLOCKS
    in_block = rest < 0
    part_in = jnp.where(in_block, col // (2 * BLOCKS), rest >> 1) & 1
    place = jnp.where(
        in_block,
        col % BLOCKS + (LY - BLOCKS) * (col // BLOCKS & 1),
        BLOCKS + (rest >> 2) + WIDE * (rest & 1),
    )
    cosine, sine = cos_sin(place, 32 * (line % LY) + rq, NY)
    part_out = line // LY
    sign = jnp.where(part_out < part_in, 1.0, -1.0)
    y_matrix = jnp.where(part_out == part_in, cosine, sign * sine) * (1.0 / math.sqrt(NX * NY))
    line = lax.broadcasted_iota(jnp.int32, (LX, LX), 0)
    col = lax.broadcasted_iota(jnp.int32, (LX, LX), 1)
    return (y_matrix, *cos_sin(line, 16 * col + rp, NX))


def call(kernel, outs, *args, scratch=(), in_hbm=False, out_hbm=False, mib=40):
    def spec(hbm):
        return pl.BlockSpec(memory_space=pltpu.HBM if hbm else pltpu.VMEM)

    return pl.pallas_call(
        kernel,
        out_shape=outs,
        in_specs=[spec(in_hbm)] * len(args),
        out_specs=spec(out_hbm),
        scratch_shapes=scratch,
        compiler_params=pltpu.CompilerParams(vmem_limit_bytes=mib * 1024 * 1024),
    )(*args)


def shape(*dims):
    return jax.ShapeDtypeStruct(dims, F32)


def body(p_now, p_prev, phase, div_star):
    padded = (PLANES + 2, LY, LX)
    chunks = call(
        stencil_kernel,
        shape(ROWS * N_CHIP, LX),
        p_now,
        p_prev,
        phase,
        div_star,
        scratch=[
            pltpu.VMEM(padded, F32),
            pltpu.VMEM(padded, F32),
            pltpu.VMEM(padded, jnp.int32),
            pltpu.VMEM((PLANES, LY, LX), F32),
            pltpu.VMEM((ROWS * N_CHIP, LX), F32),
            pltpu.SemaphoreType.DMA((PLANES // GROUP, 4)),
            pltpu.SemaphoreType.DMA((PLANES // GROUP,)),
        ],
        in_hbm=True,
        out_hbm=True,
        mib=60,
    )
    chunks = lax.all_to_all(chunks.reshape(N_CHIP, 1, ROWS * LX), CHIPS, 0, 0, tiled=True)
    chunks, rp, rq = lax.optimization_barrier(
        (
            chunks.reshape(ROWS * N_CHIP, LX),
            reversal(lax.axis_index(("zh", "x", "c")), 4),
            reversal(lax.axis_index(("zl", "y")), 5),
        )
    )
    other = lax.ppermute(chunks, "c", [(0, 1), (1, 0)])
    other, tables = lax.optimization_barrier((other, local_tables(rp, rq)))
    high, low = device_tables()
    modes = call(
        device_kernel,
        shape(4 * N_ALL, LX),
        chunks,
        other,
        jnp.asarray(high),
        jnp.asarray(low),
        scratch=[pltpu.VMEM((N_ALL, 2 * LX), F32)],
    )
    back = lax.all_to_all(modes.reshape(N_ALL, 4, LX), EVERYWHERE, 0, 0, tiled=True)
    result = call(
        local_kernel,
        shape(2, PLANES, LY, LX),
        back.reshape(4 * N_ALL, LX),
        *tables,
        scratch=[
            pltpu.VMEM((2, PLANES, LY, LX), F32),
            pltpu.SemaphoreType.DMA((PLANES // PAIR, 2)),
        ],
        out_hbm=True,
    )
    return result.reshape(2, PLANES, 1, LY, 1, LX)


def solution(mesh):
    fine = Mesh(mesh.devices.reshape(2, 4, 2, 8, 4), EVERYWHERE)
    spec = P(None, ("zl", "y"), ("zh", "x", "c"))
    return jax.shard_map(
        body,
        mesh=fine,
        in_specs=(spec, spec, spec, spec),
        out_specs=P(None, None, ("zl", "y"), None, ("zh", "x", "c"), None),
        check_vma=False,
    )
```

```python
import math

import jax
import jax.numpy as jnp
import ml_dtypes
import numpy as np
from jax import lax
from jax.experimental import pallas as pl
from jax.experimental.pallas import tpu as pltpu
from jax.sharding import Mesh
from jax.sharding import PartitionSpec as P

NX = 2048
NY = 2048
PLANES = 16
LY = 64
LX = 128
N_GX = 16
N_GY = 32
N_ALL = N_GX * N_GY
N_CHIP = N_ALL // 2
F32 = jnp.float32
BF16 = jnp.bfloat16

EVERYWHERE = ("zh", "x", "c", "zl", "y")

LIQUID = 7.0 / 8.0
MIXED = 7.0 / 9.0
QUAD = -4.0 / 9.0
LIN = 11.5 / 9.0

BLOCKS = 16
BLOCK = LX // BLOCKS
WIDE = 16
HALF = LY // 2
TEAMS = PLANES
ROWS = 5
GROUP = 4
PAIR = 2
QUARTER = LX // 4


def reversal(index, digits):
    total = 0
    for place in range(digits):
        total = total * 2 + ((index >> place) & 1)
    return total


def split(value):
    high = value.astype(BF16)
    return high, (value - high.astype(F32)).astype(BF16)


def dot3(left, right):
    left_high, left_low = left
    right_high, right_low = right
    return (
        jnp.dot(left_high, right_high, preferred_element_type=F32)
        + jnp.dot(left_high, right_low, preferred_element_type=F32)
        + jnp.dot(left_low, right_high, preferred_element_type=F32)
    )


def weighted(count, difference):
    return count * (LIN + QUAD * count) * difference


def flux(liquid_a, liquid_b, field_a, field_b):
    return jnp.where(liquid_a == liquid_b, liquid_a, MIXED) * (field_b - field_a)


def roll(value, by, axis):
    if isinstance(by, int):
        by = by % value.shape[axis]
        return pltpu.roll(value, by, axis) if by else value
    return pltpu.roll(value, by & (value.shape[axis] - 1), axis)


def lanes_of(rows):
    return lax.broadcasted_iota(jnp.int32, (rows, LX), 1)


def rows_of(rows):
    return lax.broadcasted_iota(jnp.int32, (rows, LX), 0)


def within(lane, start, count):
    return ((lane - start) & (LX - 1)) < count


def turn(value, block, sign, offset):
    value = roll(value, -offset, 0)
    for bit in (1, 2, 4, 8):
        value = jnp.where((block & bit) != 0, roll(value, -sign * bit, 0), value)
    return value


def cell_block():
    return ((lanes_of(BLOCKS) + BLOCK // 2) // BLOCK) & (BLOCKS - 1)


def stencil_kernel(
    now_hbm,
    prev_hbm,
    phase_hbm,
    div_hbm,
    out_hbm,
    now_ref,
    prev_ref,
    phase_ref,
    div_ref,
    out,
    sems,
    out_sems,
):
    copies, sent = [], []
    for g in range(PLANES // GROUP):
        first = GROUP * g + 2 if g else 0
        planes = pl.ds(first, GROUP * (g + 1) + 2 - first)
        inner = pl.ds(GROUP * g, GROUP)
        copies.append(
            [
                pltpu.make_async_copy(source.at[part], target.at[part], sems.at[g, a])
                for a, (source, target, part) in enumerate(
                    (
                        (now_hbm, now_ref, planes),
                        (prev_hbm, prev_ref, planes),
                        (phase_hbm, phase_ref, planes),
                        (div_hbm, div_ref, inner),
                    )
                )
            ]
        )
        for copy in copies[-1]:
            copy.start()

    lane = lanes_of(LY)
    row = rows_of(LY)
    sub = rows_of(8)
    block = cell_block()
    lane_in = lanes_of(TEAMS)
    owner = rows_of(TEAMS) * BLOCK
    moved = rows_of(TEAMS) % 4 == 0
    edge_lane = (lane == 0) | (lane == LX - 1)
    y_lanes = [within(lane_in, QUARTER * f + owner, BLOCK) for f in range(4)]

    def plane(k):
        return 2.0 * now_ref[k] - prev_ref[k], jnp.where(phase_ref[k] == 1, LIQUID, 0.0)

    for k in range(PLANES):
        if k % GROUP == 0:
            for copy in copies[k // GROUP]:
                copy.wait()
        if k == 0:
            field_before, liquid_before = plane(0)
            field, liquid = plane(1)
            flux_z = flux(liquid_before, liquid, field_before, field)
        field_after, liquid_after = plane(k + 2)
        flux_z_upper = flux(liquid, liquid_after, field, field_after)
        total = div_ref[k] + (flux_z_upper - flux_z)
        upper = flux(liquid, roll(liquid, -1, 1), field, roll(field, -1, 1))
        upper = jnp.where(lane == LX - 1, 0.0, upper)
        total = total + (upper - roll(upper, 1, 1))
        upper = flux(liquid, roll(liquid, -1, 0), field, roll(field, -1, 0))
        upper = jnp.where(row == LY - 1, 0.0, upper)
        total = total + (upper - roll(upper, 1, 0))
        ends = jnp.where(edge_lane, field, 0.0) + roll(
            jnp.where(edge_lane, liquid, 0.0), QUARTER, 1
        )
        faces = roll(ends[:BLOCKS], 1, 1)
        faces = faces + roll(roll(ends[LY - BLOCKS :], 1, 0), 3, 1)
        faces = faces + roll(ends[BLOCKS:HALF], 5, 1)
        faces = faces + roll(ends[HALF : HALF + WIDE], 7, 1)
        faces = jnp.where(moved, roll(faces, BLOCK, 1), faces)
        lines = jnp.broadcast_to(liquid[LY - 1 : LY], (8, LX))
        for f, line in ((2, field[LY - 1 : LY]), (1, liquid[0:1]), (0, field[0:1])):
            lines = jnp.where(sub <= f, jnp.broadcast_to(line, (8, LX)), lines)
        lines = roll(lines, BLOCK // 2, 1)
        for bit in (1, 2):
            lines = jnp.where((sub & bit) != 0, roll(lines, QUARTER * bit, 1), lines)
        for f in range(4):
            faces = jnp.where(y_lanes[f], jnp.broadcast_to(lines[f : f + 1], (TEAMS, LX)), faces)

        start = k * TEAMS * ROWS
        for r, value in enumerate(
            (
                turn(total[:BLOCKS], block, -1, 0),
                turn(total[LY - BLOCKS :], block, -1, 15),
                total[BLOCKS:HALF],
                total[HALF : HALF + WIDE],
                faces,
            )
        ):
            out[pl.ds(start + r, TEAMS, stride=ROWS), :] = value
        field, liquid, flux_z = field_after, liquid_after, flux_z_upper
        if k % GROUP == GROUP - 1:
            g = k // GROUP
            rows = pl.ds(g * GROUP * TEAMS * ROWS, GROUP * TEAMS * ROWS)
            sent.append(pltpu.make_async_copy(out.at[rows], out_hbm.at[rows], out_sems.at[g]))
            sent[-1].start()
    for copy in sent:
        copy.wait()


def device_kernel(own_ref, other_ref, high_ref, low_ref, out, cells):
    lane = lanes_of(N_GY)
    core = lax.axis_index("c")
    team = (lax.axis_index("zl") * 4 + lax.axis_index("y")) % TEAMS * BLOCK
    own_y = (lane < BLOCK) & (core == 0)
    at_last, at_first = lane == LX - 1, lane == 0
    groups = N_GX // 2

    def row(ref, g, r):
        return ref[pl.ds((g % groups) * N_GY * ROWS + r, N_GY, stride=ROWS), :]

    def mine(c, g, t):
        refs = (own_ref, other_ref) if c == 0 else (other_ref, own_ref)
        return jnp.where(core == 0, row(refs[0], g, t), row(refs[1], g, 2 + t))

    def face_row(c, g):
        refs = (own_ref, other_ref) if c == 0 else (other_ref, own_ref)
        return jnp.where(core == 0, row(refs[0], g, 4), row(refs[1], g, 4))

    def x_aligned(value):
        return roll(value, 2 * LX - 1 - 4 * core - BLOCK * (team % (4 * BLOCK) == 0), 1)

    def x_parts(here, there):
        lower = roll(there, -1, 1)
        value = weighted(roll(here + lower, -QUARTER, 1), lower - here)
        return [(value, roll(value, 1, 1)), (roll(value, -2, 1), roll(value, -1, 1))]

    def y_part(here):
        here = roll(here, LX - team, 1)
        lower = roll(here, -1, 0)
        upper = roll(here, -2 * QUARTER, 1)
        value = weighted(roll(upper + lower, -QUARTER, 1), lower - upper)
        return roll(jnp.where(own_y, value, 0.0), team + (LX - BLOCK // 2), 1)

    raw = [face_row(c, 0) for c in range(2)]
    faces = [x_aligned(value) for value in raw]
    entering = x_parts(x_aligned(face_row(1, groups - 1)), faces[0])
    for g in range(groups):
        next_raw = [face_row(c, g + 1) for c in range(2)]
        after = [x_aligned(value) for value in next_raw]
        for c in range(2):
            leaving = x_parts(faces[c], after[0] if c else faces[1])
            along_y = y_part(raw[c])
            part = [
                mine(c, g, t)
                + jnp.where(at_last, leaving[t][0], 0.0)
                - jnp.where(at_first, entering[t][1], 0.0)
                for t in range(2)
            ]
            place = pl.ds(c * N_CHIP + g * N_GY, N_GY)
            cells[place, :LX] = part[0] - roll(along_y, 1, 0)
            cells[place, LX:] = part[1] + along_y
            entering = leaving
        raw, faces = next_raw, after

    right_high, right_low = split(cells[...])
    result = dot3((high_ref[...], low_ref[...]), (right_high, right_low))
    for part in range(2):
        rows = slice(part * N_ALL, (part + 1) * N_ALL)
        out[pl.ds(2 * part, N_ALL, stride=4), :] = result[rows, :LX]
        out[pl.ds(2 * part + 1, N_ALL, stride=4), :] = result[rows, LX:]


def local_kernel(x_ref, y_matrix_ref, cos_ref, sin_ref, out_hbm, out, sems):
    y_matrix = split(y_matrix_ref[...])
    x_matrix = split(
        jnp.concatenate(
            [
                jnp.concatenate([cos_ref[...], -sin_ref[...]], axis=1),
                jnp.concatenate([sin_ref[...], cos_ref[...]], axis=1),
            ],
            axis=0,
        )
    )
    block = cell_block()
    copies = []
    for g in range(PLANES // PAIR):
        group = []
        for k in range(PAIR * g, PAIR * (g + 1)):
            start = (k // 2) * 4 * LY + (k % 2) * LY
            lines = [
                turn(x_ref[pl.ds(start + kind, BLOCKS, stride=4), :], block, 1, kind & 1)
                for kind in range(4)
            ]
            lines.append(x_ref[pl.ds(start + 2 * LY, LY), :])
            group.append(jnp.concatenate(lines, axis=0))
        lines = dot3(y_matrix, split(jnp.concatenate(group, axis=1)))
        lines = jnp.concatenate(
            [
                jnp.concatenate(
                    [lines[:LY, k * LX : (k + 1) * LX], lines[LY:, k * LX : (k + 1) * LX]], axis=1
                )
                for k in range(PAIR)
            ],
            axis=0,
        )
        modes = dot3(split(lines), x_matrix)
        for part in range(2):
            for k in range(PAIR):
                out[part, PAIR * g + k] = modes[k * LY : (k + 1) * LY, part * LX : (part + 1) * LX]
            planes = (part, pl.ds(g * PAIR, PAIR))
            copies.append(
                pltpu.make_async_copy(out.at[planes], out_hbm.at[planes], sems.at[g, part])
            )
            copies[-1].start()
    for copy in copies:
        copy.wait()


def device_tables():
    dest = np.arange(N_ALL) ^ N_ALL // 2
    rev_p = np.array([reversal(i, 4) for i in range(N_GX)])
    rev_q = np.array([reversal(i, 5) for i in range(N_GY)])
    kx = rev_p[dest // N_GY][:, None]
    ky = rev_q[dest % N_GY][:, None]
    source = np.arange(N_ALL)
    gx = (2 * (source % N_CHIP // N_GY) + source // N_CHIP ^ N_GX // 2)[None]
    gy = (source % N_GY)[None]
    angle = (2 * kx * gx + ky * gy) % N_GY * (2.0 * math.pi / N_GY)
    table = np.concatenate([np.cos(angle), -np.sin(angle)])
    high = table.astype(ml_dtypes.bfloat16)
    return high, (table - high.astype(np.float64)).astype(ml_dtypes.bfloat16)


def cos_sin(place, mode, length):
    angle = ((place * mode) % length).astype(F32) * (2.0 * math.pi / length)
    return jnp.cos(angle), jnp.sin(angle)


def local_tables(rp, rq):
    line = lax.broadcasted_iota(jnp.int32, (2 * LY, 2 * LY), 0)
    col = lax.broadcasted_iota(jnp.int32, (2 * LY, 2 * LY), 1)
    rest = col - 4 * BLOCKS
    in_block = rest < 0
    part_in = jnp.where(in_block, col // (2 * BLOCKS), rest >> 1) & 1
    place = jnp.where(
        in_block,
        col % BLOCKS + (LY - BLOCKS) * (col // BLOCKS & 1),
        BLOCKS + (rest >> 2) + WIDE * (rest & 1),
    )
    cosine, sine = cos_sin(place, 32 * (line % LY) + rq, NY)
    part_out = line // LY
    sign = jnp.where(part_out < part_in, 1.0, -1.0)
    y_matrix = jnp.where(part_out == part_in, cosine, sign * sine) * (1.0 / math.sqrt(NX * NY))
    line = lax.broadcasted_iota(jnp.int32, (LX, LX), 0)
    col = lax.broadcasted_iota(jnp.int32, (LX, LX), 1)
    return (y_matrix, *cos_sin(line, 16 * col + rp, NX))


def call(kernel, outs, *args, scratch=(), in_hbm=False, out_hbm=False, mib=40):
    def spec(hbm):
        return pl.BlockSpec(memory_space=pltpu.HBM if hbm else pltpu.VMEM)

    return pl.pallas_call(
        kernel,
        out_shape=outs,
        in_specs=[spec(in_hbm)] * len(args),
        out_specs=spec(out_hbm),
        scratch_shapes=scratch,
        compiler_params=pltpu.CompilerParams(vmem_limit_bytes=mib * 1024 * 1024),
    )(*args)


def exchange(chunks, per_core):
    order = np.arange(N_ALL).reshape(2, 4, 2, 8, 4)[::-1]
    groups = [order[:, :, c].ravel() for c in range(2)] if per_core else [order.ravel()]
    return lax.all_to_all(
        chunks,
        EVERYWHERE,
        0,
        0,
        axis_index_groups=[[int(device) for device in group] for group in groups],
        tiled=True,
    )


def shape(*dims):
    return jax.ShapeDtypeStruct(dims, F32)


def body(p_now, p_prev, phase, div_star):
    padded = (PLANES + 2, LY, LX)
    chunks = call(
        stencil_kernel,
        shape(ROWS * N_CHIP, LX),
        p_now,
        p_prev,
        phase,
        div_star,
        scratch=[
            pltpu.VMEM(padded, F32),
            pltpu.VMEM(padded, F32),
            pltpu.VMEM(padded, jnp.int32),
            pltpu.VMEM((PLANES, LY, LX), F32),
            pltpu.VMEM((ROWS * N_CHIP, LX), F32),
            pltpu.SemaphoreType.DMA((PLANES // GROUP, 4)),
            pltpu.SemaphoreType.DMA((PLANES // GROUP,)),
        ],
        in_hbm=True,
        out_hbm=True,
        mib=60,
    )
    chunks = exchange(chunks.reshape(N_CHIP, 1, ROWS * LX), per_core=True)
    chunks, rp, rq = lax.optimization_barrier(
        (
            chunks.reshape(ROWS * N_CHIP, LX),
            reversal(lax.axis_index(("zh", "x", "c")), 4),
            reversal(lax.axis_index(("zl", "y")), 5),
        )
    )
    other = lax.ppermute(chunks, "c", [(0, 1), (1, 0)])
    other, tables = lax.optimization_barrier((other, local_tables(rp, rq)))
    high, low = device_tables()
    modes = call(
        device_kernel,
        shape(4 * N_ALL, LX),
        chunks,
        other,
        jnp.asarray(high),
        jnp.asarray(low),
        scratch=[pltpu.VMEM((N_ALL, 2 * LX), F32)],
    )
    back = exchange(modes.reshape(N_ALL, 4, LX), per_core=False)
    result = call(
        local_kernel,
        shape(2, PLANES, LY, LX),
        back.reshape(4 * N_ALL, LX),
        *tables,
        scratch=[
            pltpu.VMEM((2, PLANES, LY, LX), F32),
            pltpu.SemaphoreType.DMA((PLANES // PAIR, 2)),
        ],
        out_hbm=True,
    )
    return result.reshape(2, PLANES, 1, LY, 1, LX)


def solution(mesh):
    fine = Mesh(mesh.devices.reshape(2, 4, 2, 8, 4), EVERYWHERE)
    spec = P(None, ("zl", "y"), ("zh", "x", "c"))
    return jax.shard_map(
        body,
        mesh=fine,
        in_specs=(spec, spec, spec, spec),
        out_specs=P(None, None, ("zl", "y"), None, ("zh", "x", "c"), None),
        check_vma=False,
    )
```

```python
import math

import jax
import jax.numpy as jnp
import ml_dtypes
import numpy as np
from jax import lax
from jax.experimental import pallas as pl
from jax.experimental.pallas import tpu as pltpu
from jax.sharding import Mesh
from jax.sharding import PartitionSpec as P

NX = 2048
NY = 2048
PLANES = 16
LY = 64
LX = 128
N_GX = 16
N_GY = 32
N_ALL = N_GX * N_GY
N_CHIP = N_ALL // 2
F32 = jnp.float32
BF16 = jnp.bfloat16

EVERYWHERE = ("zh", "x", "c", "zl", "y")

LIQUID = 7.0 / 8.0
MIXED = 7.0 / 9.0
QUAD = -4.0 / 9.0
LIN = 11.5 / 9.0

BLOCKS = 16
BLOCK = LX // BLOCKS
WIDE = 16
HALF = LY // 2
TEAMS = PLANES
ROWS = 5
GROUP = 4
PAIR = 2
QUARTER = LX // 4


def reversal(index, digits):
    total = 0
    for place in range(digits):
        total = total * 2 + ((index >> place) & 1)
    return total


def split(value):
    high = value.astype(BF16)
    return high, (value - high.astype(F32)).astype(BF16)


def dot3(left, right):
    left_high, left_low = left
    right_high, right_low = right
    return (
        jnp.dot(left_high, right_high, preferred_element_type=F32)
        + jnp.dot(left_high, right_low, preferred_element_type=F32)
        + jnp.dot(left_low, right_high, preferred_element_type=F32)
    )


def weighted(count, difference):
    return count * (LIN + QUAD * count) * difference


def flux(liquid_a, liquid_b, field_a, field_b):
    return jnp.where(liquid_a == liquid_b, liquid_a, MIXED) * (field_b - field_a)


def roll(value, by, axis):
    if isinstance(by, int):
        by = by % value.shape[axis]
        return pltpu.roll(value, by, axis) if by else value
    return pltpu.roll(value, by & (value.shape[axis] - 1), axis)


def lanes_of(rows):
    return lax.broadcasted_iota(jnp.int32, (rows, LX), 1)


def rows_of(rows):
    return lax.broadcasted_iota(jnp.int32, (rows, LX), 0)


def within(lane, start, count):
    return ((lane - start) & (LX - 1)) < count


def turn(value, block, sign, offset):
    value = roll(value, -offset, 0)
    for bit in (1, 2, 4, 8):
        value = jnp.where((block & bit) != 0, roll(value, -sign * bit, 0), value)
    return value


def cell_block():
    return ((lanes_of(BLOCKS) + BLOCK // 2) // BLOCK) & (BLOCKS - 1)


def stencil_kernel(
    now_hbm,
    prev_hbm,
    phase_hbm,
    div_hbm,
    out_hbm,
    now_ref,
    prev_ref,
    phase_ref,
    div_ref,
    out,
    sems,
    out_sems,
):
    copies, sent = [], []
    for g in range(PLANES // GROUP):
        first = GROUP * g + 2 if g else 0
        planes = pl.ds(first, GROUP * (g + 1) + 2 - first)
        inner = pl.ds(GROUP * g, GROUP)
        copies.append(
            [
                pltpu.make_async_copy(source.at[part], target.at[part], sems.at[g, a])
                for a, (source, target, part) in enumerate(
                    (
                        (now_hbm, now_ref, planes),
                        (prev_hbm, prev_ref, planes),
                        (phase_hbm, phase_ref, planes),
                        (div_hbm, div_ref, inner),
                    )
                )
            ]
        )
        for copy in copies[-1]:
            copy.start()

    lane = lanes_of(LY)
    row = rows_of(LY)
    sub = rows_of(8)
    block = cell_block()
    lane_in = lanes_of(TEAMS)
    owner = rows_of(TEAMS) * BLOCK
    moved = rows_of(TEAMS) % 4 == 0
    edge_lane = (lane == 0) | (lane == LX - 1)
    y_lanes = [within(lane_in, QUARTER * f + owner, BLOCK) for f in range(4)]

    def plane(k):
        return 2.0 * now_ref[k] - prev_ref[k], jnp.where(phase_ref[k] == 1, LIQUID, 0.0)

    for k in range(PLANES):
        if k % GROUP == 0:
            for copy in copies[k // GROUP]:
                copy.wait()
        if k == 0:
            field_before, liquid_before = plane(0)
            field, liquid = plane(1)
            flux_z = flux(liquid_before, liquid, field_before, field)
        field_after, liquid_after = plane(k + 2)
        flux_z_upper = flux(liquid, liquid_after, field, field_after)
        total = div_ref[k] + (flux_z_upper - flux_z)
        upper = flux(liquid, roll(liquid, -1, 1), field, roll(field, -1, 1))
        upper = jnp.where(lane == LX - 1, 0.0, upper)
        total = total + (upper - roll(upper, 1, 1))
        upper = flux(liquid, roll(liquid, -1, 0), field, roll(field, -1, 0))
        upper = jnp.where(row == LY - 1, 0.0, upper)
        total = total + (upper - roll(upper, 1, 0))
        ends = jnp.where(edge_lane, field, 0.0) + roll(
            jnp.where(edge_lane, liquid, 0.0), QUARTER, 1
        )
        faces = roll(ends[:BLOCKS], 1, 1)
        faces = faces + roll(roll(ends[LY - BLOCKS :], 1, 0), 3, 1)
        faces = faces + roll(ends[BLOCKS:HALF], 5, 1)
        faces = faces + roll(ends[HALF : HALF + WIDE], 7, 1)
        faces = jnp.where(moved, roll(faces, BLOCK, 1), faces)
        lines = jnp.broadcast_to(liquid[LY - 1 : LY], (8, LX))
        for f, line in ((2, field[LY - 1 : LY]), (1, liquid[0:1]), (0, field[0:1])):
            lines = jnp.where(sub <= f, jnp.broadcast_to(line, (8, LX)), lines)
        lines = roll(lines, BLOCK // 2, 1)
        for bit in (1, 2):
            lines = jnp.where((sub & bit) != 0, roll(lines, QUARTER * bit, 1), lines)
        for f in range(4):
            faces = jnp.where(y_lanes[f], jnp.broadcast_to(lines[f : f + 1], (TEAMS, LX)), faces)

        start = k * TEAMS * ROWS
        for r, value in enumerate(
            (
                turn(total[:BLOCKS], block, -1, 0),
                turn(total[LY - BLOCKS :], block, -1, 15),
                total[BLOCKS:HALF],
                total[HALF : HALF + WIDE],
                faces,
            )
        ):
            out[pl.ds(start + r, TEAMS, stride=ROWS), :] = value
        field, liquid, flux_z = field_after, liquid_after, flux_z_upper
        if k % GROUP == GROUP - 1:
            g = k // GROUP
            rows = pl.ds(g * GROUP * TEAMS * ROWS, GROUP * TEAMS * ROWS)
            sent.append(pltpu.make_async_copy(out.at[rows], out_hbm.at[rows], out_sems.at[g]))
            sent[-1].start()
    for copy in sent:
        copy.wait()


def device_kernel(own_ref, other_ref, high_ref, low_ref, out, cells):
    lane = lanes_of(N_GY)
    core = lax.axis_index("c")
    team = (lax.axis_index("zl") * 4 + lax.axis_index("y")) % TEAMS * BLOCK
    own_y = (lane < BLOCK) & (core == 0)
    at_last, at_first = lane == LX - 1, lane == 0
    groups = N_GX // 2

    def row(ref, g, r):
        return ref[pl.ds((g % groups) * N_GY * ROWS + r, N_GY, stride=ROWS), :]

    def mine(c, g, t):
        refs = (own_ref, other_ref) if c == 0 else (other_ref, own_ref)
        return jnp.where(core == 0, row(refs[0], g, t), row(refs[1], g, 2 + t))

    def face_row(c, g):
        refs = (own_ref, other_ref) if c == 0 else (other_ref, own_ref)
        return jnp.where(core == 0, row(refs[0], g, 4), row(refs[1], g, 4))

    def x_aligned(value):
        return roll(value, 2 * LX - 1 - 4 * core - BLOCK * (team % (4 * BLOCK) == 0), 1)

    def x_parts(here, there):
        lower = roll(there, -1, 1)
        value = weighted(roll(here + lower, -QUARTER, 1), lower - here)
        return [(value, roll(value, 1, 1)), (roll(value, -2, 1), roll(value, -1, 1))]

    def y_part(here):
        here = roll(here, LX - team, 1)
        lower = roll(here, -1, 0)
        upper = roll(here, -2 * QUARTER, 1)
        value = weighted(roll(upper + lower, -QUARTER, 1), lower - upper)
        return roll(jnp.where(own_y, value, 0.0), team + (LX - BLOCK // 2), 1)

    raw = [face_row(c, 0) for c in range(2)]
    faces = [x_aligned(value) for value in raw]
    entering = x_parts(x_aligned(face_row(1, groups - 1)), faces[0])
    for g in range(groups):
        next_raw = [face_row(c, g + 1) for c in range(2)]
        after = [x_aligned(value) for value in next_raw]
        for c in range(2):
            leaving = x_parts(faces[c], after[0] if c else faces[1])
            along_y = y_part(raw[c])
            part = [
                mine(c, g, t)
                + jnp.where(at_last, leaving[t][0], 0.0)
                - jnp.where(at_first, entering[t][1], 0.0)
                for t in range(2)
            ]
            place = pl.ds(c * N_CHIP + g * N_GY, N_GY)
            cells[place, :LX] = part[0] - roll(along_y, 1, 0)
            cells[place, LX:] = part[1] + along_y
            entering = leaving
        raw, faces = next_raw, after

    right_high, right_low = split(cells[...])
    result = dot3((high_ref[...], low_ref[...]), (right_high, right_low))
    for part in range(2):
        rows = slice(part * N_ALL, (part + 1) * N_ALL)
        out[pl.ds(2 * part, N_ALL, stride=4), :] = result[rows, :LX]
        out[pl.ds(2 * part + 1, N_ALL, stride=4), :] = result[rows, LX:]


def local_kernel(x_ref, y_matrix_ref, cos_ref, sin_ref, out_hbm, out, sems):
    y_matrix = split(y_matrix_ref[...])
    x_matrix = split(
        jnp.concatenate(
            [
                jnp.concatenate([cos_ref[...], -sin_ref[...]], axis=1),
                jnp.concatenate([sin_ref[...], cos_ref[...]], axis=1),
            ],
            axis=0,
        )
    )
    block = cell_block()
    copies = []
    for g in range(PLANES // PAIR):
        group = []
        for k in range(PAIR * g, PAIR * (g + 1)):
            start = (k // 2 ^ TEAMS // 4) * 4 * LY + (k % 2) * LY
            lines = [
                turn(x_ref[pl.ds(start + kind, BLOCKS, stride=4), :], block, 1, kind & 1)
                for kind in range(4)
            ]
            lines.append(x_ref[pl.ds(start + 2 * LY, LY), :])
            group.append(jnp.concatenate(lines, axis=0))
        lines = dot3(y_matrix, split(jnp.concatenate(group, axis=1)))
        lines = jnp.concatenate(
            [
                jnp.concatenate(
                    [lines[:LY, k * LX : (k + 1) * LX], lines[LY:, k * LX : (k + 1) * LX]], axis=1
                )
                for k in range(PAIR)
            ],
            axis=0,
        )
        modes = dot3(split(lines), x_matrix)
        for part in range(2):
            for k in range(PAIR):
                out[part, PAIR * g + k] = modes[k * LY : (k + 1) * LY, part * LX : (part + 1) * LX]
            planes = (part, pl.ds(g * PAIR, PAIR))
            copies.append(
                pltpu.make_async_copy(out.at[planes], out_hbm.at[planes], sems.at[g, part])
            )
            copies[-1].start()
    for copy in copies:
        copy.wait()


def device_tables():
    dest = np.arange(N_ALL)
    rev_p = np.array([reversal(i, 4) for i in range(N_GX)])
    rev_q = np.array([reversal(i, 5) for i in range(N_GY)])
    kx = rev_p[dest // N_GY][:, None]
    ky = rev_q[dest % N_GY][:, None]
    source = np.arange(N_ALL)
    gx = (2 * (source % N_CHIP // N_GY) + source // N_CHIP ^ N_GX // 2)[None]
    gy = (source % N_GY)[None]
    angle = (2 * kx * gx + ky * gy) % N_GY * (2.0 * math.pi / N_GY)
    table = np.concatenate([np.cos(angle), -np.sin(angle)])
    high = table.astype(ml_dtypes.bfloat16)
    return high, (table - high.astype(np.float64)).astype(ml_dtypes.bfloat16)


def cos_sin(place, mode, length):
    angle = ((place * mode) % length).astype(F32) * (2.0 * math.pi / length)
    return jnp.cos(angle), jnp.sin(angle)


def local_tables(rp, rq):
    line = lax.broadcasted_iota(jnp.int32, (2 * LY, 2 * LY), 0)
    col = lax.broadcasted_iota(jnp.int32, (2 * LY, 2 * LY), 1)
    rest = col - 4 * BLOCKS
    in_block = rest < 0
    part_in = jnp.where(in_block, col // (2 * BLOCKS), rest >> 1) & 1
    place = jnp.where(
        in_block,
        col % BLOCKS + (LY - BLOCKS) * (col // BLOCKS & 1),
        BLOCKS + (rest >> 2) + WIDE * (rest & 1),
    )
    cosine, sine = cos_sin(place, 32 * (line % LY) + rq, NY)
    part_out = line // LY
    sign = jnp.where(part_out < part_in, 1.0, -1.0)
    y_matrix = jnp.where(part_out == part_in, cosine, sign * sine) * (1.0 / math.sqrt(NX * NY))
    line = lax.broadcasted_iota(jnp.int32, (LX, LX), 0)
    col = lax.broadcasted_iota(jnp.int32, (LX, LX), 1)
    return (y_matrix, *cos_sin(line, 16 * col + rp, NX))


def call(kernel, outs, *args, scratch=(), in_hbm=False, out_hbm=False, mib=40):
    def spec(hbm):
        return pl.BlockSpec(memory_space=pltpu.HBM if hbm else pltpu.VMEM)

    return pl.pallas_call(
        kernel,
        out_shape=outs,
        in_specs=[spec(in_hbm)] * len(args),
        out_specs=spec(out_hbm),
        scratch_shapes=scratch,
        compiler_params=pltpu.CompilerParams(vmem_limit_bytes=mib * 1024 * 1024),
    )(*args)


def first_exchange(chunks):
    order = np.arange(N_ALL).reshape(2, 4, 2, 8, 4)[::-1]
    groups = [[int(device) for device in order[:, :, c].ravel()] for c in range(2)]
    return lax.all_to_all(chunks, EVERYWHERE, 0, 0, axis_index_groups=groups, tiled=True)


def shape(*dims):
    return jax.ShapeDtypeStruct(dims, F32)


def body(p_now, p_prev, phase, div_star):
    padded = (PLANES + 2, LY, LX)
    chunks = call(
        stencil_kernel,
        shape(ROWS * N_CHIP, LX),
        p_now,
        p_prev,
        phase,
        div_star,
        scratch=[
            pltpu.VMEM(padded, F32),
            pltpu.VMEM(padded, F32),
            pltpu.VMEM(padded, jnp.int32),
            pltpu.VMEM((PLANES, LY, LX), F32),
            pltpu.VMEM((ROWS * N_CHIP, LX), F32),
            pltpu.SemaphoreType.DMA((PLANES // GROUP, 4)),
            pltpu.SemaphoreType.DMA((PLANES // GROUP,)),
        ],
        in_hbm=True,
        out_hbm=True,
        mib=60,
    )
    chunks = first_exchange(chunks.reshape(N_CHIP, 1, ROWS * LX))
    chunks, rp, rq = lax.optimization_barrier(
        (
            chunks.reshape(ROWS * N_CHIP, LX),
            reversal(lax.axis_index(("zh", "x", "c")), 4),
            reversal(lax.axis_index(("zl", "y")), 5),
        )
    )
    other = lax.ppermute(chunks, "c", [(0, 1), (1, 0)])
    other, tables = lax.optimization_barrier((other, local_tables(rp, rq)))
    high, low = device_tables()
    modes = call(
        device_kernel,
        shape(4 * N_ALL, LX),
        chunks,
        other,
        jnp.asarray(high),
        jnp.asarray(low),
        scratch=[pltpu.VMEM((N_ALL, 2 * LX), F32)],
    )
    back = lax.all_to_all(modes.reshape(N_ALL, 4, LX), EVERYWHERE, 0, 0, tiled=True)
    result = call(
        local_kernel,
        shape(2, PLANES, LY, LX),
        back.reshape(4 * N_ALL, LX),
        *tables,
        scratch=[
            pltpu.VMEM((2, PLANES, LY, LX), F32),
            pltpu.SemaphoreType.DMA((PLANES // PAIR, 2)),
        ],
        out_hbm=True,
    )
    return result.reshape(2, PLANES, 1, LY, 1, LX)


def solution(mesh):
    fine = Mesh(mesh.devices.reshape(2, 4, 2, 8, 4), EVERYWHERE)
    spec = P(None, ("zl", "y"), ("zh", "x", "c"))
    return jax.shard_map(
        body,
        mesh=fine,
        in_specs=(spec, spec, spec, spec),
        out_specs=P(None, None, ("zl", "y"), None, ("zh", "x", "c"), None),
        check_vma=False,
    )
```

```python
import math

import jax
import jax.numpy as jnp
import ml_dtypes
import numpy as np
from jax import lax
from jax.experimental import pallas as pl
from jax.experimental.pallas import tpu as pltpu
from jax.sharding import Mesh
from jax.sharding import PartitionSpec as P

NX = 2048
NY = 2048
PLANES = 16
LY = 64
LX = 128
N_GX = 16
N_GY = 32
N_ALL = N_GX * N_GY
N_CHIP = N_ALL // 2
F32 = jnp.float32
BF16 = jnp.bfloat16

EVERYWHERE = ("zh", "x", "c", "zl", "y")

LIQUID = 7.0 / 8.0
MIXED = 7.0 / 9.0
QUAD = -4.0 / 9.0
LIN = 11.5 / 9.0

BLOCKS = 16
BLOCK = LX // BLOCKS
WIDE = 16
HALF = LY // 2
TEAMS = PLANES
ROWS = 5
GROUP = 4
PAIR = 2
QUARTER = LX // 4


def reversal(index, digits):
    total = 0
    for place in range(digits):
        total = total * 2 + ((index >> place) & 1)
    return total


def split(value):
    high = value.astype(BF16)
    return high, (value - high.astype(F32)).astype(BF16)


def dot3(left, right):
    left_high, left_low = left
    right_high, right_low = right
    return (
        jnp.dot(left_high, right_high, preferred_element_type=F32)
        + jnp.dot(left_high, right_low, preferred_element_type=F32)
        + jnp.dot(left_low, right_high, preferred_element_type=F32)
    )


def weighted(count, difference):
    return count * (LIN + QUAD * count) * difference


def flux(liquid_a, liquid_b, field_a, field_b):
    return jnp.where(liquid_a == liquid_b, liquid_a, MIXED) * (field_b - field_a)


def roll(value, by, axis):
    if isinstance(by, int):
        by = by % value.shape[axis]
        return pltpu.roll(value, by, axis) if by else value
    return pltpu.roll(value, by & (value.shape[axis] - 1), axis)


def lanes_of(rows):
    return lax.broadcasted_iota(jnp.int32, (rows, LX), 1)


def rows_of(rows):
    return lax.broadcasted_iota(jnp.int32, (rows, LX), 0)


def within(lane, start, count):
    return ((lane - start) & (LX - 1)) < count


def turn(value, block, sign, offset):
    value = roll(value, -offset, 0)
    for bit in (1, 2, 4, 8):
        value = jnp.where((block & bit) != 0, roll(value, -sign * bit, 0), value)
    return value


def cell_block():
    return ((lanes_of(BLOCKS) + BLOCK // 2) // BLOCK) & (BLOCKS - 1)


def stencil_kernel(
    now_hbm,
    prev_hbm,
    phase_hbm,
    div_hbm,
    out_hbm,
    now_ref,
    prev_ref,
    phase_ref,
    div_ref,
    out,
    sems,
    out_sems,
):
    copies, sent = [], []
    for g in range(PLANES // GROUP):
        first = GROUP * g + 2 if g else 0
        planes = pl.ds(first, GROUP * (g + 1) + 2 - first)
        inner = pl.ds(GROUP * g, GROUP)
        copies.append(
            [
                pltpu.make_async_copy(source.at[part], target.at[part], sems.at[g, a])
                for a, (source, target, part) in enumerate(
                    (
                        (now_hbm, now_ref, planes),
                        (prev_hbm, prev_ref, planes),
                        (phase_hbm, phase_ref, planes),
                        (div_hbm, div_ref, inner),
                    )
                )
            ]
        )
        for copy in copies[-1]:
            copy.start()

    lane = lanes_of(LY)
    row = rows_of(LY)
    sub = rows_of(8)
    block = cell_block()
    lane_in = lanes_of(TEAMS)
    owner = rows_of(TEAMS) * BLOCK
    moved = rows_of(TEAMS) % 4 == 0
    edge_lane = (lane == 0) | (lane == LX - 1)
    y_lanes = [within(lane_in, QUARTER * f + owner, BLOCK) for f in range(4)]

    def plane(k):
        return 2.0 * now_ref[k] - prev_ref[k], jnp.where(phase_ref[k] == 1, LIQUID, 0.0)

    for k in range(PLANES):
        if k % GROUP == 0:
            for copy in copies[k // GROUP]:
                copy.wait()
        if k == 0:
            field_before, liquid_before = plane(0)
            field, liquid = plane(1)
            flux_z = flux(liquid_before, liquid, field_before, field)
        field_after, liquid_after = plane(k + 2)
        flux_z_upper = flux(liquid, liquid_after, field, field_after)
        total = div_ref[k] + (flux_z_upper - flux_z)
        upper = flux(liquid, roll(liquid, -1, 1), field, roll(field, -1, 1))
        upper = jnp.where(lane == LX - 1, 0.0, upper)
        total = total + (upper - roll(upper, 1, 1))
        upper = flux(liquid, roll(liquid, -1, 0), field, roll(field, -1, 0))
        upper = jnp.where(row == LY - 1, 0.0, upper)
        total = total + (upper - roll(upper, 1, 0))
        ends = jnp.where(edge_lane, field, 0.0) + roll(
            jnp.where(edge_lane, liquid, 0.0), QUARTER, 1
        )
        faces = roll(ends[:BLOCKS], 1, 1)
        faces = faces + roll(roll(ends[LY - BLOCKS :], 1, 0), 3, 1)
        faces = faces + roll(ends[BLOCKS:HALF], 5, 1)
        faces = faces + roll(ends[HALF : HALF + WIDE], 7, 1)
        faces = jnp.where(moved, roll(faces, BLOCK, 1), faces)
        lines = jnp.broadcast_to(liquid[LY - 1 : LY], (8, LX))
        for f, line in ((2, field[LY - 1 : LY]), (1, liquid[0:1]), (0, field[0:1])):
            lines = jnp.where(sub <= f, jnp.broadcast_to(line, (8, LX)), lines)
        lines = roll(lines, BLOCK // 2, 1)
        for bit in (1, 2):
            lines = jnp.where((sub & bit) != 0, roll(lines, QUARTER * bit, 1), lines)
        for f in range(4):
            faces = jnp.where(y_lanes[f], jnp.broadcast_to(lines[f : f + 1], (TEAMS, LX)), faces)

        start = k * TEAMS * ROWS
        for r, value in enumerate(
            (
                turn(total[:BLOCKS], block, -1, 0),
                turn(total[LY - BLOCKS :], block, -1, 15),
                total[BLOCKS:HALF],
                total[HALF : HALF + WIDE],
                faces,
            )
        ):
            out[pl.ds(start + r, TEAMS, stride=ROWS), :] = value
        field, liquid, flux_z = field_after, liquid_after, flux_z_upper
        if k % GROUP == GROUP - 1:
            g = k // GROUP
            rows = pl.ds(g * GROUP * TEAMS * ROWS, GROUP * TEAMS * ROWS)
            sent.append(pltpu.make_async_copy(out.at[rows], out_hbm.at[rows], out_sems.at[g]))
            sent[-1].start()
    for copy in sent:
        copy.wait()


def device_kernel(own_ref, other_ref, high_ref, low_ref, out, cells):
    lane = lanes_of(N_GY)
    core = lax.axis_index("c")
    team = (lax.axis_index("zl") * 4 + lax.axis_index("y")) % TEAMS * BLOCK
    own_y = (lane < BLOCK) & (core == 0)
    at_last, at_first = lane == LX - 1, lane == 0
    groups = N_GX // 2

    def row(ref, g, r):
        return ref[pl.ds((g % groups) * N_GY * ROWS + r, N_GY, stride=ROWS), :]

    def mine(c, g, t):
        refs = (own_ref, other_ref) if c == 0 else (other_ref, own_ref)
        return jnp.where(core == 0, row(refs[0], g, t), row(refs[1], g, 2 + t))

    def face_row(c, g):
        refs = (own_ref, other_ref) if c == 0 else (other_ref, own_ref)
        return jnp.where(core == 0, row(refs[0], g, 4), row(refs[1], g, 4))

    def x_aligned(value):
        return roll(value, 2 * LX - 1 - 4 * core - BLOCK * (team % (4 * BLOCK) == 0), 1)

    def x_parts(here, there):
        lower = roll(there, -1, 1)
        value = weighted(roll(here + lower, -QUARTER, 1), lower - here)
        return [(value, roll(value, 1, 1)), (roll(value, -2, 1), roll(value, -1, 1))]

    def y_part(here):
        here = roll(here, LX - team, 1)
        lower = roll(here, -1, 0)
        upper = roll(here, -2 * QUARTER, 1)
        value = weighted(roll(upper + lower, -QUARTER, 1), lower - upper)
        return roll(jnp.where(own_y, value, 0.0), team + (LX - BLOCK // 2), 1)

    raw = [face_row(c, 0) for c in range(2)]
    faces = [x_aligned(value) for value in raw]
    entering = x_parts(x_aligned(face_row(1, groups - 1)), faces[0])
    for g in range(groups):
        next_raw = [face_row(c, g + 1) for c in range(2)]
        after = [x_aligned(value) for value in next_raw]
        for c in range(2):
            leaving = x_parts(faces[c], after[0] if c else faces[1])
            along_y = y_part(raw[c])
            part = [
                mine(c, g, t)
                + jnp.where(at_last, leaving[t][0], 0.0)
                - jnp.where(at_first, entering[t][1], 0.0)
                for t in range(2)
            ]
            place = pl.ds(c * N_CHIP + g * N_GY, N_GY)
            cells[place, :LX] = part[0] - roll(along_y, 1, 0)
            cells[place, LX:] = part[1] + along_y
            entering = leaving
        raw, faces = next_raw, after

    right_high, right_low = split(cells[...])
    result = dot3((high_ref[...], low_ref[...]), (right_high, right_low))
    for part in range(2):
        rows = slice(part * N_ALL, (part + 1) * N_ALL)
        out[pl.ds(2 * part, N_ALL, stride=4), :] = result[rows, :LX]
        out[pl.ds(2 * part + 1, N_ALL, stride=4), :] = result[rows, LX:]


def local_kernel(x_ref, y_matrix_ref, cos_ref, sin_ref, out_hbm, out, sems):
    y_matrix = split(y_matrix_ref[...])
    x_matrix = split(
        jnp.concatenate(
            [
                jnp.concatenate([cos_ref[...], -sin_ref[...]], axis=1),
                jnp.concatenate([sin_ref[...], cos_ref[...]], axis=1),
            ],
            axis=0,
        )
    )
    block = cell_block()
    copies = []
    for g in range(PLANES // PAIR):
        group = []
        for k in range(PAIR * g, PAIR * (g + 1)):
            start = (k // 2 ^ TEAMS // 4) * 4 * LY + (k % 2 ^ 1) * LY
            lines = [
                turn(x_ref[pl.ds(start + kind, BLOCKS, stride=4), :], block, 1, kind & 1)
                for kind in range(4)
            ]
            lines.append(x_ref[pl.ds(start + 2 * LY, LY), :])
            group.append(jnp.concatenate(lines, axis=0))
        lines = dot3(y_matrix, split(jnp.concatenate(group, axis=1)))
        lines = jnp.concatenate(
            [
                jnp.concatenate(
                    [lines[:LY, k * LX : (k + 1) * LX], lines[LY:, k * LX : (k + 1) * LX]], axis=1
                )
                for k in range(PAIR)
            ],
            axis=0,
        )
        modes = dot3(split(lines), x_matrix)
        for part in range(2):
            for k in range(PAIR):
                out[part, PAIR * g + k] = modes[k * LY : (k + 1) * LY, part * LX : (part + 1) * LX]
            planes = (part, pl.ds(g * PAIR, PAIR))
            copies.append(
                pltpu.make_async_copy(out.at[planes], out_hbm.at[planes], sems.at[g, part])
            )
            copies[-1].start()
    for copy in copies:
        copy.wait()


def device_tables():
    dest = np.arange(N_ALL)
    rev_p = np.array([reversal(i, 4) for i in range(N_GX)])
    rev_q = np.array([reversal(i, 5) for i in range(N_GY)])
    kx = rev_p[dest // N_GY][:, None]
    ky = rev_q[dest % N_GY][:, None]
    source = np.arange(N_ALL)
    gx = (2 * (source % N_CHIP // N_GY) + source // N_CHIP ^ N_GX // 2)[None]
    gy = (source % N_GY ^ N_GY // 2)[None]
    angle = (2 * kx * gx + ky * gy) % N_GY * (2.0 * math.pi / N_GY)
    table = np.concatenate([np.cos(angle), -np.sin(angle)])
    high = table.astype(ml_dtypes.bfloat16)
    return high, (table - high.astype(np.float64)).astype(ml_dtypes.bfloat16)


def cos_sin(place, mode, length):
    angle = ((place * mode) % length).astype(F32) * (2.0 * math.pi / length)
    return jnp.cos(angle), jnp.sin(angle)


def local_tables(rp, rq):
    line = lax.broadcasted_iota(jnp.int32, (2 * LY, 2 * LY), 0)
    col = lax.broadcasted_iota(jnp.int32, (2 * LY, 2 * LY), 1)
    rest = col - 4 * BLOCKS
    in_block = rest < 0
    part_in = jnp.where(in_block, col // (2 * BLOCKS), rest >> 1) & 1
    place = jnp.where(
        in_block,
        col % BLOCKS + (LY - BLOCKS) * (col // BLOCKS & 1),
        BLOCKS + (rest >> 2) + WIDE * (rest & 1),
    )
    cosine, sine = cos_sin(place, 32 * (line % LY) + rq, NY)
    part_out = line // LY
    sign = jnp.where(part_out < part_in, 1.0, -1.0)
    y_matrix = jnp.where(part_out == part_in, cosine, sign * sine) * (1.0 / math.sqrt(NX * NY))
    line = lax.broadcasted_iota(jnp.int32, (LX, LX), 0)
    col = lax.broadcasted_iota(jnp.int32, (LX, LX), 1)
    return (y_matrix, *cos_sin(line, 16 * col + rp, NX))


def call(kernel, outs, *args, scratch=(), in_hbm=False, out_hbm=False, mib=40):
    def spec(hbm):
        return pl.BlockSpec(memory_space=pltpu.HBM if hbm else pltpu.VMEM)

    return pl.pallas_call(
        kernel,
        out_shape=outs,
        in_specs=[spec(in_hbm)] * len(args),
        out_specs=spec(out_hbm),
        scratch_shapes=scratch,
        compiler_params=pltpu.CompilerParams(vmem_limit_bytes=mib * 1024 * 1024),
    )(*args)


def first_exchange(chunks):
    order = np.roll(np.arange(N_ALL).reshape(2, 4, 2, 8, 4)[::-1], 4, axis=3)
    groups = [[int(device) for device in order[:, :, c].ravel()] for c in range(2)]
    return lax.all_to_all(chunks, EVERYWHERE, 0, 0, axis_index_groups=groups, tiled=True)


def shape(*dims):
    return jax.ShapeDtypeStruct(dims, F32)


def body(p_now, p_prev, phase, div_star):
    padded = (PLANES + 2, LY, LX)
    chunks = call(
        stencil_kernel,
        shape(ROWS * N_CHIP, LX),
        p_now,
        p_prev,
        phase,
        div_star,
        scratch=[
            pltpu.VMEM(padded, F32),
            pltpu.VMEM(padded, F32),
            pltpu.VMEM(padded, jnp.int32),
            pltpu.VMEM((PLANES, LY, LX), F32),
            pltpu.VMEM((ROWS * N_CHIP, LX), F32),
            pltpu.SemaphoreType.DMA((PLANES // GROUP, 4)),
            pltpu.SemaphoreType.DMA((PLANES // GROUP,)),
        ],
        in_hbm=True,
        out_hbm=True,
        mib=60,
    )
    chunks = first_exchange(chunks.reshape(N_CHIP, 1, ROWS * LX))
    chunks, rp, rq = lax.optimization_barrier(
        (
            chunks.reshape(ROWS * N_CHIP, LX),
            reversal(lax.axis_index(("zh", "x", "c")), 4),
            reversal(lax.axis_index(("zl", "y")), 5),
        )
    )
    other = lax.ppermute(chunks, "c", [(0, 1), (1, 0)])
    other, tables = lax.optimization_barrier((other, local_tables(rp, rq)))
    high, low = device_tables()
    modes = call(
        device_kernel,
        shape(4 * N_ALL, LX),
        chunks,
        other,
        jnp.asarray(high),
        jnp.asarray(low),
        scratch=[pltpu.VMEM((N_ALL, 2 * LX), F32)],
    )
    back = lax.all_to_all(modes.reshape(N_ALL, 4, LX), EVERYWHERE, 0, 0, tiled=True)
    result = call(
        local_kernel,
        shape(2, PLANES, LY, LX),
        back.reshape(4 * N_ALL, LX),
        *tables,
        scratch=[
            pltpu.VMEM((2, PLANES, LY, LX), F32),
            pltpu.SemaphoreType.DMA((PLANES // PAIR, 2)),
        ],
        out_hbm=True,
    )
    return result.reshape(2, PLANES, 1, LY, 1, LX)


def solution(mesh):
    fine = Mesh(mesh.devices.reshape(2, 4, 2, 8, 4), EVERYWHERE)
    spec = P(None, ("zl", "y"), ("zh", "x", "c"))
    return jax.shard_map(
        body,
        mesh=fine,
        in_specs=(spec, spec, spec, spec),
        out_specs=P(None, None, ("zl", "y"), None, ("zh", "x", "c"), None),
        check_vma=False,
    )
```

```python
import math

import jax
import jax.numpy as jnp
import ml_dtypes
import numpy as np
from jax import lax
from jax.experimental import pallas as pl
from jax.experimental.pallas import tpu as pltpu
from jax.sharding import Mesh
from jax.sharding import PartitionSpec as P

NX = 2048
NY = 2048
PLANES = 16
LY = 64
LX = 128
N_GX = 16
N_GY = 32
N_ALL = N_GX * N_GY
N_CHIP = N_ALL // 2
F32 = jnp.float32
BF16 = jnp.bfloat16

EVERYWHERE = ("zh", "x", "c", "zl", "y")

LIQUID = 7.0 / 8.0
MIXED = 7.0 / 9.0
QUAD = -4.0 / 9.0
LIN = 11.5 / 9.0

BLOCKS = 16
BLOCK = LX // BLOCKS
WIDE = 16
HALF = LY // 2
TEAMS = PLANES
ROWS = 5
GROUP = 4
FIRST_CHIP = 6
FIRST_Y = 18
PAIR = 2
QUARTER = LX // 4


def reversal(index, digits):
    total = 0
    for place in range(digits):
        total = total * 2 + ((index >> place) & 1)
    return total


def split(value):
    high = value.astype(BF16)
    return high, (value - high.astype(F32)).astype(BF16)


def dot3(left, right):
    left_high, left_low = left
    right_high, right_low = right
    return (
        jnp.dot(left_high, right_high, preferred_element_type=F32)
        + jnp.dot(left_high, right_low, preferred_element_type=F32)
        + jnp.dot(left_low, right_high, preferred_element_type=F32)
    )


def weighted(count, difference):
    return count * (LIN + QUAD * count) * difference


def flux(liquid_a, liquid_b, field_a, field_b):
    return jnp.where(liquid_a == liquid_b, liquid_a, MIXED) * (field_b - field_a)


def roll(value, by, axis):
    if isinstance(by, int):
        by = by % value.shape[axis]
        return pltpu.roll(value, by, axis) if by else value
    return pltpu.roll(value, by & (value.shape[axis] - 1), axis)


def lanes_of(rows):
    return lax.broadcasted_iota(jnp.int32, (rows, LX), 1)


def rows_of(rows):
    return lax.broadcasted_iota(jnp.int32, (rows, LX), 0)


def within(lane, start, count):
    return ((lane - start) & (LX - 1)) < count


def turn(value, block, sign, offset):
    value = roll(value, -offset, 0)
    for bit in (1, 2, 4, 8):
        value = jnp.where((block & bit) != 0, roll(value, -sign * bit, 0), value)
    return value


def cell_block():
    return ((lanes_of(BLOCKS) + BLOCK // 2) // BLOCK) & (BLOCKS - 1)


def stencil_kernel(
    now_hbm,
    prev_hbm,
    phase_hbm,
    div_hbm,
    out_hbm,
    now_ref,
    prev_ref,
    phase_ref,
    div_ref,
    out,
    sems,
    out_sems,
):
    copies, sent = [], []
    for g in range(PLANES // GROUP):
        first = GROUP * g + 2 if g else 0
        planes = pl.ds(first, GROUP * (g + 1) + 2 - first)
        inner = pl.ds(GROUP * g, GROUP)
        copies.append(
            [
                pltpu.make_async_copy(source.at[part], target.at[part], sems.at[g, a])
                for a, (source, target, part) in enumerate(
                    (
                        (now_hbm, now_ref, planes),
                        (prev_hbm, prev_ref, planes),
                        (phase_hbm, phase_ref, planes),
                        (div_hbm, div_ref, inner),
                    )
                )
            ]
        )
        for copy in copies[-1]:
            copy.start()

    lane = lanes_of(LY)
    row = rows_of(LY)
    sub = rows_of(8)
    block = cell_block()
    lane_in = lanes_of(TEAMS)
    owner = rows_of(TEAMS) * BLOCK
    moved = rows_of(TEAMS) % 4 == 0
    edge_lane = (lane == 0) | (lane == LX - 1)
    y_lanes = [within(lane_in, QUARTER * f + owner, BLOCK) for f in range(4)]

    def plane(k):
        return 2.0 * now_ref[k] - prev_ref[k], jnp.where(phase_ref[k] == 1, LIQUID, 0.0)

    for k in range(PLANES):
        if k % GROUP == 0:
            for copy in copies[k // GROUP]:
                copy.wait()
        if k == 0:
            field_before, liquid_before = plane(0)
            field, liquid = plane(1)
            flux_z = flux(liquid_before, liquid, field_before, field)
        field_after, liquid_after = plane(k + 2)
        flux_z_upper = flux(liquid, liquid_after, field, field_after)
        total = div_ref[k] + (flux_z_upper - flux_z)
        upper = flux(liquid, roll(liquid, -1, 1), field, roll(field, -1, 1))
        upper = jnp.where(lane == LX - 1, 0.0, upper)
        total = total + (upper - roll(upper, 1, 1))
        upper = flux(liquid, roll(liquid, -1, 0), field, roll(field, -1, 0))
        upper = jnp.where(row == LY - 1, 0.0, upper)
        total = total + (upper - roll(upper, 1, 0))
        ends = jnp.where(edge_lane, field, 0.0) + roll(
            jnp.where(edge_lane, liquid, 0.0), QUARTER, 1
        )
        faces = roll(ends[:BLOCKS], 1, 1)
        faces = faces + roll(roll(ends[LY - BLOCKS :], 1, 0), 3, 1)
        faces = faces + roll(ends[BLOCKS:HALF], 5, 1)
        faces = faces + roll(ends[HALF : HALF + WIDE], 7, 1)
        faces = jnp.where(moved, roll(faces, BLOCK, 1), faces)
        lines = jnp.broadcast_to(liquid[LY - 1 : LY], (8, LX))
        for f, line in ((2, field[LY - 1 : LY]), (1, liquid[0:1]), (0, field[0:1])):
            lines = jnp.where(sub <= f, jnp.broadcast_to(line, (8, LX)), lines)
        lines = roll(lines, BLOCK // 2, 1)
        for bit in (1, 2):
            lines = jnp.where((sub & bit) != 0, roll(lines, QUARTER * bit, 1), lines)
        for f in range(4):
            faces = jnp.where(y_lanes[f], jnp.broadcast_to(lines[f : f + 1], (TEAMS, LX)), faces)

        start = k * TEAMS * ROWS
        for r, value in enumerate(
            (
                turn(total[:BLOCKS], block, -1, 0),
                turn(total[LY - BLOCKS :], block, -1, 15),
                total[BLOCKS:HALF],
                total[HALF : HALF + WIDE],
                faces,
            )
        ):
            out[pl.ds(start + r, TEAMS, stride=ROWS), :] = value
        field, liquid, flux_z = field_after, liquid_after, flux_z_upper
        if k % GROUP == GROUP - 1:
            g = k // GROUP
            rows = pl.ds(g * GROUP * TEAMS * ROWS, GROUP * TEAMS * ROWS)
            sent.append(pltpu.make_async_copy(out.at[rows], out_hbm.at[rows], out_sems.at[g]))
            sent[-1].start()
    for copy in sent:
        copy.wait()


def device_kernel(own_ref, other_ref, high_ref, low_ref, out, cells):
    lane = lanes_of(N_GY)
    core = lax.axis_index("c")
    own_place = lax.axis_index("zl") * 4 + lax.axis_index("y") + (N_GY - FIRST_Y)
    team = own_place % TEAMS * BLOCK
    own_y = (lane < BLOCK) & (core == 0)
    at_last, at_first = lane == LX - 1, lane == 0
    groups = N_GX // 2

    def row(ref, g, r):
        return ref[pl.ds((g % groups) * N_GY * ROWS + r, N_GY, stride=ROWS), :]

    def mine(c, g, t):
        refs = (own_ref, other_ref) if c == 0 else (other_ref, own_ref)
        return jnp.where(core == 0, row(refs[0], g, t), row(refs[1], g, 2 + t))

    def face_row(c, g):
        refs = (own_ref, other_ref) if c == 0 else (other_ref, own_ref)
        return jnp.where(core == 0, row(refs[0], g, 4), row(refs[1], g, 4))

    def x_aligned(value):
        return roll(value, 2 * LX - 1 - 4 * core - BLOCK * (team % (4 * BLOCK) == 0), 1)

    def x_parts(here, there):
        lower = roll(there, -1, 1)
        value = weighted(roll(here + lower, -QUARTER, 1), lower - here)
        return [(value, roll(value, 1, 1)), (roll(value, -2, 1), roll(value, -1, 1))]

    def y_part(here):
        here = roll(here, LX - team, 1)
        lower = roll(here, -1, 0)
        upper = roll(here, -2 * QUARTER, 1)
        value = weighted(roll(upper + lower, -QUARTER, 1), lower - upper)
        return roll(jnp.where(own_y, value, 0.0), team + (LX - BLOCK // 2), 1)

    raw = [face_row(c, 0) for c in range(2)]
    faces = [x_aligned(value) for value in raw]
    entering = x_parts(x_aligned(face_row(1, groups - 1)), faces[0])
    for g in range(groups):
        next_raw = [face_row(c, g + 1) for c in range(2)]
        after = [x_aligned(value) for value in next_raw]
        for c in range(2):
            leaving = x_parts(faces[c], after[0] if c else faces[1])
            along_y = y_part(raw[c])
            part = [
                mine(c, g, t)
                + jnp.where(at_last, leaving[t][0], 0.0)
                - jnp.where(at_first, entering[t][1], 0.0)
                for t in range(2)
            ]
            place = pl.ds(c * N_CHIP + g * N_GY, N_GY)
            cells[place, :LX] = part[0] - roll(along_y, 1, 0)
            cells[place, LX:] = part[1] + along_y
            entering = leaving
        raw, faces = next_raw, after

    right_high, right_low = split(cells[...])
    result = dot3((high_ref[...], low_ref[...]), (right_high, right_low))
    for part in range(2):
        rows = slice(part * N_ALL, (part + 1) * N_ALL)
        out[pl.ds(2 * part, N_ALL, stride=4), :] = result[rows, :LX]
        out[pl.ds(2 * part + 1, N_ALL, stride=4), :] = result[rows, LX:]


def local_kernel(x_ref, y_matrix_ref, cos_ref, sin_ref, out_hbm, out, sems):
    y_matrix = split(y_matrix_ref[...])
    x_matrix = split(
        jnp.concatenate(
            [
                jnp.concatenate([cos_ref[...], -sin_ref[...]], axis=1),
                jnp.concatenate([sin_ref[...], cos_ref[...]], axis=1),
            ],
            axis=0,
        )
    )
    block = cell_block()
    copies = []
    for g in range(PLANES // PAIR):
        group = []
        for k in range(PAIR * g, PAIR * (g + 1)):
            start = (k // 2) * 4 * LY + (k % 2) * LY
            lines = [
                turn(x_ref[pl.ds(start + kind, BLOCKS, stride=4), :], block, 1, kind & 1)
                for kind in range(4)
            ]
            lines.append(x_ref[pl.ds(start + 2 * LY, LY), :])
            group.append(jnp.concatenate(lines, axis=0))
        lines = dot3(y_matrix, split(jnp.concatenate(group, axis=1)))
        lines = jnp.concatenate(
            [
                jnp.concatenate(
                    [lines[:LY, k * LX : (k + 1) * LX], lines[LY:, k * LX : (k + 1) * LX]], axis=1
                )
                for k in range(PAIR)
            ],
            axis=0,
        )
        modes = dot3(split(lines), x_matrix)
        for part in range(2):
            for k in range(PAIR):
                out[part, PAIR * g + k] = modes[k * LY : (k + 1) * LY, part * LX : (part + 1) * LX]
            planes = (part, pl.ds(g * PAIR, PAIR))
            copies.append(
                pltpu.make_async_copy(out.at[planes], out_hbm.at[planes], sems.at[g, part])
            )
            copies[-1].start()
    for copy in copies:
        copy.wait()


def listed():
    devices = np.arange(N_ALL).reshape(N_GX // 2, 2, N_GY)
    return np.roll(devices, (-FIRST_CHIP, -FIRST_Y), axis=(0, 2))


def device_tables():
    dest = listed().ravel()
    rev_p = np.array([reversal(i, 4) for i in range(N_GX)])
    rev_q = np.array([reversal(i, 5) for i in range(N_GY)])
    kx = rev_p[dest // N_GY][:, None]
    ky = rev_q[dest % N_GY][:, None]
    source = listed().transpose(1, 0, 2).ravel()[None]
    gx, gy = source // N_GY, source % N_GY
    angle = (2 * kx * gx + ky * gy) % N_GY * (2.0 * math.pi / N_GY)
    table = np.concatenate([np.cos(angle), -np.sin(angle)])
    high = table.astype(ml_dtypes.bfloat16)
    return high, (table - high.astype(np.float64)).astype(ml_dtypes.bfloat16)


def cos_sin(place, mode, length):
    angle = ((place * mode) % length).astype(F32) * (2.0 * math.pi / length)
    return jnp.cos(angle), jnp.sin(angle)


def local_tables(rp, rq):
    line = lax.broadcasted_iota(jnp.int32, (2 * LY, 2 * LY), 0)
    col = lax.broadcasted_iota(jnp.int32, (2 * LY, 2 * LY), 1)
    rest = col - 4 * BLOCKS
    in_block = rest < 0
    part_in = jnp.where(in_block, col // (2 * BLOCKS), rest >> 1) & 1
    place = jnp.where(
        in_block,
        col % BLOCKS + (LY - BLOCKS) * (col // BLOCKS & 1),
        BLOCKS + (rest >> 2) + WIDE * (rest & 1),
    )
    cosine, sine = cos_sin(place, 32 * (line % LY) + rq, NY)
    part_out = line // LY
    sign = jnp.where(part_out < part_in, 1.0, -1.0)
    y_matrix = jnp.where(part_out == part_in, cosine, sign * sine) * (1.0 / math.sqrt(NX * NY))
    line = lax.broadcasted_iota(jnp.int32, (LX, LX), 0)
    col = lax.broadcasted_iota(jnp.int32, (LX, LX), 1)
    return (y_matrix, *cos_sin(line, 16 * col + rp, NX))


def call(kernel, outs, *args, scratch=(), in_hbm=False, out_hbm=False, mib=40):
    def spec(hbm):
        return pl.BlockSpec(memory_space=pltpu.HBM if hbm else pltpu.VMEM)

    return pl.pallas_call(
        kernel,
        out_shape=outs,
        in_specs=[spec(in_hbm)] * len(args),
        out_specs=spec(out_hbm),
        scratch_shapes=scratch,
        compiler_params=pltpu.CompilerParams(vmem_limit_bytes=mib * 1024 * 1024),
    )(*args)


def exchange(chunks, per_core):
    order = listed()
    groups = [order[:, c].ravel() for c in range(2)] if per_core else [order.ravel()]
    groups = [[int(device) for device in group] for group in groups]
    return lax.all_to_all(chunks, EVERYWHERE, 0, 0, axis_index_groups=groups, tiled=True)


def shape(*dims):
    return jax.ShapeDtypeStruct(dims, F32)


def body(p_now, p_prev, phase, div_star):
    padded = (PLANES + 2, LY, LX)
    chunks = call(
        stencil_kernel,
        shape(ROWS * N_CHIP, LX),
        p_now,
        p_prev,
        phase,
        div_star,
        scratch=[
            pltpu.VMEM(padded, F32),
            pltpu.VMEM(padded, F32),
            pltpu.VMEM(padded, jnp.int32),
            pltpu.VMEM((PLANES, LY, LX), F32),
            pltpu.VMEM((ROWS * N_CHIP, LX), F32),
            pltpu.SemaphoreType.DMA((PLANES // GROUP, 4)),
            pltpu.SemaphoreType.DMA((PLANES // GROUP,)),
        ],
        in_hbm=True,
        out_hbm=True,
        mib=60,
    )
    chunks = exchange(chunks.reshape(N_CHIP, 1, ROWS * LX), per_core=True)
    chunks, rp, rq = lax.optimization_barrier(
        (
            chunks.reshape(ROWS * N_CHIP, LX),
            reversal(lax.axis_index(("zh", "x", "c")), 4),
            reversal(lax.axis_index(("zl", "y")), 5),
        )
    )
    other = lax.ppermute(chunks, "c", [(0, 1), (1, 0)])
    other, tables = lax.optimization_barrier((other, local_tables(rp, rq)))
    high, low = device_tables()
    modes = call(
        device_kernel,
        shape(4 * N_ALL, LX),
        chunks,
        other,
        jnp.asarray(high),
        jnp.asarray(low),
        scratch=[pltpu.VMEM((N_ALL, 2 * LX), F32)],
    )
    back = exchange(modes.reshape(N_ALL, 4, LX), per_core=False)
    result = call(
        local_kernel,
        shape(2, PLANES, LY, LX),
        back.reshape(4 * N_ALL, LX),
        *tables,
        scratch=[
            pltpu.VMEM((2, PLANES, LY, LX), F32),
            pltpu.SemaphoreType.DMA((PLANES // PAIR, 2)),
        ],
        out_hbm=True,
    )
    return result.reshape(2, PLANES, 1, LY, 1, LX)


def solution(mesh):
    fine = Mesh(mesh.devices.reshape(2, 4, 2, 8, 4), EVERYWHERE)
    spec = P(None, ("zl", "y"), ("zh", "x", "c"))
    return jax.shard_map(
        body,
        mesh=fine,
        in_specs=(spec, spec, spec, spec),
        out_specs=P(None, None, ("zl", "y"), None, ("zh", "x", "c"), None),
        check_vma=False,
    )
```

```python
import math

import jax
import jax.numpy as jnp
import ml_dtypes
import numpy as np
from jax import lax
from jax.experimental import pallas as pl
from jax.experimental.pallas import tpu as pltpu
from jax.sharding import Mesh
from jax.sharding import PartitionSpec as P

NX = 2048
NY = 2048
PLANES = 16
LY = 64
LX = 128
N_GX = 16
N_GY = 32
N_ALL = N_GX * N_GY
N_CHIP = N_ALL // 2
F32 = jnp.float32
BF16 = jnp.bfloat16

EVERYWHERE = ("zh", "x", "c", "zl", "y")

LIQUID = 7.0 / 8.0
MIXED = 7.0 / 9.0
QUAD = -4.0 / 9.0
LIN = 11.5 / 9.0

BLOCKS = 16
BLOCK = LX // BLOCKS
WIDE = 16
HALF = LY // 2
TEAMS = PLANES
ROWS = 5
GROUP = 4
FIRST_CHIP = 6
FIRST_Y = 16
PAIR = 2
QUARTER = LX // 4


def reversal(index, digits):
    total = 0
    for place in range(digits):
        total = total * 2 + ((index >> place) & 1)
    return total


def split(value):
    high = value.astype(BF16)
    return high, (value - high.astype(F32)).astype(BF16)


def dot3(left, right):
    left_high, left_low = left
    right_high, right_low = right
    return (
        jnp.dot(left_high, right_high, preferred_element_type=F32)
        + jnp.dot(left_high, right_low, preferred_element_type=F32)
        + jnp.dot(left_low, right_high, preferred_element_type=F32)
    )


def weighted(count, difference):
    return count * (LIN + QUAD * count) * difference


def flux(liquid_a, liquid_b, field_a, field_b):
    return jnp.where(liquid_a == liquid_b, liquid_a, MIXED) * (field_b - field_a)


def roll(value, by, axis):
    if isinstance(by, int):
        by = by % value.shape[axis]
        return pltpu.roll(value, by, axis) if by else value
    return pltpu.roll(value, by & (value.shape[axis] - 1), axis)


def lanes_of(rows):
    return lax.broadcasted_iota(jnp.int32, (rows, LX), 1)


def rows_of(rows):
    return lax.broadcasted_iota(jnp.int32, (rows, LX), 0)


def within(lane, start, count):
    return ((lane - start) & (LX - 1)) < count


def turn(value, block, sign, offset):
    value = roll(value, -offset, 0)
    for bit in (1, 2, 4, 8):
        value = jnp.where((block & bit) != 0, roll(value, -sign * bit, 0), value)
    return value


def cell_block():
    return ((lanes_of(BLOCKS) + BLOCK // 2) // BLOCK) & (BLOCKS - 1)


def stencil_kernel(
    now_hbm,
    prev_hbm,
    phase_hbm,
    div_hbm,
    out_hbm,
    now_ref,
    prev_ref,
    phase_ref,
    div_ref,
    out,
    sems,
    out_sems,
):
    copies, sent = [], []
    for g in range(PLANES // GROUP):
        first = GROUP * g + 2 if g else 0
        planes = pl.ds(first, GROUP * (g + 1) + 2 - first)
        inner = pl.ds(GROUP * g, GROUP)
        copies.append(
            [
                pltpu.make_async_copy(source.at[part], target.at[part], sems.at[g, a])
                for a, (source, target, part) in enumerate(
                    (
                        (now_hbm, now_ref, planes),
                        (prev_hbm, prev_ref, planes),
                        (phase_hbm, phase_ref, planes),
                        (div_hbm, div_ref, inner),
                    )
                )
            ]
        )
        for copy in copies[-1]:
            copy.start()

    lane = lanes_of(LY)
    row = rows_of(LY)
    sub = rows_of(8)
    block = cell_block()
    lane_in = lanes_of(TEAMS)
    owner = rows_of(TEAMS) * BLOCK
    moved = rows_of(TEAMS) % 4 == 0
    edge_lane = (lane == 0) | (lane == LX - 1)
    y_lanes = [within(lane_in, QUARTER * f + owner, BLOCK) for f in range(4)]

    def plane(k):
        return 2.0 * now_ref[k] - prev_ref[k], jnp.where(phase_ref[k] == 1, LIQUID, 0.0)

    for k in range(PLANES):
        if k % GROUP == 0:
            for copy in copies[k // GROUP]:
                copy.wait()
        if k == 0:
            field_before, liquid_before = plane(0)
            field, liquid = plane(1)
            flux_z = flux(liquid_before, liquid, field_before, field)
        field_after, liquid_after = plane(k + 2)
        flux_z_upper = flux(liquid, liquid_after, field, field_after)
        total = div_ref[k] + (flux_z_upper - flux_z)
        upper = flux(liquid, roll(liquid, -1, 1), field, roll(field, -1, 1))
        upper = jnp.where(lane == LX - 1, 0.0, upper)
        total = total + (upper - roll(upper, 1, 1))
        upper = flux(liquid, roll(liquid, -1, 0), field, roll(field, -1, 0))
        upper = jnp.where(row == LY - 1, 0.0, upper)
        total = total + (upper - roll(upper, 1, 0))
        ends = jnp.where(edge_lane, field, 0.0) + roll(
            jnp.where(edge_lane, liquid, 0.0), QUARTER, 1
        )
        faces = roll(ends[:BLOCKS], 1, 1)
        faces = faces + roll(roll(ends[LY - BLOCKS :], 1, 0), 3, 1)
        faces = faces + roll(ends[BLOCKS:HALF], 5, 1)
        faces = faces + roll(ends[HALF : HALF + WIDE], 7, 1)
        faces = jnp.where(moved, roll(faces, BLOCK, 1), faces)
        lines = jnp.broadcast_to(liquid[LY - 1 : LY], (8, LX))
        for f, line in ((2, field[LY - 1 : LY]), (1, liquid[0:1]), (0, field[0:1])):
            lines = jnp.where(sub <= f, jnp.broadcast_to(line, (8, LX)), lines)
        lines = roll(lines, BLOCK // 2, 1)
        for bit in (1, 2):
            lines = jnp.where((sub & bit) != 0, roll(lines, QUARTER * bit, 1), lines)
        for f in range(4):
            faces = jnp.where(y_lanes[f], jnp.broadcast_to(lines[f : f + 1], (TEAMS, LX)), faces)

        start = k * TEAMS * ROWS
        for r, value in enumerate(
            (
                turn(total[:BLOCKS], block, -1, 0),
                turn(total[LY - BLOCKS :], block, -1, 15),
                total[BLOCKS:HALF],
                total[HALF : HALF + WIDE],
                faces,
            )
        ):
            out[pl.ds(start + r, TEAMS, stride=ROWS), :] = value
        field, liquid, flux_z = field_after, liquid_after, flux_z_upper
        if k % GROUP == GROUP - 1:
            g = k // GROUP
            rows = pl.ds(g * GROUP * TEAMS * ROWS, GROUP * TEAMS * ROWS)
            sent.append(pltpu.make_async_copy(out.at[rows], out_hbm.at[rows], out_sems.at[g]))
            sent[-1].start()
    for copy in sent:
        copy.wait()


def device_kernel(own_ref, other_ref, high_ref, low_ref, out, cells):
    lane = lanes_of(N_GY)
    core = lax.axis_index("c")
    own_place = lax.axis_index("zl") * 4 + lax.axis_index("y") + (N_GY - FIRST_Y)
    team = own_place % TEAMS * BLOCK
    own_y = (lane < BLOCK) & (core == 0)
    at_last, at_first = lane == LX - 1, lane == 0
    groups = N_GX // 2

    def row(ref, g, r):
        return ref[pl.ds((g % groups) * N_GY * ROWS + r, N_GY, stride=ROWS), :]

    def mine(c, g, t):
        refs = (own_ref, other_ref) if c == 0 else (other_ref, own_ref)
        return jnp.where(core == 0, row(refs[0], g, t), row(refs[1], g, 2 + t))

    def face_row(c, g):
        refs = (own_ref, other_ref) if c == 0 else (other_ref, own_ref)
        return jnp.where(core == 0, row(refs[0], g, 4), row(refs[1], g, 4))

    def x_aligned(value):
        return roll(value, 2 * LX - 1 - 4 * core - BLOCK * (team % (4 * BLOCK) == 0), 1)

    def x_parts(here, there):
        lower = roll(there, -1, 1)
        value = weighted(roll(here + lower, -QUARTER, 1), lower - here)
        return [(value, roll(value, 1, 1)), (roll(value, -2, 1), roll(value, -1, 1))]

    def y_part(here):
        here = roll(here, LX - team, 1)
        lower = roll(here, -1, 0)
        upper = roll(here, -2 * QUARTER, 1)
        value = weighted(roll(upper + lower, -QUARTER, 1), lower - upper)
        return roll(jnp.where(own_y, value, 0.0), team + (LX - BLOCK // 2), 1)

    raw = [face_row(c, 0) for c in range(2)]
    faces = [x_aligned(value) for value in raw]
    entering = x_parts(x_aligned(face_row(1, groups - 1)), faces[0])
    for g in range(groups):
        next_raw = [face_row(c, g + 1) for c in range(2)]
        after = [x_aligned(value) for value in next_raw]
        for c in range(2):
            leaving = x_parts(faces[c], after[0] if c else faces[1])
            along_y = y_part(raw[c])
            part = [
                mine(c, g, t)
                + jnp.where(at_last, leaving[t][0], 0.0)
                - jnp.where(at_first, entering[t][1], 0.0)
                for t in range(2)
            ]
            place = pl.ds(c * N_CHIP + g * N_GY, N_GY)
            cells[place, :LX] = part[0] - roll(along_y, 1, 0)
            cells[place, LX:] = part[1] + along_y
            entering = leaving
        raw, faces = next_raw, after

    right_high, right_low = split(cells[...])
    result = dot3((high_ref[...], low_ref[...]), (right_high, right_low))
    for part in range(2):
        rows = slice(part * N_ALL, (part + 1) * N_ALL)
        out[pl.ds(2 * part, N_ALL, stride=4), :] = result[rows, :LX]
        out[pl.ds(2 * part + 1, N_ALL, stride=4), :] = result[rows, LX:]


def local_kernel(x_ref, y_matrix_ref, cos_ref, sin_ref, out_hbm, out, sems):
    y_matrix = split(y_matrix_ref[...])
    x_matrix = split(
        jnp.concatenate(
            [
                jnp.concatenate([cos_ref[...], -sin_ref[...]], axis=1),
                jnp.concatenate([sin_ref[...], cos_ref[...]], axis=1),
            ],
            axis=0,
        )
    )
    block = cell_block()
    copies = []
    for g in range(PLANES // PAIR):
        group = []
        for k in range(PAIR * g, PAIR * (g + 1)):
            chip = (k // 2 + FIRST_CHIP) % (N_GX // 2)
            half = (k % 2 + FIRST_Y // TEAMS) % 2
            start = chip * 4 * LY + half * LY
            lines = [
                turn(x_ref[pl.ds(start + kind, BLOCKS, stride=4), :], block, 1, kind & 1)
                for kind in range(4)
            ]
            lines.append(x_ref[pl.ds(start + 2 * LY, LY), :])
            group.append(jnp.concatenate(lines, axis=0))
        lines = dot3(y_matrix, split(jnp.concatenate(group, axis=1)))
        lines = jnp.concatenate(
            [
                jnp.concatenate(
                    [lines[:LY, k * LX : (k + 1) * LX], lines[LY:, k * LX : (k + 1) * LX]], axis=1
                )
                for k in range(PAIR)
            ],
            axis=0,
        )
        modes = dot3(split(lines), x_matrix)
        for part in range(2):
            for k in range(PAIR):
                out[part, PAIR * g + k] = modes[k * LY : (k + 1) * LY, part * LX : (part + 1) * LX]
            planes = (part, pl.ds(g * PAIR, PAIR))
            copies.append(
                pltpu.make_async_copy(out.at[planes], out_hbm.at[planes], sems.at[g, part])
            )
            copies[-1].start()
    for copy in copies:
        copy.wait()


def listed():
    devices = np.arange(N_ALL).reshape(N_GX // 2, 2, N_GY)
    return np.roll(devices, (-FIRST_CHIP, -FIRST_Y), axis=(0, 2))


def device_tables():
    dest = np.arange(N_ALL)
    rev_p = np.array([reversal(i, 4) for i in range(N_GX)])
    rev_q = np.array([reversal(i, 5) for i in range(N_GY)])
    kx = rev_p[dest // N_GY][:, None]
    ky = rev_q[dest % N_GY][:, None]
    source = listed().transpose(1, 0, 2).ravel()[None]
    gx, gy = source // N_GY, source % N_GY
    angle = (2 * kx * gx + ky * gy) % N_GY * (2.0 * math.pi / N_GY)
    table = np.concatenate([np.cos(angle), -np.sin(angle)])
    high = table.astype(ml_dtypes.bfloat16)
    return high, (table - high.astype(np.float64)).astype(ml_dtypes.bfloat16)


def cos_sin(place, mode, length):
    angle = ((place * mode) % length).astype(F32) * (2.0 * math.pi / length)
    return jnp.cos(angle), jnp.sin(angle)


def local_tables(rp, rq):
    line = lax.broadcasted_iota(jnp.int32, (2 * LY, 2 * LY), 0)
    col = lax.broadcasted_iota(jnp.int32, (2 * LY, 2 * LY), 1)
    rest = col - 4 * BLOCKS
    in_block = rest < 0
    part_in = jnp.where(in_block, col // (2 * BLOCKS), rest >> 1) & 1
    place = jnp.where(
        in_block,
        col % BLOCKS + (LY - BLOCKS) * (col // BLOCKS & 1),
        BLOCKS + (rest >> 2) + WIDE * (rest & 1),
    )
    cosine, sine = cos_sin(place, 32 * (line % LY) + rq, NY)
    part_out = line // LY
    sign = jnp.where(part_out < part_in, 1.0, -1.0)
    y_matrix = jnp.where(part_out == part_in, cosine, sign * sine) * (1.0 / math.sqrt(NX * NY))
    line = lax.broadcasted_iota(jnp.int32, (LX, LX), 0)
    col = lax.broadcasted_iota(jnp.int32, (LX, LX), 1)
    return (y_matrix, *cos_sin(line, 16 * col + rp, NX))


def call(kernel, outs, *args, scratch=(), in_hbm=False, out_hbm=False, mib=40):
    def spec(hbm):
        return pl.BlockSpec(memory_space=pltpu.HBM if hbm else pltpu.VMEM)

    return pl.pallas_call(
        kernel,
        out_shape=outs,
        in_specs=[spec(in_hbm)] * len(args),
        out_specs=spec(out_hbm),
        scratch_shapes=scratch,
        compiler_params=pltpu.CompilerParams(vmem_limit_bytes=mib * 1024 * 1024),
    )(*args)


def first_exchange(chunks):
    groups = [[int(device) for device in listed()[:, c].ravel()] for c in range(2)]
    return lax.all_to_all(chunks, EVERYWHERE, 0, 0, axis_index_groups=groups, tiled=True)


def shape(*dims):
    return jax.ShapeDtypeStruct(dims, F32)


def body(p_now, p_prev, phase, div_star):
    padded = (PLANES + 2, LY, LX)
    chunks = call(
        stencil_kernel,
        shape(ROWS * N_CHIP, LX),
        p_now,
        p_prev,
        phase,
        div_star,
        scratch=[
            pltpu.VMEM(padded, F32),
            pltpu.VMEM(padded, F32),
            pltpu.VMEM(padded, jnp.int32),
            pltpu.VMEM((PLANES, LY, LX), F32),
            pltpu.VMEM((ROWS * N_CHIP, LX), F32),
            pltpu.SemaphoreType.DMA((PLANES // GROUP, 4)),
            pltpu.SemaphoreType.DMA((PLANES // GROUP,)),
        ],
        in_hbm=True,
        out_hbm=True,
        mib=60,
    )
    chunks = first_exchange(chunks.reshape(N_CHIP, 1, ROWS * LX))
    chunks, rp, rq = lax.optimization_barrier(
        (
            chunks.reshape(ROWS * N_CHIP, LX),
            reversal(lax.axis_index(("zh", "x", "c")), 4),
            reversal(lax.axis_index(("zl", "y")), 5),
        )
    )
    other = lax.ppermute(chunks, "c", [(0, 1), (1, 0)])
    other, tables = lax.optimization_barrier((other, local_tables(rp, rq)))
    high, low = device_tables()
    modes = call(
        device_kernel,
        shape(4 * N_ALL, LX),
        chunks,
        other,
        jnp.asarray(high),
        jnp.asarray(low),
        scratch=[pltpu.VMEM((N_ALL, 2 * LX), F32)],
    )
    back = lax.all_to_all(modes.reshape(N_ALL, 4, LX), EVERYWHERE, 0, 0, tiled=True)
    result = call(
        local_kernel,
        shape(2, PLANES, LY, LX),
        back.reshape(4 * N_ALL, LX),
        *tables,
        scratch=[
            pltpu.VMEM((2, PLANES, LY, LX), F32),
            pltpu.SemaphoreType.DMA((PLANES // PAIR, 2)),
        ],
        out_hbm=True,
    )
    return result.reshape(2, PLANES, 1, LY, 1, LX)


def solution(mesh):
    fine = Mesh(mesh.devices.reshape(2, 4, 2, 8, 4), EVERYWHERE)
    spec = P(None, ("zl", "y"), ("zh", "x", "c"))
    return jax.shard_map(
        body,
        mesh=fine,
        in_specs=(spec, spec, spec, spec),
        out_specs=P(None, None, ("zl", "y"), None, ("zh", "x", "c"), None),
        check_vma=False,
    )
```

```python
import math

import jax
import jax.numpy as jnp
import ml_dtypes
import numpy as np
from jax import lax
from jax.experimental import pallas as pl
from jax.experimental.pallas import tpu as pltpu
from jax.sharding import Mesh
from jax.sharding import PartitionSpec as P

NX = 2048
NY = 2048
PLANES = 16
LY = 64
LX = 128
N_GX = 16
N_GY = 32
N_ALL = N_GX * N_GY
N_CHIP = N_ALL // 2
F32 = jnp.float32
BF16 = jnp.bfloat16

EVERYWHERE = ("zh", "x", "c", "zl", "y")

LIQUID = 7.0 / 8.0
MIXED = 7.0 / 9.0
QUAD = -4.0 / 9.0
LIN = 11.5 / 9.0

BLOCKS = 16
BLOCK = LX // BLOCKS
WIDE = 16
HALF = LY // 2
TEAMS = PLANES
ROWS = 5
GROUP = 4
FIRST_CHIP = 7
FIRST_Y = 16
PAIR = 2
QUARTER = LX // 4


def reversal(index, digits):
    total = 0
    for place in range(digits):
        total = total * 2 + ((index >> place) & 1)
    return total


def split(value):
    high = value.astype(BF16)
    return high, (value - high.astype(F32)).astype(BF16)


def dot3(left, right):
    left_high, left_low = left
    right_high, right_low = right
    return (
        jnp.dot(left_high, right_high, preferred_element_type=F32)
        + jnp.dot(left_high, right_low, preferred_element_type=F32)
        + jnp.dot(left_low, right_high, preferred_element_type=F32)
    )


def weighted(count, difference):
    return count * (LIN + QUAD * count) * difference


def flux(liquid_a, liquid_b, field_a, field_b):
    return jnp.where(liquid_a == liquid_b, liquid_a, MIXED) * (field_b - field_a)


def roll(value, by, axis):
    if isinstance(by, int):
        by = by % value.shape[axis]
        return pltpu.roll(value, by, axis) if by else value
    return pltpu.roll(value, by & (value.shape[axis] - 1), axis)


def lanes_of(rows):
    return lax.broadcasted_iota(jnp.int32, (rows, LX), 1)


def rows_of(rows):
    return lax.broadcasted_iota(jnp.int32, (rows, LX), 0)


def within(lane, start, count):
    return ((lane - start) & (LX - 1)) < count


def turn(value, block, sign, offset):
    value = roll(value, -offset, 0)
    for bit in (1, 2, 4, 8):
        value = jnp.where((block & bit) != 0, roll(value, -sign * bit, 0), value)
    return value


def cell_block():
    return ((lanes_of(BLOCKS) + BLOCK // 2) // BLOCK) & (BLOCKS - 1)


def stencil_kernel(
    now_hbm,
    prev_hbm,
    phase_hbm,
    div_hbm,
    out_hbm,
    now_ref,
    prev_ref,
    phase_ref,
    div_ref,
    out,
    sems,
    out_sems,
):
    copies, sent = [], []
    for g in range(PLANES // GROUP):
        first = GROUP * g + 2 if g else 0
        planes = pl.ds(first, GROUP * (g + 1) + 2 - first)
        inner = pl.ds(GROUP * g, GROUP)
        copies.append(
            [
                pltpu.make_async_copy(source.at[part], target.at[part], sems.at[g, a])
                for a, (source, target, part) in enumerate(
                    (
                        (now_hbm, now_ref, planes),
                        (prev_hbm, prev_ref, planes),
                        (phase_hbm, phase_ref, planes),
                        (div_hbm, div_ref, inner),
                    )
                )
            ]
        )
        for copy in copies[-1]:
            copy.start()

    lane = lanes_of(LY)
    row = rows_of(LY)
    sub = rows_of(8)
    block = cell_block()
    lane_in = lanes_of(TEAMS)
    owner = rows_of(TEAMS) * BLOCK
    moved = rows_of(TEAMS) % 4 == 0
    edge_lane = (lane == 0) | (lane == LX - 1)
    y_lanes = [within(lane_in, QUARTER * f + owner, BLOCK) for f in range(4)]

    def plane(k):
        return 2.0 * now_ref[k] - prev_ref[k], jnp.where(phase_ref[k] == 1, LIQUID, 0.0)

    for k in range(PLANES):
        if k % GROUP == 0:
            for copy in copies[k // GROUP]:
                copy.wait()
        if k == 0:
            field_before, liquid_before = plane(0)
            field, liquid = plane(1)
            flux_z = flux(liquid_before, liquid, field_before, field)
        field_after, liquid_after = plane(k + 2)
        flux_z_upper = flux(liquid, liquid_after, field, field_after)
        total = div_ref[k] + (flux_z_upper - flux_z)
        upper = flux(liquid, roll(liquid, -1, 1), field, roll(field, -1, 1))
        upper = jnp.where(lane == LX - 1, 0.0, upper)
        total = total + (upper - roll(upper, 1, 1))
        upper = flux(liquid, roll(liquid, -1, 0), field, roll(field, -1, 0))
        upper = jnp.where(row == LY - 1, 0.0, upper)
        total = total + (upper - roll(upper, 1, 0))
        ends = jnp.where(edge_lane, field, 0.0) + roll(
            jnp.where(edge_lane, liquid, 0.0), QUARTER, 1
        )
        faces = roll(ends[:BLOCKS], 1, 1)
        faces = faces + roll(roll(ends[LY - BLOCKS :], 1, 0), 3, 1)
        faces = faces + roll(ends[BLOCKS:HALF], 5, 1)
        faces = faces + roll(ends[HALF : HALF + WIDE], 7, 1)
        faces = jnp.where(moved, roll(faces, BLOCK, 1), faces)
        lines = jnp.broadcast_to(liquid[LY - 1 : LY], (8, LX))
        for f, line in ((2, field[LY - 1 : LY]), (1, liquid[0:1]), (0, field[0:1])):
            lines = jnp.where(sub <= f, jnp.broadcast_to(line, (8, LX)), lines)
        lines = roll(lines, BLOCK // 2, 1)
        for bit in (1, 2):
            lines = jnp.where((sub & bit) != 0, roll(lines, QUARTER * bit, 1), lines)
        for f in range(4):
            faces = jnp.where(y_lanes[f], jnp.broadcast_to(lines[f : f + 1], (TEAMS, LX)), faces)

        start = k * TEAMS * ROWS
        for r, value in enumerate(
            (
                turn(total[:BLOCKS], block, -1, 0),
                turn(total[LY - BLOCKS :], block, -1, 15),
                total[BLOCKS:HALF],
                total[HALF : HALF + WIDE],
                faces,
            )
        ):
            out[pl.ds(start + r, TEAMS, stride=ROWS), :] = value
        field, liquid, flux_z = field_after, liquid_after, flux_z_upper
        if k % GROUP == GROUP - 1:
            g = k // GROUP
            rows = pl.ds(g * GROUP * TEAMS * ROWS, GROUP * TEAMS * ROWS)
            sent.append(pltpu.make_async_copy(out.at[rows], out_hbm.at[rows], out_sems.at[g]))
            sent[-1].start()
    for copy in sent:
        copy.wait()


def device_kernel(own_ref, other_ref, high_ref, low_ref, out, cells):
    lane = lanes_of(N_GY)
    core = lax.axis_index("c")
    own_place = lax.axis_index("zl") * 4 + lax.axis_index("y") + (N_GY - FIRST_Y)
    team = own_place % TEAMS * BLOCK
    own_y = (lane < BLOCK) & (core == 0)
    at_last, at_first = lane == LX - 1, lane == 0
    groups = N_GX // 2

    def row(ref, g, r):
        return ref[pl.ds((g % groups) * N_GY * ROWS + r, N_GY, stride=ROWS), :]

    def mine(c, g, t):
        refs = (own_ref, other_ref) if c == 0 else (other_ref, own_ref)
        return jnp.where(core == 0, row(refs[0], g, t), row(refs[1], g, 2 + t))

    def face_row(c, g):
        refs = (own_ref, other_ref) if c == 0 else (other_ref, own_ref)
        return jnp.where(core == 0, row(refs[0], g, 4), row(refs[1], g, 4))

    def x_aligned(value):
        return roll(value, 2 * LX - 1 - 4 * core - BLOCK * (team % (4 * BLOCK) == 0), 1)

    def x_parts(here, there):
        lower = roll(there, -1, 1)
        value = weighted(roll(here + lower, -QUARTER, 1), lower - here)
        return [(value, roll(value, 1, 1)), (roll(value, -2, 1), roll(value, -1, 1))]

    def y_part(here):
        here = roll(here, LX - team, 1)
        lower = roll(here, -1, 0)
        upper = roll(here, -2 * QUARTER, 1)
        value = weighted(roll(upper + lower, -QUARTER, 1), lower - upper)
        return roll(jnp.where(own_y, value, 0.0), team + (LX - BLOCK // 2), 1)

    raw = [face_row(c, 0) for c in range(2)]
    faces = [x_aligned(value) for value in raw]
    entering = x_parts(x_aligned(face_row(1, groups - 1)), faces[0])
    for g in range(groups):
        next_raw = [face_row(c, g + 1) for c in range(2)]
        after = [x_aligned(value) for value in next_raw]
        for c in range(2):
            leaving = x_parts(faces[c], after[0] if c else faces[1])
            along_y = y_part(raw[c])
            part = [
                mine(c, g, t)
                + jnp.where(at_last, leaving[t][0], 0.0)
                - jnp.where(at_first, entering[t][1], 0.0)
                for t in range(2)
            ]
            place = pl.ds(c * N_CHIP + g * N_GY, N_GY)
            cells[place, :LX] = part[0] - roll(along_y, 1, 0)
            cells[place, LX:] = part[1] + along_y
            entering = leaving
        raw, faces = next_raw, after

    right_high, right_low = split(cells[...])
    result = dot3((high_ref[...], low_ref[...]), (right_high, right_low))
    for part in range(2):
        rows = slice(part * N_ALL, (part + 1) * N_ALL)
        out[pl.ds(2 * part, N_ALL, stride=4), :] = result[rows, :LX]
        out[pl.ds(2 * part + 1, N_ALL, stride=4), :] = result[rows, LX:]


def local_kernel(x_ref, y_matrix_ref, cos_ref, sin_ref, out_hbm, out, sems):
    y_matrix = split(y_matrix_ref[...])
    x_matrix = split(
        jnp.concatenate(
            [
                jnp.concatenate([cos_ref[...], -sin_ref[...]], axis=1),
                jnp.concatenate([sin_ref[...], cos_ref[...]], axis=1),
            ],
            axis=0,
        )
    )
    block = cell_block()
    copies = []
    for g in range(PLANES // PAIR):
        group = []
        for k in range(PAIR * g, PAIR * (g + 1)):
            chip = (k // 2 + FIRST_CHIP) % (N_GX // 2)
            half = (k % 2 + FIRST_Y // TEAMS) % 2
            start = chip * 4 * LY + half * LY
            lines = [
                turn(x_ref[pl.ds(start + kind, BLOCKS, stride=4), :], block, 1, kind & 1)
                for kind in range(4)
            ]
            lines.append(x_ref[pl.ds(start + 2 * LY, LY), :])
            group.append(jnp.concatenate(lines, axis=0))
        lines = dot3(y_matrix, split(jnp.concatenate(group, axis=1)))
        lines = jnp.concatenate(
            [
                jnp.concatenate(
                    [lines[:LY, k * LX : (k + 1) * LX], lines[LY:, k * LX : (k + 1) * LX]], axis=1
                )
                for k in range(PAIR)
            ],
            axis=0,
        )
        modes = dot3(split(lines), x_matrix)
        for part in range(2):
            for k in range(PAIR):
                out[part, PAIR * g + k] = modes[k * LY : (k + 1) * LY, part * LX : (part + 1) * LX]
            planes = (part, pl.ds(g * PAIR, PAIR))
            copies.append(
                pltpu.make_async_copy(out.at[planes], out_hbm.at[planes], sems.at[g, part])
            )
            copies[-1].start()
    for copy in copies:
        copy.wait()


def listed():
    devices = np.arange(N_ALL).reshape(N_GX // 2, 2, N_GY)
    return np.roll(devices, (-FIRST_CHIP, -FIRST_Y), axis=(0, 2))


def device_tables():
    dest = np.arange(N_ALL)
    rev_p = np.array([reversal(i, 4) for i in range(N_GX)])
    rev_q = np.array([reversal(i, 5) for i in range(N_GY)])
    kx = rev_p[dest // N_GY][:, None]
    ky = rev_q[dest % N_GY][:, None]
    source = listed().transpose(1, 0, 2).ravel()[None]
    gx, gy = source // N_GY, source % N_GY
    angle = (2 * kx * gx + ky * gy) % N_GY * (2.0 * math.pi / N_GY)
    table = np.concatenate([np.cos(angle), -np.sin(angle)])
    high = table.astype(ml_dtypes.bfloat16)
    return high, (table - high.astype(np.float64)).astype(ml_dtypes.bfloat16)


def cos_sin(place, mode, length):
    angle = ((place * mode) % length).astype(F32) * (2.0 * math.pi / length)
    return jnp.cos(angle), jnp.sin(angle)


def local_tables(rp, rq):
    line = lax.broadcasted_iota(jnp.int32, (2 * LY, 2 * LY), 0)
    col = lax.broadcasted_iota(jnp.int32, (2 * LY, 2 * LY), 1)
    rest = col - 4 * BLOCKS
    in_block = rest < 0
    part_in = jnp.where(in_block, col // (2 * BLOCKS), rest >> 1) & 1
    place = jnp.where(
        in_block,
        col % BLOCKS + (LY - BLOCKS) * (col // BLOCKS & 1),
        BLOCKS + (rest >> 2) + WIDE * (rest & 1),
    )
    cosine, sine = cos_sin(place, 32 * (line % LY) + rq, NY)
    part_out = line // LY
    sign = jnp.where(part_out < part_in, 1.0, -1.0)
    y_matrix = jnp.where(part_out == part_in, cosine, sign * sine) * (1.0 / math.sqrt(NX * NY))
    line = lax.broadcasted_iota(jnp.int32, (LX, LX), 0)
    col = lax.broadcasted_iota(jnp.int32, (LX, LX), 1)
    return (y_matrix, *cos_sin(line, 16 * col + rp, NX))


def call(kernel, outs, *args, scratch=(), in_hbm=False, out_hbm=False, mib=40):
    def spec(hbm):
        return pl.BlockSpec(memory_space=pltpu.HBM if hbm else pltpu.VMEM)

    return pl.pallas_call(
        kernel,
        out_shape=outs,
        in_specs=[spec(in_hbm)] * len(args),
        out_specs=spec(out_hbm),
        scratch_shapes=scratch,
        compiler_params=pltpu.CompilerParams(vmem_limit_bytes=mib * 1024 * 1024),
    )(*args)


def first_exchange(chunks):
    groups = [[int(device) for device in listed()[:, c].ravel()] for c in range(2)]
    return lax.all_to_all(chunks, EVERYWHERE, 0, 0, axis_index_groups=groups, tiled=True)


def shape(*dims):
    return jax.ShapeDtypeStruct(dims, F32)


def body(p_now, p_prev, phase, div_star):
    padded = (PLANES + 2, LY, LX)
    chunks = call(
        stencil_kernel,
        shape(ROWS * N_CHIP, LX),
        p_now,
        p_prev,
        phase,
        div_star,
        scratch=[
            pltpu.VMEM(padded, F32),
            pltpu.VMEM(padded, F32),
            pltpu.VMEM(padded, jnp.int32),
            pltpu.VMEM((PLANES, LY, LX), F32),
            pltpu.VMEM((ROWS * N_CHIP, LX), F32),
            pltpu.SemaphoreType.DMA((PLANES // GROUP, 4)),
            pltpu.SemaphoreType.DMA((PLANES // GROUP,)),
        ],
        in_hbm=True,
        out_hbm=True,
        mib=60,
    )
    chunks = first_exchange(chunks.reshape(N_CHIP, 1, ROWS * LX))
    chunks, rp, rq = lax.optimization_barrier(
        (
            chunks.reshape(ROWS * N_CHIP, LX),
            reversal(lax.axis_index(("zh", "x", "c")), 4),
            reversal(lax.axis_index(("zl", "y")), 5),
        )
    )
    other = lax.ppermute(chunks, "c", [(0, 1), (1, 0)])
    other, tables = lax.optimization_barrier((other, local_tables(rp, rq)))
    high, low = device_tables()
    modes = call(
        device_kernel,
        shape(4 * N_ALL, LX),
        chunks,
        other,
        jnp.asarray(high),
        jnp.asarray(low),
        scratch=[pltpu.VMEM((N_ALL, 2 * LX), F32)],
    )
    back = lax.all_to_all(modes.reshape(N_ALL, 4, LX), EVERYWHERE, 0, 0, tiled=True)
    result = call(
        local_kernel,
        shape(2, PLANES, LY, LX),
        back.reshape(4 * N_ALL, LX),
        *tables,
        scratch=[
            pltpu.VMEM((2, PLANES, LY, LX), F32),
            pltpu.SemaphoreType.DMA((PLANES // PAIR, 2)),
        ],
        out_hbm=True,
    )
    return result.reshape(2, PLANES, 1, LY, 1, LX)


def solution(mesh):
    fine = Mesh(mesh.devices.reshape(2, 4, 2, 8, 4), EVERYWHERE)
    spec = P(None, ("zl", "y"), ("zh", "x", "c"))
    return jax.shard_map(
        body,
        mesh=fine,
        in_specs=(spec, spec, spec, spec),
        out_specs=P(None, None, ("zl", "y"), None, ("zh", "x", "c"), None),
        check_vma=False,
    )
```
